32 devices in a mesh: len: 4 (over y, x), energy: 4 (over z), mom: 2 (over core).
Axes of the slice: x: 2, y: 2, z: 4, core: 2. Of those that a mesh axis runs over, the one named last changes fastest.
Arguments:
- hamiltonian: float32 [2, 4, 2, 128, 128], P('mom', 'len'), may hold values from -0.5 to 0.5
- sigma_prev: float32 [2, 4, 16, 2, 128, 128], P('mom', 'len', 'energy'), may hold values from -0.25 to 0.25
- coupling: float32 [4, 128, 128], P('len'), may hold values from -1.5 to 1.5
- coupling_pattern: int32 [128, 128], replicated, may hold values 0 or 1
- phonon_shift: int32 [4], replicated, may hold values from 1 to 8
- phonon_weight: float32 [4], replicated, may hold values from 0.5 to 2
Outputs:
- sigma_retarded: float32 [2, 4, 16, 2, 128, 128], P('mom', 'len', 'energy')
- sigma_lesser: float32 [2, 4, 16, 2, 128, 128], P('mom', 'len', 'energy')
The draws below stay inside these ranges and needn't reach their ends.
All inputs are finite; a program needn't handle non-finite values.
Results may differ from the reference program's by a relative error of at most 0.0001.
Values sent between devices are 32-bit elements; how exact they have to be, the bound alone decides.
No kernel may reach another device: no remote copies, remote signals or barrier semaphores. Data moves between devices by JAX's collectives and lax.ppermute only.
A program may use at most 128 MiB of HBM per device.

```python
import math
import jax
import jax.numpy as jnp
from jax import lax

NORB = 128
NPHON = 4
NEWTON = 2
LAYERS = 4
ENERGIES = 16
MOMENTA = 2


def set_ends(values, stream_key, least, largest):
    spot = [jax.random.randint(jax.random.fold_in(stream_key, axis), (), 0, length) for axis, length in enumerate(values.shape)]
    longest = values.shape.index(max(values.shape))
    next_to = spot[:longest] + [(spot[longest] + 1) % values.shape[longest]] + spot[longest + 1:]
    return values.at[tuple(spot)].set(least).at[tuple(next_to)].set(largest)


def shard_levels(key, shape, shards, least, top_value):
    factor_of, own = 1.0, jax.random.fold_in(key, 6)
    for dim, blocks in shards:
        draws = jnp.exp(jax.random.uniform(jax.random.fold_in(own, dim), (blocks,), jnp.float32, least / len(shards), top_value / len(shards)))
        factor_of = factor_of * jnp.repeat(draws, shape[dim] // blocks).reshape([-1 if axis == dim else 1 for axis in range(len(shape))])
    return factor_of


def gaussian(rng, dims, deviation, most, split=(), kind=jnp.bfloat16):
    result = jax.random.normal(rng, dims, jnp.float32) * deviation
    if len(split) > 0:
        result = shard_levels(rng, dims, split, -0.22, 0.18) * result
    return jnp.clip(result, min=-most, max=most).astype(kind)


def setup_inputs(seed: int = 0) -> dict:
    streams_of = jax.random.split(jax.random.key(seed), 7)
    return {
        "hamiltonian": gaussian(streams_of[0], (MOMENTA, LAYERS, 2, NORB, NORB), NORB ** -0.5, 0.5, ((0, 2), (1, 4)), jnp.float32),
        "sigma_prev": gaussian(streams_of[1], (MOMENTA, LAYERS, ENERGIES, 2, NORB, NORB), (4 * NORB) ** -0.5, 0.25, ((0, 2), (1, 4), (2, 4)), jnp.float32),
        "coupling": gaussian(streams_of[2], (LAYERS, NORB, NORB), (NORB // 9) ** -0.5, 1.5, ((0, 4),), jnp.float32),
        "coupling_pattern": set_ends((jax.random.randint(streams_of[3], (NORB, NORB), 0, 2) < 1).astype(jnp.int32), jax.random.fold_in(streams_of[3], 1), 0, 1),
        "phonon_shift": set_ends(jax.random.randint(streams_of[4], (NPHON,), 1, ENERGIES // 2 + 1), jax.random.fold_in(streams_of[4], 1), 1, (ENERGIES // 2 + 1) - 1).astype(jnp.int32),
        "phonon_weight": jnp.clip(jnp.exp(jax.random.uniform(streams_of[5], (NPHON,), jnp.float32, math.log(0.5), math.log(2.0))), 0.5, 2.0),
    }


HIGHEST = lax.Precision.HIGHEST


def cmul(left, right):
    def prod(a, b):
        return jnp.einsum("eij,ejk->eik", a, b, precision=HIGHEST)
    real = prod(left[:, 0], right[:, 0]) - prod(left[:, 1], right[:, 1])
    imag = prod(left[:, 0], right[:, 1]) + prod(left[:, 1], right[:, 0])
    return jnp.stack([real, imag], axis=1)


def bond_left(bond, mat):
    return jnp.einsum("ij,ecjk->ecik", bond, mat, precision=HIGHEST)


def bond_right(mat, bond):
    return jnp.einsum("ecij,jk->ecik", mat, bond, precision=HIGHEST)


def scale_by(mat, qre, qim):
    qre = qre[:, None, None]
    qim = qim[:, None, None]
    real = qre * mat[:, 0] - qim * mat[:, 1]
    imag = qre * mat[:, 1] + qim * mat[:, 0]
    return jnp.stack([real, imag], axis=1)


def invert(ham, sig, zre, zim):
    eye = jnp.eye(ham.shape[-1], dtype=jnp.float32)
    eye_c = jnp.stack([eye, jnp.zeros_like(eye)])
    dmat = scale_by(jnp.broadcast_to(eye_c, sig.shape), zre, zim) - ham[None] - sig
    mag = zre * zre + zim * zim
    qre = zre / mag
    qim = -zim / mag
    inverse = scale_by(2.0 * eye_c - scale_by(dmat, qre, qim), qre, qim)
    for step in range(NEWTON):
        inverse = cmul(inverse, 2.0 * eye_c - cmul(dmat, inverse))
    return inverse


def kernels(shift, weight, total):
    index = jnp.arange(total, dtype=jnp.int32)
    own = (index[None, None, :] == index[None, :, None] - shift[:, None, None]).astype(jnp.float32)
    other = (index[None, None, :] == index[None, :, None] + shift[:, None, None]).astype(jnp.float32)
    own = jnp.sum(weight[:, None, None] * own, axis=0)
    other = jnp.sum(weight[:, None, None] * other, axis=0)
    return own, other


def channels(green, occupation):
    diff_re = green[:, 0] - jnp.swapaxes(green[:, 0], -1, -2)
    diff_im = green[:, 1] + jnp.swapaxes(green[:, 1], -1, -2)
    scale = occupation[:, None, None]
    return jnp.stack([green[:, 0], green[:, 1], scale * diff_re, scale * diff_im], axis=1)


def reference(hamiltonian, sigma_prev, coupling, coupling_pattern, phonon_shift, phonon_weight):
    mask = coupling_pattern.astype(jnp.float32)
    energy_pos = jnp.arange(ENERGIES, dtype=jnp.int32).astype(jnp.float32)
    zre = 5.0 + 2.0 * energy_pos / ENERGIES
    zim = jnp.ones_like(zre)
    occupation = 1.0 / (1.0 + jnp.exp(8.0 * energy_pos / ENERGIES - 4.0))
    bonds = [coupling[layer] * mask for layer in range(LAYERS)]
    stacked = []
    for momentum in range(MOMENTA):
        blocks = [invert(hamiltonian[momentum, layer], sigma_prev[momentum, layer], zre, zim) for layer in range(LAYERS)]
        zero = jnp.zeros_like(blocks[0])
        lefts = [zero]
        gleft = blocks[0]
        for layer in range(1, LAYERS):
            term = bond_right(bond_left(bonds[layer], gleft), bonds[layer].T)
            lefts.append(term)
            gleft = blocks[layer] + cmul(cmul(blocks[layer], term), blocks[layer])
        rights = [zero for layer in range(LAYERS)]
        gright = blocks[LAYERS - 1]
        for layer in range(LAYERS - 2, -1, -1):
            term = bond_right(bond_left(bonds[layer + 1].T, gright), bonds[layer + 1])
            rights[layer] = term
            gright = blocks[layer] + cmul(cmul(blocks[layer], term), blocks[layer])
        row = []
        for layer in range(LAYERS):
            green = blocks[layer] + cmul(cmul(blocks[layer], lefts[layer] + rights[layer]), blocks[layer])
            row.append(channels(green, occupation))
        stacked.append(row)
    own, other = kernels(phonon_shift, phonon_weight, ENERGIES)
    combined = []
    for momentum in range(MOMENTA):
        row = []
        for layer in range(LAYERS):
            lower = stacked[momentum][layer - 1] if layer > 0 else jnp.zeros_like(stacked[momentum][layer])
            upper = stacked[momentum][layer + 1] if layer + 1 < LAYERS else jnp.zeros_like(stacked[momentum][layer])
            row.append(stacked[momentum][layer] + 0.5 * (lower + upper))
        combined.append(row)
    retarded = []
    lesser = []
    for momentum in range(MOMENTA):
        ret_row = []
        les_row = []
        for layer in range(LAYERS):
            mine = combined[momentum][layer]
            theirs = combined[1 - momentum][layer]
            out = jnp.einsum("ef,fcij->ecij", own, mine, precision=HIGHEST) + 0.5 * jnp.einsum("ef,fcij->ecij", other, theirs, precision=HIGHEST)
            ret_row.append(out[:, :2])
            les_row.append(out[:, 2:])
        retarded.append(jnp.stack(ret_row))
        lesser.append(jnp.stack(les_row))
    return jnp.stack(retarded), jnp.stack(lesser)
```

```python
import functools

import jax
import jax.numpy as jnp
from jax import lax
from jax.experimental import pallas as pl
from jax.experimental.pallas import tpu as pltpu
from jax.sharding import PartitionSpec as P

F32 = jnp.float32
BF16 = jnp.bfloat16
VMEM_LIMIT = 16 * 1024 * 1024


def split(x):
    high = x.astype(BF16)
    return high, (x - high.astype(F32)).astype(BF16)


def dot(a, b):
    return jnp.dot(a, b, preferred_element_type=F32)


def dot3(a, b):
    rows = a[0].shape[0]
    both = dot(jnp.concatenate([a[0], a[1]], axis=0), b[0])
    return both[:rows] + (both[rows:] + dot(a[0], b[1]))


def right_form(m):
    n = m.shape[0]
    re, im = m[:, :n], m[:, n:]
    return jnp.concatenate([m, jnp.concatenate([-im, re], axis=1)], axis=0)


def right_pair(m):
    high, low = split(m)
    return right_form(high), right_form(low)


def identity(n):
    rows = lax.broadcasted_iota(jnp.int32, (n, 2 * n), 0)
    cols = lax.broadcasted_iota(jnp.int32, (n, 2 * n), 1)
    return (rows == cols).astype(F32)


def inverse_kernel(total, ham_ref, sig_ref, out_ref):
    local_e, _, n, _ = sig_ref.shape
    start = lax.axis_index("energy") * local_e
    eye = identity(n)
    for e in range(local_e):
        pos = jnp.full((1, n), start + e, jnp.int32).astype(F32)
        zre = 5.0 + 2.0 * pos / total
        mag = zre * zre + 1.0
        qre = zre / mag
        qim = -1.0 / mag
        sre = ham_ref[0] + sig_ref[e, 0]
        sim = ham_ref[1] + sig_ref[e, 1]
        a1 = jnp.concatenate([qre * sre - qim * sim, qre * sim + qim * sre], axis=1)
        a1_pair = split(a1)
        a1_right = (right_form(a1_pair[0]), right_form(a1_pair[1]))
        a2 = dot3(a1_pair, a1_right)
        a2_pair = split(a2)
        a2_right = (right_form(a2_pair[0]), right_form(a2_pair[1]))
        a3 = dot3(a1_pair, a2_right)
        a4 = dot3(a2_pair, a2_right)
        p = eye + (a1 + (a2 + a3))
        x = p + dot3(split(p), right_pair(a4))
        re, im = x[:, :n], x[:, n:]
        out_ref[e, 0] = qre * re - qim * im
        out_ref[e, 1] = qre * im + qim * re


def chain_kernel(g_ref, coupling_ref, pattern_ref, out_ref):
    layers, per, _, n, _ = g_ref.shape
    mask = pattern_ref[...].astype(F32)
    bonds = [None] + [coupling_ref[l] * mask for l in range(1, layers)]
    bonds_t = [None] + [b.T for b in bonds[1:]]
    for p in range(per):
        g = [jnp.concatenate([g_ref[l, p, 0], g_ref[l, p, 1]], axis=1) for l in range(layers)]
        down = [None] * layers
        up = [None] * layers
        for l in range(layers):
            high, low = split(g[l])
            tall = (
                jnp.concatenate([high[:, :n], high[:, n:]], axis=0),
                jnp.concatenate([low[:, :n], low[:, n:]], axis=0),
            )
            wide = (high, low)
            if l > 0:
                u = dot3(tall, split(bonds[l]))
                v = dot3(split(bonds_t[l]), wide)
                down[l] = (split(jnp.concatenate([u[:n], u[n:]], axis=1)), right_pair(v))
            if l + 1 < layers:
                u = dot3(tall, split(bonds_t[l + 1]))
                v = dot3(split(bonds[l + 1]), wide)
                up[l] = (split(jnp.concatenate([u[:n], u[n:]], axis=1)), right_pair(v))
        green = list(g)
        gleft = g[0]
        gright = g[layers - 1]
        for step in range(1, layers):
            l = step
            u, v = down[l]
            term = dot3(split(dot3(u, right_pair(gleft))), v)
            green[l] = green[l] + term
            gleft = g[l] + term
            l = layers - 1 - step
            u, v = up[l]
            term = dot3(split(dot3(u, right_pair(gright))), v)
            green[l] = green[l] + term
            gright = g[l] + term
        for l in range(layers):
            near = [green[m] for m in (l - 1, l + 1) if 0 <= m < layers]
            y = green[l] + 0.5 * sum(near[1:], near[0]) if near else green[l]
            out_ref[l, p, 0] = y[:, :n]
            out_ref[l, p, 1] = y[:, n:]


def occupation(pos, total, n):
    return 1.0 / (1.0 + jnp.exp(8.0 * jnp.full((1, n), pos, jnp.int32).astype(F32) / total - 4.0))


def mix_kernel(total, distances, first, last, shift_ref, weight_ref, *refs):
    count = len(distances)
    own, other = refs[:count], refs[count : 2 * count]
    ret_in, les_in = (None, None) if first else refs[2 * count : 2 * count + 2]
    ret_ref, les_ref = refs[-2:]
    local_e, _, n, _ = own[0].shape
    phonons = shift_ref.shape[0]
    start = lax.axis_index("energy") * local_e
    shifts = [shift_ref[m] for m in range(phonons)]
    weights = [weight_ref[m] for m in range(phonons)]

    def coefficient(t):
        value = 0.0
        for s, w in zip(shifts, weights):
            value = value + jnp.where(s == t, w, 0.0)
        return value

    most = total // 2
    coefficients = {}
    for d in distances:
        for t in range(d * local_e - local_e + 1, d * local_e + local_e):
            if 1 <= t <= most and t not in coefficients:
                coefficients[t] = coefficient(t)
    occ_own = {}
    occ_other = {}
    for d in distances:
        for b in range(local_e):
            occ_own[d, b] = occupation(start - d * local_e + b, total, n)
            occ_other[d, b] = occupation(start + d * local_e + b, total, n)
    for a in range(local_e):
        ret = [jnp.zeros((n, n), F32) if first else ret_in[a, c] for c in range(2)]
        les = [jnp.zeros((n, n), F32) if first else les_in[a, c] for c in range(2)]
        for i, d in enumerate(distances):
            for b in range(local_e):
                for source, t, occ, factor in (
                    (own[i], d * local_e + a - b, occ_own[d, b], 1.0),
                    (other[i], d * local_e + b - a, occ_other[d, b], 0.5),
                ):
                    if not 1 <= t <= most:
                        continue
                    w = coefficients[t] * factor
                    for c in range(2):
                        value = w * source[b, c]
                        ret[c] = ret[c] + value
                        les[c] = les[c] + occ * value
        if last:
            les = [les[0] - les[0].T, les[1] + les[1].T]
        for c in range(2):
            ret_ref[a, c] = ret[c]
            les_ref[a, c] = les[c]


def whole(count):
    return [pl.BlockSpec(memory_space=pltpu.VMEM)] * count


def params():
    return pltpu.CompilerParams(vmem_limit_bytes=VMEM_LIMIT)


def shards(hamiltonian, sigma_prev, coupling, coupling_pattern, phonon_shift, phonon_weight):
    local_e, _, n, _ = sigma_prev.shape[2:]
    layers = lax.axis_size("len")
    count = lax.axis_size("energy")
    moms = lax.axis_size("mom")
    total = local_e * count
    per = local_e // layers
    block = (local_e, 2, n, n)

    couplings = lax.all_gather(coupling[0], "len", axis=0)
    g = pl.pallas_call(
        functools.partial(inverse_kernel, total),
        out_shape=jax.ShapeDtypeStruct(block, F32),
        in_specs=whole(2),
        out_specs=pl.BlockSpec(memory_space=pltpu.VMEM),
        compiler_params=params(),
        name="inverse",
    )(hamiltonian[0, 0], sigma_prev[0, 0])
    g = lax.all_to_all(g, "len", split_axis=0, concat_axis=0, tiled=True)
    y = pl.pallas_call(
        chain_kernel,
        out_shape=jax.ShapeDtypeStruct((layers, per, 2, n, n), F32),
        in_specs=whole(3),
        out_specs=pl.BlockSpec(memory_space=pltpu.VMEM),
        compiler_params=params(),
        name="chains",
    )(g.reshape(layers, per, 2, n, n), couplings, coupling_pattern)
    y = lax.all_to_all(y.reshape(block), "len", split_axis=0, concat_axis=0, tiled=True)

    reach = -(-(total // 2) // local_e)
    both = ("energy", "mom")
    up_pairs = [(z, z + 1) for z in range(count - 1)]
    down_pairs = [(z + 1, z) for z in range(count - 1)]
    cross = [
        ((z + 1) * moms + k, z * moms + (moms - 1 - k)) for z in range(count - 1) for k in range(moms)
    ]
    own = [y]
    other = []
    for d in range(1, reach + 1):
        own.append(lax.ppermute(own[-1], "energy", up_pairs))
        if d == 1:
            other.append(lax.ppermute(y, both, cross))
        else:
            other.append(lax.ppermute(other[-1], "energy", down_pairs))
    other.insert(0, lax.ppermute(y, "mom", [(k, moms - 1 - k) for k in range(moms)]))

    groups = [(0, 1)] + [
        tuple(range(d, min(d + 4, reach + 1))) for d in range(2, reach + 1, 4)
    ]
    smem = pl.BlockSpec(memory_space=pltpu.SMEM)
    sums = []
    for i, group in enumerate(groups):
        blocks = [own[d] for d in group] + [other[d] for d in group] + list(sums)
        sums = pl.pallas_call(
            functools.partial(mix_kernel, total, group, i == 0, i == len(groups) - 1),
            out_shape=[jax.ShapeDtypeStruct(block, F32)] * 2,
            in_specs=[smem, smem] + whole(len(blocks)),
            out_specs=whole(2),
            compiler_params=params(),
            name="mix",
        )(phonon_shift, phonon_weight, *blocks)
    retarded, lesser = sums
    return (retarded[None, None], lesser[None, None])


def solution(mesh):
    in_specs = (
        P("mom", "len", None, None, None),
        P("mom", "len", "energy", None, None, None),
        P("len", None, None),
        P(),
        P(),
        P(),
    )
    out_specs = (
        P("mom", "len", "energy", None, None, None),
        P("mom", "len", "energy", None, None, None),
    )
    return jax.shard_map(shards, mesh=mesh, in_specs=in_specs, out_specs=out_specs, check_vma=False)
```

```python
import functools

import jax
import jax.numpy as jnp
from jax import lax
from jax.experimental import pallas as pl
from jax.experimental.pallas import tpu as pltpu
from jax.sharding import PartitionSpec as P

F32 = jnp.float32
BF16 = jnp.bfloat16
VMEM_LIMIT = 16 * 1024 * 1024


def split(x):
    high = x.astype(BF16)
    return high, (x - high.astype(F32)).astype(BF16)


def dot(a, b):
    return jnp.dot(a, b, preferred_element_type=F32)


def dot3(a, b):
    rows = a[0].shape[0]
    both = dot(jnp.concatenate([a[0], a[1]], axis=0), b[0])
    return both[:rows] + (both[rows:] + dot(a[0], b[1]))


def right_form(m):
    n = m.shape[0]
    re, im = m[:, :n], m[:, n:]
    return jnp.concatenate([m, jnp.concatenate([-im, re], axis=1)], axis=0)


def right_pair(m):
    high, low = split(m)
    return right_form(high), right_form(low)


def identity(n):
    rows = lax.broadcasted_iota(jnp.int32, (n, 2 * n), 0)
    cols = lax.broadcasted_iota(jnp.int32, (n, 2 * n), 1)
    return (rows == cols).astype(F32)


def orders(layers):
    first = list(range(1, layers))
    second = list(first)
    if layers > 2:
        second[0], second[1] = second[1], second[0]
    return first, second


def peers(layers):
    here = lax.axis_index("len")
    core = lax.axis_index("mom")
    first, second = orders(layers)
    return [here] + [here ^ jnp.where(core == 0, a, b) for a, b in zip(first, second)]


def inverse_kernel(total, ham_ref, sig_ref, *out_refs):
    local_e, _, n, _ = sig_ref.shape
    layers = len(out_refs)
    per = local_e // layers
    start = lax.axis_index("energy") * local_e
    eye = identity(n)
    for out_ref, peer in reversed(list(zip(out_refs, peers(layers)))):
        for p in range(per):
            e = peer * per + p
            pos = jnp.full((1, n), start + e, jnp.int32).astype(F32)
            zre = 5.0 + 2.0 * pos / total
            mag = zre * zre + 1.0
            qre = zre / mag
            qim = -1.0 / mag
            sre = ham_ref[0] + sig_ref[e, 0]
            sim = ham_ref[1] + sig_ref[e, 1]
            a1 = jnp.concatenate([qre * sre - qim * sim, qre * sim + qim * sre], axis=1)
            a1_pair = split(a1)
            a1_right = (right_form(a1_pair[0]), right_form(a1_pair[1]))
            a2 = dot3(a1_pair, a1_right)
            a2_pair = split(a2)
            a2_right = (right_form(a2_pair[0]), right_form(a2_pair[1]))
            a3 = dot3(a1_pair, a2_right)
            a4 = dot3(a2_pair, a2_right)
            s = eye + (a1 + (a2 + a3))
            x = s + dot3(split(s), right_pair(a4))
            re, im = x[:, :n], x[:, n:]
            out_ref[p, 0] = qre * re - qim * im
            out_ref[p, 1] = qre * im + qim * re


def chain_kernel(layers, *refs):
    g_slots, coupling_slots = refs[:layers], refs[layers : 2 * layers]
    pattern_ref = refs[2 * layers]
    out_slots = refs[2 * layers + 1 : 3 * layers + 1]
    g_ref, bond_ref = refs[3 * layers + 1 :]
    _, per, _, n, _ = g_ref.shape
    mask = pattern_ref[...].astype(F32)
    for peer, g_slot, coupling_slot in zip(peers(layers), g_slots, coupling_slots):
        g_ref[peer] = g_slot[...]
        bond_ref[peer] = coupling_slot[...] * mask
    bonds = [None] + [bond_ref[l] for l in range(1, layers)]
    bonds_t = [None] + [b.T for b in bonds[1:]]
    for p in range(per):
        g = [jnp.concatenate([g_ref[l, p, 0], g_ref[l, p, 1]], axis=1) for l in range(layers)]
        down = [None] * layers
        up = [None] * layers
        for l in range(layers):
            high, low = split(g[l])
            tall = (
                jnp.concatenate([high[:, :n], high[:, n:]], axis=0),
                jnp.concatenate([low[:, :n], low[:, n:]], axis=0),
            )
            wide = (high, low)
            if l > 0:
                u = dot3(tall, split(bonds[l]))
                v = dot3(split(bonds_t[l]), wide)
                down[l] = (split(jnp.concatenate([u[:n], u[n:]], axis=1)), right_pair(v))
            if l + 1 < layers:
                u = dot3(tall, split(bonds_t[l + 1]))
                v = dot3(split(bonds[l + 1]), wide)
                up[l] = (split(jnp.concatenate([u[:n], u[n:]], axis=1)), right_pair(v))
        green = list(g)
        gleft = g[0]
        gright = g[layers - 1]
        for step in range(1, layers):
            l = step
            u, v = down[l]
            term = dot3(split(dot3(u, right_pair(gleft))), v)
            green[l] = green[l] + term
            gleft = g[l] + term
            l = layers - 1 - step
            u, v = up[l]
            term = dot3(split(dot3(u, right_pair(gright))), v)
            green[l] = green[l] + term
            gright = g[l] + term
        for l in range(layers):
            near = [green[m] for m in (l - 1, l + 1) if 0 <= m < layers]
            y = green[l] + 0.5 * sum(near[1:], near[0]) if near else green[l]
            g_ref[l, p, 0] = y[:, :n]
            g_ref[l, p, 1] = y[:, n:]
    for peer, out_slot in zip(peers(layers), out_slots):
        out_slot[...] = g_ref[peer]


def pack_kernel(*refs):
    slots, out_ref = refs[:-1], refs[-1]
    per = slots[0].shape[0]
    for peer, slot in zip(peers(len(slots)), slots):
        for p in range(per):
            out_ref[peer * per + p] = slot[p]


def momenta_kernel(own_ref, other_ref, zero_ref, one_ref):
    core = lax.axis_index("mom")

    @pl.when(core == 0)
    def _():
        zero_ref[...] = own_ref[...]
        one_ref[...] = other_ref[...]

    @pl.when(core != 0)
    def _():
        zero_ref[...] = other_ref[...]
        one_ref[...] = own_ref[...]


def occupation(pos, total, n):
    return 1.0 / (1.0 + jnp.exp(8.0 * jnp.full((1, n), pos, jnp.int32).astype(F32) / total - 4.0))


def mix_kernel(total, distances, first, last, shift_ref, weight_ref, *refs):
    count = len(distances)
    blocks = refs[:count], refs[count : 2 * count]
    sums_in = (None, None) if first else refs[2 * count : 2 * count + 2]
    ret_ref, les_ref = refs[-2:]
    local_e, _, n, _ = blocks[0][0].shape
    phonons = shift_ref.shape[0]
    start = lax.axis_index("energy") * local_e
    core = lax.axis_index("mom")
    shifts = [shift_ref[m] for m in range(phonons)]
    weights = [weight_ref[m] for m in range(phonons)]

    def coefficient(t):
        value = 0.0
        for s, w in zip(shifts, weights):
            value = value + jnp.where(s == t, w, 0.0)
        return value

    def body(own, other):
        ret_in, les_in = sums_in
        most = total // 2
        coefficients = {}
        for d in distances:
            for t in range(d * local_e - local_e + 1, d * local_e + local_e):
                if 1 <= t <= most and t not in coefficients:
                    coefficients[t] = coefficient(t)
        occ_own = {}
        occ_other = {}
        for d in distances:
            for b in range(local_e):
                occ_own[d, b] = occupation(start - d * local_e + b, total, n)
                occ_other[d, b] = occupation(start + d * local_e + b, total, n)
        for a in range(local_e):
            ret = [jnp.zeros((n, n), F32) if first else ret_in[a, c] for c in range(2)]
            les = [jnp.zeros((n, n), F32) if first else les_in[a, c] for c in range(2)]
            for i, d in enumerate(distances):
                for b in range(local_e):
                    for source, t, occ, factor in (
                        (own[i], d * local_e + a - b, occ_own[d, b], 1.0),
                        (other[i], d * local_e + b - a, occ_other[d, b], 0.5),
                    ):
                        if not 1 <= t <= most:
                            continue
                        w = coefficients[t] * factor
                        for c in range(2):
                            value = w * source[b, c]
                            ret[c] = ret[c] + value
                            les[c] = les[c] + occ * value
            if last:
                les = [les[0] - les[0].T, les[1] + les[1].T]
            for c in range(2):
                ret_ref[a, c] = ret[c]
                les_ref[a, c] = les[c]

    @pl.when(core == 0)
    def _():
        body(*blocks)

    @pl.when(core != 0)
    def _():
        body(*blocks[::-1])


def whole(count):
    return [pl.BlockSpec(memory_space=pltpu.VMEM)] * count


def params():
    return pltpu.CompilerParams(vmem_limit_bytes=VMEM_LIMIT)


def shards(hamiltonian, sigma_prev, coupling, coupling_pattern, phonon_shift, phonon_weight):
    local_e, _, n, _ = sigma_prev.shape[2:]
    layers = lax.axis_size("len")
    count = lax.axis_size("energy")
    moms = lax.axis_size("mom")
    total = local_e * count
    per = local_e // layers
    block = jax.ShapeDtypeStruct((local_e, 2, n, n), F32)
    part = jax.ShapeDtypeStruct((per, 2, n, n), F32)

    first, second = orders(layers)

    def exchange(slots):
        received = [slots[0]]
        for slot, a, b in zip(slots[1:], first, second):
            pairs = [
                (l * moms + k, (l ^ (a if k == 0 else b)) * moms + k)
                for l in range(layers)
                for k in range(moms)
            ]
            received.append(lax.ppermute(slot, ("len", "mom"), pairs))
        return received

    couplings = exchange([coupling[0]] * layers)
    g = pl.pallas_call(
        functools.partial(inverse_kernel, total),
        out_shape=[part] * layers,
        in_specs=whole(2),
        out_specs=whole(layers),
        compiler_params=params(),
        name="inverse",
    )(hamiltonian[0, 0], sigma_prev[0, 0])
    y = pl.pallas_call(
        functools.partial(chain_kernel, layers),
        out_shape=[part] * layers,
        in_specs=whole(2 * layers + 1),
        out_specs=whole(layers),
        scratch_shapes=[pltpu.VMEM((layers, per, 2, n, n), F32), pltpu.VMEM((layers, n, n), F32)],
        compiler_params=params(),
        name="chains",
    )(*exchange(g), *couplings, coupling_pattern)
    y = pl.pallas_call(
        pack_kernel,
        out_shape=block,
        in_specs=whole(layers),
        out_specs=whole(1)[0],
        compiler_params=params(),
        name="pack",
    )(*exchange(y))
    swapped = lax.ppermute(y, "mom", [(k, moms - 1 - k) for k in range(moms)])
    zero, one = pl.pallas_call(
        momenta_kernel,
        out_shape=[block] * 2,
        in_specs=whole(2),
        out_specs=whole(2),
        compiler_params=params(),
        name="momenta",
    )(y, swapped)

    reach = -(-(total // 2) // local_e)
    up_down = []
    down_up = []
    for z in range(count - 1):
        low, high = z * moms, (z + 1) * moms
        up_down += [(low, high), (high + 1, low + 1)]
        down_up += [(high, low), (low + 1, high + 1)]
    zeros = [zero]
    ones = [one]
    for d in range(1, reach + 1):
        zeros.append(lax.ppermute(zeros[-1], ("energy", "mom"), up_down))
        ones.append(lax.ppermute(ones[-1], ("energy", "mom"), down_up))

    groups = [(0, 1)] + [
        tuple(range(d, min(d + 4, reach + 1))) for d in range(2, reach + 1, 4)
    ]
    smem = pl.BlockSpec(memory_space=pltpu.SMEM)
    sums = []
    for i, group in enumerate(groups):
        blocks = [zeros[d] for d in group] + [ones[d] for d in group] + list(sums)
        sums = pl.pallas_call(
            functools.partial(mix_kernel, total, group, i == 0, i == len(groups) - 1),
            out_shape=[block] * 2,
            in_specs=[smem, smem] + whole(len(blocks)),
            out_specs=whole(2),
            compiler_params=params(),
            name="mix",
        )(phonon_shift, phonon_weight, *blocks)
    retarded, lesser = sums
    return (retarded[None, None], lesser[None, None])


def solution(mesh):
    in_specs = (
        P("mom", "len", None, None, None),
        P("mom", "len", "energy", None, None, None),
        P("len", None, None),
        P(),
        P(),
        P(),
    )
    out_specs = (
        P("mom", "len", "energy", None, None, None),
        P("mom", "len", "energy", None, None, None),
    )
    return jax.shard_map(shards, mesh=mesh, in_specs=in_specs, out_specs=out_specs, check_vma=False)
```

```python
import functools

import jax
import jax.numpy as jnp
from jax import lax
from jax.experimental import pallas as pl
from jax.experimental.pallas import tpu as pltpu
from jax.sharding import PartitionSpec as P

F32 = jnp.float32
BF16 = jnp.bfloat16
VMEM_LIMIT = 16 * 1024 * 1024


def split(x):
    high = x.astype(BF16)
    return high, (x - high.astype(F32)).astype(BF16)


def dot(a, b):
    return jnp.dot(a, b, preferred_element_type=F32)


def dot3(a, b):
    rows = a[0].shape[0]
    both = dot(jnp.concatenate([a[0], a[1]], axis=0), b[0])
    return both[:rows] + (both[rows:] + dot(a[0], b[1]))


def right_form(m):
    n = m.shape[0]
    re, im = m[:, :n], m[:, n:]
    return jnp.concatenate([m, jnp.concatenate([-im, re], axis=1)], axis=0)


def right_pair(m):
    high, low = split(m)
    return right_form(high), right_form(low)


def identity(n):
    rows = lax.broadcasted_iota(jnp.int32, (n, 2 * n), 0)
    cols = lax.broadcasted_iota(jnp.int32, (n, 2 * n), 1)
    return (rows == cols).astype(F32)


def orders(layers):
    first = list(range(1, layers))
    second = list(first)
    if layers > 2:
        second[0], second[1] = second[1], second[0]
    return first, second


def peers(layers):
    here = lax.axis_index("len")
    core = lax.axis_index("mom")
    first, second = orders(layers)
    return [here] + [here ^ jnp.where(core == 0, a, b) for a, b in zip(first, second)]


def inverse_kernel(total, ham_any, sig_any, coupling_any, pattern_any, *refs):
    ham_ref, sig_ref, coupling_ref, pattern_ref, sems = refs[-5:]
    out_refs = refs[:-5]
    layers, per, _, n, _ = sig_ref.shape
    slots = list(zip(peers(layers), out_refs))[::-1]
    copies = [pltpu.make_async_copy(ham_any, ham_ref, sems.at[layers])]
    for i, (peer, _) in enumerate(slots):
        copies.append(
            pltpu.make_async_copy(sig_any.at[pl.ds(peer * per, per)], sig_ref.at[i], sems.at[i])
        )
    copies.append(pltpu.make_async_copy(coupling_any, coupling_ref, sems.at[layers + 1]))
    copies.append(pltpu.make_async_copy(pattern_any, pattern_ref, sems.at[layers + 2]))
    for copy in copies:
        copy.start()
    start = lax.axis_index("energy") * (layers * per)
    eye = identity(n)
    copies[0].wait()
    for i, (peer, out_ref) in enumerate(slots):
        copies[1 + i].wait()
        for p in range(per):
            pos = jnp.full((1, n), start + peer * per + p, jnp.int32).astype(F32)
            zre = 5.0 + 2.0 * pos / total
            mag = zre * zre + 1.0
            qre = zre / mag
            qim = -1.0 / mag
            sre = ham_ref[0] + sig_ref[i, p, 0]
            sim = ham_ref[1] + sig_ref[i, p, 1]
            a1 = jnp.concatenate([qre * sre - qim * sim, qre * sim + qim * sre], axis=1)
            a1_pair = split(a1)
            a1_right = (right_form(a1_pair[0]), right_form(a1_pair[1]))
            a2 = dot3(a1_pair, a1_right)
            a2_pair = split(a2)
            a2_right = (right_form(a2_pair[0]), right_form(a2_pair[1]))
            a3 = dot3(a1_pair, a2_right)
            a4 = dot3(a2_pair, a2_right)
            s = eye + (a1 + (a2 + a3))
            x = s + dot3(split(s), right_pair(a4))
            re, im = x[:, :n], x[:, n:]
            out_ref[2 * p] = qre * re - qim * im
            out_ref[2 * p + 1] = qre * im + qim * re
    copies[-2].wait()
    copies[-1].wait()
    bond = coupling_ref[...] * pattern_ref[...].astype(F32)
    for _, out_ref in slots:
        out_ref[2 * per] = bond


def chain_kernel(layers, *refs):
    in_slots, out_slots = refs[:layers], refs[layers : 2 * layers]
    g_ref, bond_ref = refs[2 * layers :]
    _, per, _, n, _ = g_ref.shape
    for peer, in_slot in zip(peers(layers), in_slots):
        for p in range(per):
            g_ref[peer, p] = in_slot[2 * p : 2 * p + 2]
        bond_ref[peer] = in_slot[2 * per]
    bonds = [None] + [bond_ref[l] for l in range(1, layers)]
    bonds_t = [None] + [b.T for b in bonds[1:]]
    for p in range(per):
        g = [jnp.concatenate([g_ref[l, p, 0], g_ref[l, p, 1]], axis=1) for l in range(layers)]
        down = [None] * layers
        up = [None] * layers
        for l in range(layers):
            high, low = split(g[l])
            tall = (
                jnp.concatenate([high[:, :n], high[:, n:]], axis=0),
                jnp.concatenate([low[:, :n], low[:, n:]], axis=0),
            )
            wide = (high, low)
            if l > 0:
                u = dot3(tall, split(bonds[l]))
                v = dot3(split(bonds_t[l]), wide)
                down[l] = (split(jnp.concatenate([u[:n], u[n:]], axis=1)), right_pair(v))
            if l + 1 < layers:
                u = dot3(tall, split(bonds_t[l + 1]))
                v = dot3(split(bonds[l + 1]), wide)
                up[l] = (split(jnp.concatenate([u[:n], u[n:]], axis=1)), right_pair(v))
        green = list(g)
        gleft = g[0]
        gright = g[layers - 1]
        for step in range(1, layers):
            l = step
            u, v = down[l]
            term = dot3(split(dot3(u, right_pair(gleft))), v)
            green[l] = green[l] + term
            gleft = g[l] + term
            l = layers - 1 - step
            u, v = up[l]
            term = dot3(split(dot3(u, right_pair(gright))), v)
            green[l] = green[l] + term
            gright = g[l] + term
        for l in range(layers):
            near = [green[m] for m in (l - 1, l + 1) if 0 <= m < layers]
            y = green[l] + 0.5 * sum(near[1:], near[0]) if near else green[l]
            g_ref[l, p, 0] = y[:, :n]
            g_ref[l, p, 1] = y[:, n:]
    for peer, out_slot in zip(peers(layers), out_slots):
        out_slot[...] = g_ref[peer]


def pack_kernel(*refs):
    slots, out_ref = refs[:-1], refs[-1]
    per = slots[0].shape[0]
    for i, slot in enumerate(slots):
        out_ref[i * per : (i + 1) * per] = slot[...]


def momenta_kernel(*refs):
    count = len(refs) // 2 - 1
    own, other = refs[:count], refs[count : 2 * count]
    zero_ref, one_ref = refs[2 * count :]
    core = lax.axis_index("mom")

    @pl.when(core == 0)
    def _():
        pack_kernel(*own, zero_ref)
        pack_kernel(*other, one_ref)

    @pl.when(core != 0)
    def _():
        pack_kernel(*other, zero_ref)
        pack_kernel(*own, one_ref)


def occupation(pos, total, n):
    return 1.0 / (1.0 + jnp.exp(8.0 * jnp.full((1, n), pos, jnp.int32).astype(F32) / total - 4.0))


def mix_kernel(total, distances, chunks, first, last, shift_ref, weight_ref, *refs):
    count = len(distances) * chunks
    blocks = refs[-2:]
    sums_in = (None, None) if first else refs[2 * count : 2 * count + 2]
    ret_ref, les_ref = refs[-4:-2]
    _, local_e, _, n, _ = blocks[0].shape
    layers = lax.axis_size("len")
    per = local_e // layers
    here = lax.axis_index("len")
    each = layers // chunks
    for momentum, order in enumerate(orders(layers)):
        masks = [0] + order
        for i in range(count):
            source = refs[momentum * count + i]
            for s in range(each):
                peer = here ^ masks[i % chunks * each + s]
                for p in range(per):
                    blocks[momentum][i // chunks, peer * per + p] = source[s * per + p]
    phonons = shift_ref.shape[0]
    start = lax.axis_index("energy") * local_e
    core = lax.axis_index("mom")
    shifts = [shift_ref[m] for m in range(phonons)]
    weights = [weight_ref[m] for m in range(phonons)]

    def coefficient(t):
        value = 0.0
        for s, w in zip(shifts, weights):
            value = value + jnp.where(s == t, w, 0.0)
        return value

    def body(own, other):
        ret_in, les_in = sums_in
        most = total // 2
        coefficients = {}
        for d in distances:
            for t in range(d * local_e - local_e + 1, d * local_e + local_e):
                if 1 <= t <= most and t not in coefficients:
                    coefficients[t] = coefficient(t)
        occ_own = {}
        occ_other = {}
        for d in distances:
            for b in range(local_e):
                occ_own[d, b] = occupation(start - d * local_e + b, total, n)
                occ_other[d, b] = occupation(start + d * local_e + b, total, n)
        for a in range(local_e):
            ret = [jnp.zeros((n, n), F32) if first else ret_in[a, c] for c in range(2)]
            les = [jnp.zeros((n, n), F32) if first else les_in[a, c] for c in range(2)]
            for i, d in enumerate(distances):
                for b in range(local_e):
                    for source, t, occ, factor in (
                        (own.at[i], d * local_e + a - b, occ_own[d, b], 1.0),
                        (other.at[i], d * local_e + b - a, occ_other[d, b], 0.5),
                    ):
                        if not 1 <= t <= most:
                            continue
                        w = coefficients[t] * factor
                        for c in range(2):
                            value = w * source[b, c]
                            ret[c] = ret[c] + value
                            les[c] = les[c] + occ * value
            if last:
                les = [les[0] - les[0].T, les[1] + les[1].T]
            for c in range(2):
                ret_ref[a, c] = ret[c]
                les_ref[a, c] = les[c]

    @pl.when(core == 0)
    def _():
        body(*blocks)

    @pl.when(core != 0)
    def _():
        body(*blocks[::-1])


def whole(count):
    return [pl.BlockSpec(memory_space=pltpu.VMEM)] * count


def params():
    return pltpu.CompilerParams(vmem_limit_bytes=VMEM_LIMIT)


def shards(hamiltonian, sigma_prev, coupling, coupling_pattern, phonon_shift, phonon_weight):
    local_e, _, n, _ = sigma_prev.shape[2:]
    layers = lax.axis_size("len")
    count = lax.axis_size("energy")
    moms = lax.axis_size("mom")
    total = local_e * count
    per = local_e // layers
    block = jax.ShapeDtypeStruct((local_e, 2, n, n), F32)
    part = jax.ShapeDtypeStruct((per, 2, n, n), F32)

    first, second = orders(layers)

    def exchange(slots, i):
        if i == 0:
            return slots[0]
        pairs = []
        for l in range(layers):
            for k in range(moms):
                peer = l ^ (first, second)[k][i - 1]
                pairs.append((l * moms + k, peer * moms + k))
        return lax.ppermute(slots[i], ("len", "mom"), pairs)

    anywhere = pl.BlockSpec(memory_space=pltpu.HBM)
    sent = pl.pallas_call(
        functools.partial(inverse_kernel, total),
        out_shape=[jax.ShapeDtypeStruct((2 * per + 1, n, n), F32)] * layers,
        in_specs=[anywhere] * 4,
        out_specs=whole(layers),
        scratch_shapes=[
            pltpu.VMEM((2, n, n), F32),
            pltpu.VMEM((layers, per, 2, n, n), F32),
            pltpu.VMEM((n, n), F32),
            pltpu.VMEM((n, n), jnp.int32),
            pltpu.SemaphoreType.DMA((layers + 3,)),
        ],
        compiler_params=params(),
        name="inverse",
    )(
        *(
            pltpu.with_memory_space_constraint(value, pltpu.HBM)
            for value in (hamiltonian[0, 0], sigma_prev[0, 0], coupling[0], coupling_pattern)
        )
    )
    sent = pl.pallas_call(
        functools.partial(chain_kernel, layers),
        out_shape=[part] * layers,
        in_specs=whole(layers),
        out_specs=whole(layers),
        scratch_shapes=[pltpu.VMEM((layers, per, 2, n, n), F32), pltpu.VMEM((layers, n, n), F32)],
        compiler_params=params(),
        name="chains",
    )(*[exchange(sent, i) for i in range(layers)])
    def swap(value):
        return lax.ppermute(value, "mom", [(k, moms - 1 - k) for k in range(moms)])

    reach = -(-(total // 2) // local_e)

    def hop(value, d, role):
        pairs = []
        for z in range(count - 1):
            low, high = z * moms, (z + 1) * moms
            if z >= d - 1:
                pairs.append((low + role, high + role))
            if z <= count - 1 - d:
                pairs.append((high + 1 - role, low + 1 - role))
        return lax.ppermute(value, ("energy", "mom"), pairs)

    chunks = 2
    each = layers // chunks
    piece = jax.ShapeDtypeStruct((each * per, 2, n, n), F32)
    by_chunk = []
    zeros = [[], []]
    ones = [[], []]
    after = swap(sent[0])
    swapped = [after]
    for c in range(chunks):
        now = range(c * each, (c + 1) * each)
        if c == 0:
            own = [exchange(sent, i) for i in now]
            swapped += [swap(value) for value in own[1:]]
        else:
            own = [exchange(sent, i) for i in now]
            own, _ = lax.optimization_barrier((own, by_chunk[-1]))
            own = [
                pl.pallas_call(
                    pack_kernel,
                    out_shape=piece,
                    in_specs=whole(each),
                    out_specs=whole(1)[0],
                    compiler_params=params(),
                    name="pack",
                )(*own)
            ]
            swapped = [swap(value) for value in own]
        by_chunk.append(
            pl.pallas_call(
                momenta_kernel,
                out_shape=[piece] * 2,
                in_specs=whole(2 * len(own)),
                out_specs=whole(2),
                compiler_params=params(),
                name="momenta",
            )(*own, *swapped)
        )
        zero, one = by_chunk[-1]
        if c > 0:
            zero, _ = lax.optimization_barrier((zero, zeros[1][-1]))
            one, _ = lax.optimization_barrier((one, ones[1][-1]))
        zeros[0].append(zero)
        ones[0].append(one)
        zeros[1].append(hop(zero, 1, 0))
        ones[1].append(hop(one, 1, 1))
        if c == 0:
            later, _ = lax.optimization_barrier((sent[each:], after))
            sent = list(sent[:each]) + list(later)

    for d in range(2, reach + 1):
        zeros.append([hop(value, d, 0) for value in zeros[-1]])
        ones.append([hop(value, d, 1) for value in ones[-1]])

    groups = [(0, 1)] + [
        tuple(range(d, min(d + 4, reach + 1))) for d in range(2, reach + 1, 4)
    ]
    smem = pl.BlockSpec(memory_space=pltpu.SMEM)
    sums = []
    for i, group in enumerate(groups):
        blocks = sum([zeros[d] for d in group] + [ones[d] for d in group], []) + list(sums)
        sums = pl.pallas_call(
            functools.partial(mix_kernel, total, group, chunks, i == 0, i == len(groups) - 1),
            out_shape=[block] * 2,
            in_specs=[smem, smem] + whole(len(blocks)),
            out_specs=whole(2),
            scratch_shapes=[pltpu.VMEM((len(group),) + block.shape, F32)] * 2,
            compiler_params=params(),
            name="mix",
        )(phonon_shift, phonon_weight, *blocks)
    retarded, lesser = sums
    return (retarded[None, None], lesser[None, None])


def solution(mesh):
    in_specs = (
        P("mom", "len", None, None, None),
        P("mom", "len", "energy", None, None, None),
        P("len", None, None),
        P(),
        P(),
        P(),
    )
    out_specs = (
        P("mom", "len", "energy", None, None, None),
        P("mom", "len", "energy", None, None, None),
    )
    return jax.shard_map(shards, mesh=mesh, in_specs=in_specs, out_specs=out_specs, check_vma=False)
```

```python
import functools

import jax
import jax.numpy as jnp
from jax import lax
from jax.experimental import pallas as pl
from jax.experimental.pallas import tpu as pltpu
from jax.sharding import PartitionSpec as P

F32 = jnp.float32
BF16 = jnp.bfloat16
VMEM_LIMIT = 16 * 1024 * 1024


def split(x):
    high = x.astype(BF16)
    return high, (x - high.astype(F32)).astype(BF16)


def dot(a, b):
    return jnp.dot(a, b, preferred_element_type=F32)


def dot3(a, b):
    rows = a[0].shape[0]
    both = dot(jnp.concatenate([a[0], a[1]], axis=0), b[0])
    return both[:rows] + (both[rows:] + dot(a[0], b[1]))


def right_form(m):
    n = m.shape[0]
    re, im = m[:, :n], m[:, n:]
    return jnp.concatenate([m, jnp.concatenate([-im, re], axis=1)], axis=0)


def right_pair(m):
    high, low = split(m)
    return right_form(high), right_form(low)


def identity(n):
    rows = lax.broadcasted_iota(jnp.int32, (n, 2 * n), 0)
    cols = lax.broadcasted_iota(jnp.int32, (n, 2 * n), 1)
    return (rows == cols).astype(F32)


def inverse_kernel(total, ham_any, sig_any, coupling_any, pattern_any, out_ref, *refs):
    buffers, sems = refs[:-1], refs[-1]
    sources = (ham_any, sig_any, coupling_any, pattern_any)
    copies = [
        pltpu.make_async_copy(source, buffer, sems.at[i])
        for i, (source, buffer) in enumerate(zip(sources, buffers))
    ]
    for copy in copies:
        copy.start()
    for copy in copies:
        copy.wait()
    ham_ref, sig_ref, coupling_ref, pattern_ref = buffers
    layers = out_ref.shape[0]
    local_e, _, n, _ = sig_ref.shape
    per = local_e // layers
    start = lax.axis_index("energy") * local_e
    eye = identity(n)
    bond = coupling_ref[...] * pattern_ref[...].astype(F32)
    for l in range(layers):
        out_ref[l, 2 * per] = bond
        for p in range(per):
            e = l * per + p
            pos = jnp.full((1, n), start + e, jnp.int32).astype(F32)
            zre = 5.0 + 2.0 * pos / total
            mag = zre * zre + 1.0
            qre = zre / mag
            qim = -1.0 / mag
            sre = ham_ref[0] + sig_ref[e, 0]
            sim = ham_ref[1] + sig_ref[e, 1]
            a1 = jnp.concatenate([qre * sre - qim * sim, qre * sim + qim * sre], axis=1)
            a1_pair = split(a1)
            a1_right = (right_form(a1_pair[0]), right_form(a1_pair[1]))
            a2 = dot3(a1_pair, a1_right)
            a2_pair = split(a2)
            a2_right = (right_form(a2_pair[0]), right_form(a2_pair[1]))
            a3 = dot3(a1_pair, a2_right)
            a4 = dot3(a2_pair, a2_right)
            s = eye + (a1 + (a2 + a3))
            x = s + dot3(split(s), right_pair(a4))
            re, im = x[:, :n], x[:, n:]
            out_ref[l, 2 * p] = qre * re - qim * im
            out_ref[l, 2 * p + 1] = qre * im + qim * re


def chain_kernel(in_ref, out_ref):
    layers, parts, n, _ = in_ref.shape
    per = parts // 2
    bonds = [None] + [in_ref[l, 2 * per] for l in range(1, layers)]
    bonds_t = [None] + [b.T for b in bonds[1:]]
    for p in range(per):
        g = [
            jnp.concatenate([in_ref[l, 2 * p], in_ref[l, 2 * p + 1]], axis=1)
            for l in range(layers)
        ]
        down = [None] * layers
        up = [None] * layers
        for l in range(layers):
            high, low = split(g[l])
            tall = (
                jnp.concatenate([high[:, :n], high[:, n:]], axis=0),
                jnp.concatenate([low[:, :n], low[:, n:]], axis=0),
            )
            wide = (high, low)
            if l > 0:
                u = dot3(tall, split(bonds[l]))
                v = dot3(split(bonds_t[l]), wide)
                down[l] = (split(jnp.concatenate([u[:n], u[n:]], axis=1)), right_pair(v))
            if l + 1 < layers:
                u = dot3(tall, split(bonds_t[l + 1]))
                v = dot3(split(bonds[l + 1]), wide)
                up[l] = (split(jnp.concatenate([u[:n], u[n:]], axis=1)), right_pair(v))
        green = list(g)
        gleft = g[0]
        gright = g[layers - 1]
        for step in range(1, layers):
            l = step
            u, v = down[l]
            term = dot3(split(dot3(u, right_pair(gleft))), v)
            green[l] = green[l] + term
            gleft = g[l] + term
            l = layers - 1 - step
            u, v = up[l]
            term = dot3(split(dot3(u, right_pair(gright))), v)
            green[l] = green[l] + term
            gright = g[l] + term
        for l in range(layers):
            near = [green[m] for m in (l - 1, l + 1) if 0 <= m < layers]
            y = green[l] + 0.5 * sum(near[1:], near[0]) if near else green[l]
            out_ref[l * per + p, 0] = y[:, :n]
            out_ref[l * per + p, 1] = y[:, n:]

def momenta_kernel(own_ref, other_ref, zero_ref, one_ref):
    core = lax.axis_index("mom")

    @pl.when(core == 0)
    def _():
        zero_ref[...] = own_ref[...]
        one_ref[...] = other_ref[...]

    @pl.when(core != 0)
    def _():
        zero_ref[...] = other_ref[...]
        one_ref[...] = own_ref[...]


def occupation(pos, total, n):
    return 1.0 / (1.0 + jnp.exp(8.0 * jnp.full((1, n), pos, jnp.int32).astype(F32) / total - 4.0))


def mix_kernel(total, distances, first, last, shift_ref, weight_ref, *refs):
    count = len(distances)
    blocks = refs[:count], refs[count : 2 * count]
    inputs = 2 * count + (0 if first else 2)
    sums_in = refs[2 * count : inputs]
    results = refs[inputs : inputs + 2]
    targets = refs[inputs + 2 : inputs + 4] if last else results
    local_e, _, n, _ = blocks[0][0].shape
    phonons = shift_ref.shape[0]
    start = lax.axis_index("energy") * local_e
    core = lax.axis_index("mom")
    shifts = [shift_ref[m] for m in range(phonons)]
    weights = [weight_ref[m] for m in range(phonons)]

    def coefficient(t):
        value = 0.0
        for s, w in zip(shifts, weights):
            value = value + jnp.where(s == t, w, 0.0)
        return value

    def copy_out(i, a):
        return pltpu.make_async_copy(targets[i].at[a], results[i].at[a], refs[-1].at[i, a])

    def body(own, other):
        most = total // 2
        coefficients = {}
        for d in distances:
            for t in range(d * local_e - local_e + 1, d * local_e + local_e):
                if 1 <= t <= most and t not in coefficients:
                    coefficients[t] = coefficient(t)
        occ_own = {}
        occ_other = {}
        for d in distances:
            for b in range(local_e):
                occ_own[d, b] = occupation(start - d * local_e + b, total, n)
                occ_other[d, b] = occupation(start + d * local_e + b, total, n)
        for a in range(local_e):
            if first:
                ret = [jnp.zeros((n, n), F32)] * 2
                les = list(ret)
            else:
                ret = [sums_in[0][a, c] for c in range(2)]
                les = [sums_in[1][a, c] for c in range(2)]
            for i, d in enumerate(distances):
                for b in range(local_e):
                    for source, t, occ, factor in (
                        (own[i], d * local_e + a - b, occ_own[d, b], 1.0),
                        (other[i], d * local_e + b - a, occ_other[d, b], 0.5),
                    ):
                        if not 1 <= t <= most:
                            continue
                        w = coefficients[t] * factor
                        for c in range(2):
                            value = w * source[b, c]
                            ret[c] = ret[c] + value
                            les[c] = les[c] + occ * value
            if last:
                les = [les[0] - les[0].T, les[1] + les[1].T]
            for c in range(2):
                targets[0][a, c] = ret[c]
                targets[1][a, c] = les[c]
            if last:
                copy_out(0, a).start()
                copy_out(1, a).start()

    @pl.when(core == 0)
    def _():
        body(*blocks)

    @pl.when(core != 0)
    def _():
        body(*blocks[::-1])

    if last:
        for a in range(local_e):
            copy_out(0, a).wait()
            copy_out(1, a).wait()


def whole(count):
    return [pl.BlockSpec(memory_space=pltpu.VMEM)] * count


def params():
    return pltpu.CompilerParams(vmem_limit_bytes=VMEM_LIMIT)


def shards(hamiltonian, sigma_prev, coupling, coupling_pattern, phonon_shift, phonon_weight):
    local_e, _, n, _ = sigma_prev.shape[2:]
    layers = lax.axis_size("len")
    count = lax.axis_size("energy")
    moms = lax.axis_size("mom")
    total = local_e * count
    per = local_e // layers
    block = jax.ShapeDtypeStruct((local_e, 2, n, n), F32)
    anywhere = pl.BlockSpec(memory_space=pltpu.HBM)
    inputs = (hamiltonian[0, 0], sigma_prev[0, 0], coupling[0], coupling_pattern)
    sent = pl.pallas_call(
        functools.partial(inverse_kernel, total),
        out_shape=jax.ShapeDtypeStruct((layers, 2 * per + 1, n, n), F32),
        in_specs=[anywhere] * 4,
        out_specs=whole(1)[0],
        scratch_shapes=[pltpu.VMEM(value.shape, value.dtype) for value in inputs]
        + [pltpu.SemaphoreType.DMA((4,))],
        compiler_params=params(),
        name="inverse",
    )(*(pltpu.with_memory_space_constraint(value, pltpu.HBM) for value in inputs))
    sent = pl.pallas_call(
        chain_kernel,
        out_shape=block,
        in_specs=whole(1),
        out_specs=whole(1)[0],
        compiler_params=params(),
        name="chains",
    )(lax.all_to_all(sent, "len", split_axis=0, concat_axis=0, tiled=True))
    own = lax.all_to_all(sent, "len", split_axis=0, concat_axis=0, tiled=True)

    zero, one = pl.pallas_call(
        momenta_kernel,
        out_shape=[block] * 2,
        in_specs=whole(2),
        out_specs=whole(2),
        compiler_params=params(),
        name="momenta",
    )(own, lax.ppermute(own, "mom", [(k, moms - 1 - k) for k in range(moms)]))

    reach = -(-(total // 2) // local_e)

    def hop(value, d, role):
        pairs = []
        for z in range(count - 1):
            low, high = z * moms, (z + 1) * moms
            if z >= d - 1:
                pairs.append((low + role, high + role))
            if z <= count - 1 - d:
                pairs.append((high + 1 - role, low + 1 - role))
        return lax.ppermute(value, ("energy", "mom"), pairs)

    zeros = [zero]
    ones = [one]
    for d in range(1, reach + 1):
        zeros.append(hop(zeros[-1], d, 0))
        ones.append(hop(ones[-1], d, 1))

    groups = [(0, 1)] + [
        tuple(range(d, min(d + 4, reach + 1))) for d in range(2, reach + 1, 4)
    ]
    smem = pl.BlockSpec(memory_space=pltpu.SMEM)
    sums = []
    for i, group in enumerate(groups):
        blocks = [zeros[d] for d in group] + [ones[d] for d in group] + list(sums)
        last = i == len(groups) - 1
        scratch = [pltpu.VMEM(block.shape, F32)] * 2 + [pltpu.SemaphoreType.DMA((2, local_e))]
        sums = pl.pallas_call(
            functools.partial(mix_kernel, total, group, i == 0, last),
            out_shape=[block] * 2,
            in_specs=[smem, smem] + whole(len(blocks)),
            out_specs=[pl.BlockSpec(memory_space=pl.ANY)] * 2 if last else whole(2),
            scratch_shapes=scratch if last else [],
            compiler_params=params(),
            name="mix",
        )(phonon_shift, phonon_weight, *blocks)
    retarded, lesser = sums
    return (retarded[None, None], lesser[None, None])


def solution(mesh):
    in_specs = (
        P("mom", "len", None, None, None),
        P("mom", "len", "energy", None, None, None),
        P("len", None, None),
        P(),
        P(),
        P(),
    )
    out_specs = (
        P("mom", "len", "energy", None, None, None),
        P("mom", "len", "energy", None, None, None),
    )
    return jax.shard_map(shards, mesh=mesh, in_specs=in_specs, out_specs=out_specs, check_vma=False)
```

```python
import functools

import jax
import jax.numpy as jnp
from jax import lax
from jax.experimental import pallas as pl
from jax.experimental.pallas import tpu as pltpu
from jax.sharding import PartitionSpec as P

F32 = jnp.float32
BF16 = jnp.bfloat16
VMEM_LIMIT = 16 * 1024 * 1024


def split(x):
    high = x.astype(BF16)
    return high, (x - high.astype(F32)).astype(BF16)


def dot(a, b):
    return jnp.dot(a, b, preferred_element_type=F32)


def dot3(a, b):
    rows = a[0].shape[0]
    both = dot(jnp.concatenate([a[0], a[1]], axis=0), b[0])
    return both[:rows] + (both[rows:] + dot(a[0], b[1]))


def right_form(m):
    n = m.shape[0]
    re, im = m[:, :n], m[:, n:]
    return jnp.concatenate([m, jnp.concatenate([-im, re], axis=1)], axis=0)


def right_pair(m):
    high, low = split(m)
    return right_form(high), right_form(low)


def identity(n):
    rows = lax.broadcasted_iota(jnp.int32, (n, 2 * n), 0)
    cols = lax.broadcasted_iota(jnp.int32, (n, 2 * n), 1)
    return (rows == cols).astype(F32)


def orders(layers):
    first = list(range(1, layers))
    second = list(first)
    if layers > 2:
        second[0], second[1] = second[1], second[0]
    return first, second


def peers(layers):
    here = lax.axis_index("len")
    core = lax.axis_index("mom")
    first, second = orders(layers)
    return [here] + [here ^ jnp.where(core == 0, a, b) for a, b in zip(first, second)]


def inverse_kernel(total, layers, slots, ham_any, sig_any, coupling_any, pattern_any, *refs):
    out_refs = refs[: len(slots)]
    ham_ref, sig_ref, coupling_ref, pattern_ref, sems = refs[len(slots) :]
    _, per, _, n, _ = sig_ref.shape
    towards = [peers(layers)[slot] for slot in slots]
    copies = [
        pltpu.make_async_copy(ham_any, ham_ref, sems.at[0]),
        pltpu.make_async_copy(coupling_any, coupling_ref, sems.at[1]),
        pltpu.make_async_copy(pattern_any, pattern_ref, sems.at[2]),
    ]
    for i, peer in enumerate(towards):
        group = sig_any.at[pl.ds(peer * per, per)]
        copies.append(pltpu.make_async_copy(group, sig_ref.at[i], sems.at[3 + i]))
    for copy in copies:
        copy.start()
    for copy in copies:
        copy.wait()
    start = lax.axis_index("energy") * (layers * per)
    eye = identity(n)
    bond = coupling_ref[...] * pattern_ref[...].astype(F32)
    for i, (peer, out_ref) in enumerate(zip(towards, out_refs)):
        out_ref[2 * per] = bond
        for p in range(per):
            pos = jnp.full((1, n), start + peer * per + p, jnp.int32).astype(F32)
            zre = 5.0 + 2.0 * pos / total
            mag = zre * zre + 1.0
            qre = zre / mag
            qim = -1.0 / mag
            sre = ham_ref[0] + sig_ref[i, p, 0]
            sim = ham_ref[1] + sig_ref[i, p, 1]
            a1 = jnp.concatenate([qre * sre - qim * sim, qre * sim + qim * sre], axis=1)
            a1_pair = split(a1)
            a1_right = (right_form(a1_pair[0]), right_form(a1_pair[1]))
            a2 = dot3(a1_pair, a1_right)
            a2_pair = split(a2)
            a2_right = (right_form(a2_pair[0]), right_form(a2_pair[1]))
            a3 = dot3(a1_pair, a2_right)
            a4 = dot3(a2_pair, a2_right)
            s = eye + (a1 + (a2 + a3))
            x = s + dot3(split(s), right_pair(a4))
            re, im = x[:, :n], x[:, n:]
            out_ref[2 * p] = qre * re - qim * im
            out_ref[2 * p + 1] = qre * im + qim * re


def chain_kernel(layers, *refs):
    in_slots, out_slots = refs[:layers], refs[layers : 2 * layers]
    g_ref, bond_ref = refs[2 * layers :]
    _, per, _, n, _ = g_ref.shape
    for peer, in_slot in zip(peers(layers), in_slots):
        for p in range(per):
            g_ref[peer, p] = in_slot[2 * p : 2 * p + 2]
        bond_ref[peer] = in_slot[2 * per]
    bonds = [None] + [bond_ref[l] for l in range(1, layers)]
    bonds_t = [None] + [b.T for b in bonds[1:]]
    for p in range(per):
        g = [jnp.concatenate([g_ref[l, p, 0], g_ref[l, p, 1]], axis=1) for l in range(layers)]
        down = [None] * layers
        up = [None] * layers
        for l in range(layers):
            high, low = split(g[l])
            tall = (
                jnp.concatenate([high[:, :n], high[:, n:]], axis=0),
                jnp.concatenate([low[:, :n], low[:, n:]], axis=0),
            )
            wide = (high, low)
            if l > 0:
                u = dot3(tall, split(bonds[l]))
                v = dot3(split(bonds_t[l]), wide)
                down[l] = (split(jnp.concatenate([u[:n], u[n:]], axis=1)), right_pair(v))
            if l + 1 < layers:
                u = dot3(tall, split(bonds_t[l + 1]))
                v = dot3(split(bonds[l + 1]), wide)
                up[l] = (split(jnp.concatenate([u[:n], u[n:]], axis=1)), right_pair(v))
        green = list(g)
        gleft = g[0]
        gright = g[layers - 1]
        for step in range(1, layers):
            l = step
            u, v = down[l]
            term = dot3(split(dot3(u, right_pair(gleft))), v)
            green[l] = green[l] + term
            gleft = g[l] + term
            l = layers - 1 - step
            u, v = up[l]
            term = dot3(split(dot3(u, right_pair(gright))), v)
            green[l] = green[l] + term
            gright = g[l] + term
        for l in range(layers):
            near = [green[m] for m in (l - 1, l + 1) if 0 <= m < layers]
            y = green[l] + 0.5 * sum(near[1:], near[0]) if near else green[l]
            g_ref[l, p, 0] = y[:, :n]
            g_ref[l, p, 1] = y[:, n:]
    for peer, out_slot in zip(peers(layers), out_slots):
        out_slot[...] = g_ref[peer]


def momenta_kernel(layers, *refs):
    core = lax.axis_index("mom")
    here = lax.axis_index("len")
    per = refs[0].shape[0]
    first, second = orders(layers)

    def place(slots, order, out_ref):
        for mask, slot in zip([0] + order, slots):
            for p in range(per):
                out_ref[(here ^ mask) * per + p] = slot[p]

    own, other = refs[:layers], refs[layers : 2 * layers]

    @pl.when(core == 0)
    def _():
        place(own, first, refs[-2])
        place(other, second, refs[-1])

    @pl.when(core != 0)
    def _():
        place(other, first, refs[-2])
        place(own, second, refs[-1])


def occupation(pos, total, n):
    return 1.0 / (1.0 + jnp.exp(8.0 * jnp.full((1, n), pos, jnp.int32).astype(F32) / total - 4.0))


def mix_kernel(total, distances, first, last, shift_ref, weight_ref, *refs):
    count = len(distances)
    blocks = refs[:count], refs[count : 2 * count]
    inputs = 2 * count + (0 if first else 2)
    sums_in = refs[2 * count : inputs]
    results = refs[inputs : inputs + 2]
    targets = refs[inputs + 2 : inputs + 4] if last else results
    local_e, _, n, _ = blocks[0][0].shape
    phonons = shift_ref.shape[0]
    start = lax.axis_index("energy") * local_e
    core = lax.axis_index("mom")
    shifts = [shift_ref[m] for m in range(phonons)]
    weights = [weight_ref[m] for m in range(phonons)]

    def coefficient(t):
        value = 0.0
        for s, w in zip(shifts, weights):
            value = value + jnp.where(s == t, w, 0.0)
        return value

    def copy_out(i, a):
        return pltpu.make_async_copy(targets[i].at[a], results[i].at[a], refs[-1].at[i, a])

    def body(own, other):
        most = total // 2
        coefficients = {}
        for d in distances:
            for t in range(d * local_e - local_e + 1, d * local_e + local_e):
                if 1 <= t <= most and t not in coefficients:
                    coefficients[t] = coefficient(t)
        occ_own = {}
        occ_other = {}
        for d in distances:
            for b in range(local_e):
                occ_own[d, b] = occupation(start - d * local_e + b, total, n)
                occ_other[d, b] = occupation(start + d * local_e + b, total, n)
        for a in range(local_e):
            if first:
                ret = [jnp.zeros((n, n), F32)] * 2
                les = list(ret)
            else:
                ret = [sums_in[0][a, c] for c in range(2)]
                les = [sums_in[1][a, c] for c in range(2)]
            for i, d in enumerate(distances):
                for b in range(local_e):
                    for source, t, occ, factor in (
                        (own[i], d * local_e + a - b, occ_own[d, b], 1.0),
                        (other[i], d * local_e + b - a, occ_other[d, b], 0.5),
                    ):
                        if not 1 <= t <= most:
                            continue
                        w = coefficients[t] * factor
                        for c in range(2):
                            value = w * source[b, c]
                            ret[c] = ret[c] + value
                            les[c] = les[c] + occ * value
            if last:
                les = [les[0] - les[0].T, les[1] + les[1].T]
            for c in range(2):
                targets[0][a, c] = ret[c]
                targets[1][a, c] = les[c]
            if last:
                copy_out(0, a).start()
                copy_out(1, a).start()

    @pl.when(core == 0)
    def _():
        body(*blocks)

    @pl.when(core != 0)
    def _():
        body(*blocks[::-1])

    if last:
        for a in range(local_e):
            copy_out(0, a).wait()
            copy_out(1, a).wait()


def whole(count):
    return [pl.BlockSpec(memory_space=pltpu.VMEM)] * count


def params():
    return pltpu.CompilerParams(vmem_limit_bytes=VMEM_LIMIT)


def shards(hamiltonian, sigma_prev, coupling, coupling_pattern, phonon_shift, phonon_weight):
    local_e, _, n, _ = sigma_prev.shape[2:]
    layers = lax.axis_size("len")
    count = lax.axis_size("energy")
    moms = lax.axis_size("mom")
    total = local_e * count
    per = local_e // layers
    block = jax.ShapeDtypeStruct((local_e, 2, n, n), F32)
    first, second = orders(layers)

    def exchange(slots, i):
        if i == 0:
            return slots[0]
        pairs = []
        for l in range(layers):
            for k in range(moms):
                peer = l ^ (first, second)[k][i - 1]
                pairs.append((l * moms + k, peer * moms + k))
        return lax.ppermute(slots[i], ("len", "mom"), pairs)

    anywhere = pl.BlockSpec(memory_space=pltpu.HBM)
    inputs = (hamiltonian[0, 0], sigma_prev[0, 0], coupling[0], coupling_pattern)
    inputs = [pltpu.with_memory_space_constraint(value, pltpu.HBM) for value in inputs]

    def inverse(slots):
        return pl.pallas_call(
            functools.partial(inverse_kernel, total, layers, slots),
            out_shape=[jax.ShapeDtypeStruct((2 * per + 1, n, n), F32)] * len(slots),
            in_specs=[anywhere] * 4,
            out_specs=whole(len(slots)),
            scratch_shapes=[
                pltpu.VMEM((2, n, n), F32),
                pltpu.VMEM((len(slots), per, 2, n, n), F32),
                pltpu.VMEM((n, n), F32),
                pltpu.VMEM((n, n), jnp.int32),
                pltpu.SemaphoreType.DMA((3 + len(slots),)),
            ],
            compiler_params=params(),
            cost_estimate=pl.CostEstimate(
                flops=len(slots) * per * 96 * n**3, bytes_accessed=len(slots) * 8 * n * n, transcendentals=0
            ),
            name="inverse",
        )(*inputs)

    half = (layers + 1) // 2
    early = tuple(range(1, half + 1))
    late = tuple(range(half + 1, layers)) + (0,)
    sent = dict(zip(early, inverse(early))) | dict(zip(late, inverse(late)))
    part = jax.ShapeDtypeStruct((per, 2, n, n), F32)
    sent = pl.pallas_call(
        functools.partial(chain_kernel, layers),
        out_shape=[part] * layers,
        in_specs=whole(layers),
        out_specs=whole(layers),
        scratch_shapes=[pltpu.VMEM((layers, per, 2, n, n), F32), pltpu.VMEM((layers, n, n), F32)],
        compiler_params=params(),
        name="chains",
    )(*[exchange(sent, i) for i in range(layers)])
    own = [exchange(sent, i) for i in range(layers)]
    other = [lax.ppermute(v, "mom", [(k, moms - 1 - k) for k in range(moms)]) for v in own]
    zero, one = pl.pallas_call(
        functools.partial(momenta_kernel, layers),
        out_shape=[block] * 2,
        in_specs=whole(2 * layers),
        out_specs=whole(2),
        compiler_params=params(),
        name="momenta",
    )(*own, *other)

    reach = -(-(total // 2) // local_e)

    def hop(value, d, role):
        pairs = []
        for z in range(count - 1):
            low, high = z * moms, (z + 1) * moms
            if z >= d - 1:
                pairs.append((low + role, high + role))
            if z <= count - 1 - d:
                pairs.append((high + 1 - role, low + 1 - role))
        return lax.ppermute(value, ("energy", "mom"), pairs)

    zeros = [zero]
    ones = [one]
    for d in range(1, reach + 1):
        zeros.append(hop(zeros[-1], d, 0))
        ones.append(hop(ones[-1], d, 1))

    groups = [(0, 1)] + [
        tuple(range(d, min(d + 4, reach + 1))) for d in range(2, reach + 1, 4)
    ]
    smem = pl.BlockSpec(memory_space=pltpu.SMEM)
    sums = []
    for i, group in enumerate(groups):
        blocks = [zeros[d] for d in group] + [ones[d] for d in group] + list(sums)
        last = i == len(groups) - 1
        scratch = [pltpu.VMEM(block.shape, F32)] * 2 + [pltpu.SemaphoreType.DMA((2, local_e))]
        sums = pl.pallas_call(
            functools.partial(mix_kernel, total, group, i == 0, last),
            out_shape=[block] * 2,
            in_specs=[smem, smem] + whole(len(blocks)),
            out_specs=[pl.BlockSpec(memory_space=pl.ANY)] * 2 if last else whole(2),
            scratch_shapes=scratch if last else [],
            compiler_params=params(),
            name="mix",
        )(phonon_shift, phonon_weight, *blocks)
    retarded, lesser = sums
    return (retarded[None, None], lesser[None, None])


def solution(mesh):
    in_specs = (
        P("mom", "len", None, None, None),
        P("mom", "len", "energy", None, None, None),
        P("len", None, None),
        P(),
        P(),
        P(),
    )
    out_specs = (
        P("mom", "len", "energy", None, None, None),
        P("mom", "len", "energy", None, None, None),
    )
    return jax.shard_map(shards, mesh=mesh, in_specs=in_specs, out_specs=out_specs, check_vma=False)
```

```python
import functools

import jax
import jax.numpy as jnp
from jax import lax
from jax.experimental import pallas as pl
from jax.experimental.pallas import tpu as pltpu
from jax.sharding import PartitionSpec as P

F32 = jnp.float32
BF16 = jnp.bfloat16
VMEM_LIMIT = 16 * 1024 * 1024


def split(x):
    high = x.astype(BF16)
    return high, (x - high.astype(F32)).astype(BF16)


def dot(a, b):
    return jnp.dot(a, b, preferred_element_type=F32)


def dot3(a, b):
    rows = a[0].shape[0]
    both = dot(jnp.concatenate([a[0], a[1]], axis=0), b[0])
    return both[:rows] + (both[rows:] + dot(a[0], b[1]))


def right_form(m):
    n = m.shape[0]
    re, im = m[:, :n], m[:, n:]
    return jnp.concatenate([m, jnp.concatenate([-im, re], axis=1)], axis=0)


def right_pair(m):
    high, low = split(m)
    return right_form(high), right_form(low)


def identity(n):
    rows = lax.broadcasted_iota(jnp.int32, (n, 2 * n), 0)
    cols = lax.broadcasted_iota(jnp.int32, (n, 2 * n), 1)
    return (rows == cols).astype(F32)


def orders(layers):
    first = list(range(1, layers))
    second = list(first)
    if layers > 2:
        second[0], second[1] = second[1], second[0]
    return first, second


def peers(layers):
    here = lax.axis_index("len")
    core = lax.axis_index("mom")
    first, second = orders(layers)
    return [here] + [here ^ jnp.where(core == 0, a, b) for a, b in zip(first, second)]


def inverse_kernel(total, layers, slots, ham_any, sig_any, coupling_any, pattern_any, *refs):
    out_refs = refs[: len(slots)]
    ham_ref, sig_ref, coupling_ref, pattern_ref, sems = refs[len(slots) :]
    _, per, _, n, _ = sig_ref.shape
    towards = [peers(layers)[slot] for slot in slots]
    copies = [
        pltpu.make_async_copy(ham_any, ham_ref, sems.at[0]),
        pltpu.make_async_copy(coupling_any, coupling_ref, sems.at[1]),
        pltpu.make_async_copy(pattern_any, pattern_ref, sems.at[2]),
    ]
    for i, peer in enumerate(towards):
        group = sig_any.at[pl.ds(peer * per, per)]
        copies.append(pltpu.make_async_copy(group, sig_ref.at[i], sems.at[3 + i]))
    for copy in copies:
        copy.start()
    for copy in copies:
        copy.wait()
    start = lax.axis_index("energy") * (layers * per)
    eye = identity(n)
    bond = coupling_ref[...] * pattern_ref[...].astype(F32)
    for i, (peer, out_ref) in enumerate(zip(towards, out_refs)):
        out_ref[2 * per] = bond
        for p in range(per):
            pos = jnp.full((1, n), start + peer * per + p, jnp.int32).astype(F32)
            zre = 5.0 + 2.0 * pos / total
            mag = zre * zre + 1.0
            qre = zre / mag
            qim = -1.0 / mag
            sre = ham_ref[0] + sig_ref[i, p, 0]
            sim = ham_ref[1] + sig_ref[i, p, 1]
            a1 = jnp.concatenate([qre * sre - qim * sim, qre * sim + qim * sre], axis=1)
            a1_pair = split(a1)
            a1_right = (right_form(a1_pair[0]), right_form(a1_pair[1]))
            a2 = dot3(a1_pair, a1_right)
            a2_pair = split(a2)
            a2_right = (right_form(a2_pair[0]), right_form(a2_pair[1]))
            a3 = dot3(a1_pair, a2_right)
            a4 = dot3(a2_pair, a2_right)
            s = eye + (a1 + (a2 + a3))
            x = s + dot3(split(s), right_pair(a4))
            re, im = x[:, :n], x[:, n:]
            out_ref[2 * p] = qre * re - qim * im
            out_ref[2 * p + 1] = qre * im + qim * re


def chain_kernel(layers, *refs):
    in_slots, out_slots = refs[:layers], refs[layers : 2 * layers]
    g_ref, bond_ref = refs[2 * layers :]
    _, per, _, n, _ = g_ref.shape
    for peer, in_slot in zip(peers(layers), in_slots):
        for p in range(per):
            g_ref[peer, p] = in_slot[2 * p : 2 * p + 2]
        bond_ref[peer] = in_slot[2 * per]
    bonds = [None] + [bond_ref[l] for l in range(1, layers)]
    bonds_t = [None] + [b.T for b in bonds[1:]]
    for p in range(per):
        g = [jnp.concatenate([g_ref[l, p, 0], g_ref[l, p, 1]], axis=1) for l in range(layers)]
        down = [None] * layers
        up = [None] * layers
        for l in range(layers):
            high, low = split(g[l])
            tall = (
                jnp.concatenate([high[:, :n], high[:, n:]], axis=0),
                jnp.concatenate([low[:, :n], low[:, n:]], axis=0),
            )
            wide = (high, low)
            if l > 0:
                u = dot3(tall, split(bonds[l]))
                v = dot3(split(bonds_t[l]), wide)
                down[l] = (split(jnp.concatenate([u[:n], u[n:]], axis=1)), right_pair(v))
            if l + 1 < layers:
                u = dot3(tall, split(bonds_t[l + 1]))
                v = dot3(split(bonds[l + 1]), wide)
                up[l] = (split(jnp.concatenate([u[:n], u[n:]], axis=1)), right_pair(v))
        green = list(g)
        gleft = g[0]
        gright = g[layers - 1]
        for step in range(1, layers):
            l = step
            u, v = down[l]
            term = dot3(split(dot3(u, right_pair(gleft))), v)
            green[l] = green[l] + term
            gleft = g[l] + term
            l = layers - 1 - step
            u, v = up[l]
            term = dot3(split(dot3(u, right_pair(gright))), v)
            green[l] = green[l] + term
            gright = g[l] + term
        for l in range(layers):
            near = [green[m] for m in (l - 1, l + 1) if 0 <= m < layers]
            y = green[l] + 0.5 * sum(near[1:], near[0]) if near else green[l]
            g_ref[l, p, 0] = y[:, :n]
            g_ref[l, p, 1] = y[:, n:]
    for peer, out_slot in zip(peers(layers), out_slots):
        out_slot[...] = g_ref[peer]


def momentum_kernel(momentum, layers, *refs):
    core = lax.axis_index("mom")
    here = lax.axis_index("len")
    out_ref = refs[-1]
    per = refs[0].shape[0]
    masks = [0] + orders(layers)[momentum]

    def place(slots):
        for mask, slot in zip(masks, slots):
            for p in range(per):
                out_ref[(here ^ mask) * per + p] = slot[p]

    @pl.when(core == momentum)
    def _():
        place(refs[:layers])

    @pl.when(core != momentum)
    def _():
        place(refs[layers : 2 * layers])


def occupation(pos, total, n):
    return 1.0 / (1.0 + jnp.exp(8.0 * jnp.full((1, n), pos, jnp.int32).astype(F32) / total - 4.0))


def mix_kernel(total, items, first, last, shift_ref, weight_ref, *refs):
    count = len(items)
    inputs = count + (0 if first else 2)
    sums_in = refs[count:inputs]
    results = refs[inputs : inputs + 2]
    targets = refs[inputs + 2 : inputs + 4] if last else results
    local_e, _, n, _ = refs[0].shape
    phonons = shift_ref.shape[0]
    start = lax.axis_index("energy") * local_e
    core = lax.axis_index("mom")
    shifts = [shift_ref[m] for m in range(phonons)]
    weights = [weight_ref[m] for m in range(phonons)]

    def coefficient(t):
        value = 0.0
        for s, w in zip(shifts, weights):
            value = value + jnp.where(s == t, w, 0.0)
        return value

    def copy_out(i, a):
        return pltpu.make_async_copy(targets[i].at[a], results[i].at[a], refs[-1].at[i, a])

    def body(here):
        most = total // 2
        coefficients = {}
        terms = [[] for _ in range(local_e)]
        for i, (momentum, d) in enumerate(items):
            sign, factor = (-1, 1.0) if momentum == here else (1, 0.5)
            for b in range(local_e):
                occ = occupation(start + sign * d * local_e + b, total, n)
                for a in range(local_e):
                    t = d * local_e + sign * (b - a)
                    if 1 <= t <= most:
                        if t not in coefficients:
                            coefficients[t] = coefficient(t)
                        terms[a].append((refs[i], b, coefficients[t] * factor, occ))
        for a in range(local_e):
            if first:
                ret = [jnp.zeros((n, n), F32)] * 2
                les = list(ret)
            else:
                ret = [sums_in[0][a, c] for c in range(2)]
                les = [sums_in[1][a, c] for c in range(2)]
            for source, b, w, occ in terms[a]:
                for c in range(2):
                    value = w * source[b, c]
                    ret[c] = ret[c] + value
                    les[c] = les[c] + occ * value
            if last:
                les = [les[0] - les[0].T, les[1] + les[1].T]
            for c in range(2):
                targets[0][a, c] = ret[c]
                targets[1][a, c] = les[c]
            if last:
                copy_out(0, a).start()
                copy_out(1, a).start()

    @pl.when(core == 0)
    def _():
        body(0)

    @pl.when(core != 0)
    def _():
        body(1)

    if last:
        for a in range(local_e):
            copy_out(0, a).wait()
            copy_out(1, a).wait()


def whole(count):
    return [pl.BlockSpec(memory_space=pltpu.VMEM)] * count


def params():
    return pltpu.CompilerParams(vmem_limit_bytes=VMEM_LIMIT)


def shards(hamiltonian, sigma_prev, coupling, coupling_pattern, phonon_shift, phonon_weight):
    local_e, _, n, _ = sigma_prev.shape[2:]
    layers = lax.axis_size("len")
    count = lax.axis_size("energy")
    moms = lax.axis_size("mom")
    total = local_e * count
    per = local_e // layers
    block = jax.ShapeDtypeStruct((local_e, 2, n, n), F32)
    first, second = orders(layers)

    def exchange(slots, i):
        if i == 0:
            return slots[0]
        pairs = []
        for l in range(layers):
            for k in range(moms):
                peer = l ^ (first, second)[k][i - 1]
                pairs.append((l * moms + k, peer * moms + k))
        return lax.ppermute(slots[i], ("len", "mom"), pairs)

    anywhere = pl.BlockSpec(memory_space=pltpu.HBM)
    inputs = (hamiltonian[0, 0], sigma_prev[0, 0], coupling[0], coupling_pattern)
    inputs = [pltpu.with_memory_space_constraint(value, pltpu.HBM) for value in inputs]

    def inverse(slots):
        return pl.pallas_call(
            functools.partial(inverse_kernel, total, layers, slots),
            out_shape=[jax.ShapeDtypeStruct((2 * per + 1, n, n), F32)] * len(slots),
            in_specs=[anywhere] * 4,
            out_specs=whole(len(slots)),
            scratch_shapes=[
                pltpu.VMEM((2, n, n), F32),
                pltpu.VMEM((len(slots), per, 2, n, n), F32),
                pltpu.VMEM((n, n), F32),
                pltpu.VMEM((n, n), jnp.int32),
                pltpu.SemaphoreType.DMA((3 + len(slots),)),
            ],
            compiler_params=params(),
            cost_estimate=pl.CostEstimate(
                flops=len(slots) * per * 96 * n**3, bytes_accessed=len(slots) * 8 * n * n, transcendentals=0
            ),
            name="inverse",
        )(*inputs)

    half = (layers + 1) // 2
    early = tuple(range(1, half + 1))
    late = tuple(range(half + 1, layers)) + (0,)
    sent = dict(zip(early, inverse(early))) | dict(zip(late, inverse(late)))
    part = jax.ShapeDtypeStruct((per, 2, n, n), F32)
    sent = pl.pallas_call(
        functools.partial(chain_kernel, layers),
        out_shape=[part] * layers,
        in_specs=whole(layers),
        out_specs=whole(layers),
        scratch_shapes=[pltpu.VMEM((layers, per, 2, n, n), F32), pltpu.VMEM((layers, n, n), F32)],
        compiler_params=params(),
        name="chains",
    )(*[exchange(sent, i) for i in range(layers)])
    own = [exchange(sent, i) for i in range(layers)]
    both_ways = [(k, moms - 1 - k) for k in range(moms)]
    other = [lax.ppermute(v, "mom", both_ways) for v in own[:-1]]

    def momentum_blocks(momentum, last_slot):
        return pl.pallas_call(
            functools.partial(momentum_kernel, momentum, layers),
            out_shape=block,
            in_specs=whole(2 * layers),
            out_specs=whole(1)[0],
            compiler_params=params(),
            name="momentum",
        )(*own, *other, last_slot)

    zero = momentum_blocks(0, lax.ppermute(own[-1], "mom", both_ways[:1]))
    held, _ = lax.optimization_barrier((own[-1], zero))
    one = momentum_blocks(1, lax.ppermute(held, "mom", both_ways[1:]))

    reach = -(-(total // 2) // local_e)

    def hop(value, d, role):
        pairs = []
        for z in range(count - 1):
            low, high = z * moms, (z + 1) * moms
            if z >= d - 1:
                pairs.append((low + role, high + role))
            if z <= count - 1 - d:
                pairs.append((high + 1 - role, low + 1 - role))
        return lax.ppermute(value, ("energy", "mom"), pairs)

    smem = pl.BlockSpec(memory_space=pltpu.SMEM)

    def mix(items, blocks, sums, last=False):
        scratch = [pltpu.VMEM(block.shape, F32)] * 2 + [pltpu.SemaphoreType.DMA((2, local_e))]
        return pl.pallas_call(
            functools.partial(mix_kernel, total, items, not sums, last),
            out_shape=[block] * 2,
            in_specs=[smem, smem] + whole(len(blocks) + len(sums)),
            out_specs=[pl.BlockSpec(memory_space=pl.ANY)] * 2 if last else whole(2),
            scratch_shapes=scratch if last else [],
            compiler_params=params(),
            name="mix",
        )(phonon_shift, phonon_weight, *blocks, *sums)

    sums = mix([(0, 0), (1, 0)], [zero, one], [])
    one, _ = lax.optimization_barrier((one, sums))
    for d in range(1, reach + 1):
        zero = hop(zero, d, 0)
        one = hop(one, d, 1)
        if d < reach:
            sums = mix([(0, d), (1, d)], [zero, one], sums)
    sums = mix([(0, reach)], [zero], sums)
    sums = mix([(1, reach)], [one], sums, last=True)
    retarded, lesser = sums
    return (retarded[None, None], lesser[None, None])


def solution(mesh):
    in_specs = (
        P("mom", "len", None, None, None),
        P("mom", "len", "energy", None, None, None),
        P("len", None, None),
        P(),
        P(),
        P(),
    )
    out_specs = (
        P("mom", "len", "energy", None, None, None),
        P("mom", "len", "energy", None, None, None),
    )
    return jax.shard_map(shards, mesh=mesh, in_specs=in_specs, out_specs=out_specs, check_vma=False)
```

```python
import functools

import jax
import jax.numpy as jnp
from jax import lax
from jax.experimental import pallas as pl
from jax.experimental.pallas import tpu as pltpu
from jax.sharding import PartitionSpec as P

F32 = jnp.float32
BF16 = jnp.bfloat16
VMEM_LIMIT = 16 * 1024 * 1024


def split(x):
    high = x.astype(BF16)
    return high, (x - high.astype(F32)).astype(BF16)


def dot(a, b):
    return jnp.dot(a, b, preferred_element_type=F32)


def dot3(a, b):
    rows = a[0].shape[0]
    both = dot(jnp.concatenate([a[0], a[1]], axis=0), b[0])
    return both[:rows] + (both[rows:] + dot(a[0], b[1]))


def right_form(m):
    n = m.shape[0]
    re, im = m[:, :n], m[:, n:]
    return jnp.concatenate([m, jnp.concatenate([-im, re], axis=1)], axis=0)


def right_pair(m):
    high, low = split(m)
    return right_form(high), right_form(low)


def identity(n):
    rows = lax.broadcasted_iota(jnp.int32, (n, 2 * n), 0)
    cols = lax.broadcasted_iota(jnp.int32, (n, 2 * n), 1)
    return (rows == cols).astype(F32)


def orders(layers):
    first = [layers - 1] + list(range(1, layers - 1))
    second = list(first)
    if layers > 3:
        second[1], second[2] = second[2], second[1]
    return first, second


def peers(layers):
    here = lax.axis_index("len")
    core = lax.axis_index("mom")
    first, second = orders(layers)
    return [here] + [here ^ jnp.where(core == 0, a, b) for a, b in zip(first, second)]


def inverse_kernel(total, layers, slots, ham_any, sig_any, coupling_any, pattern_any, *refs):
    out_refs = refs[: len(slots)]
    ham_ref, sig_ref, coupling_ref, pattern_ref, sems = refs[len(slots) :]
    _, per, _, n, _ = sig_ref.shape
    towards = [peers(layers)[slot] for slot in slots]
    copies = [
        pltpu.make_async_copy(ham_any, ham_ref, sems.at[0]),
        pltpu.make_async_copy(coupling_any, coupling_ref, sems.at[1]),
        pltpu.make_async_copy(pattern_any, pattern_ref, sems.at[2]),
    ]
    for i, peer in enumerate(towards):
        group = sig_any.at[pl.ds(peer * per, per)]
        copies.append(pltpu.make_async_copy(group, sig_ref.at[i], sems.at[3 + i]))
    for copy in copies:
        copy.start()
    for copy in copies:
        copy.wait()
    start = lax.axis_index("energy") * (layers * per)
    eye = identity(n)
    bond = coupling_ref[...] * pattern_ref[...].astype(F32)
    for i, (peer, out_ref) in enumerate(zip(towards, out_refs)):
        out_ref[2 * per] = bond
        for p in range(per):
            pos = jnp.full((1, n), start + peer * per + p, jnp.int32).astype(F32)
            zre = 5.0 + 2.0 * pos / total
            mag = zre * zre + 1.0
            qre = zre / mag
            qim = -1.0 / mag
            sre = ham_ref[0] + sig_ref[i, p, 0]
            sim = ham_ref[1] + sig_ref[i, p, 1]
            a1 = jnp.concatenate([qre * sre - qim * sim, qre * sim + qim * sre], axis=1)
            a1_pair = split(a1)
            a1_right = (right_form(a1_pair[0]), right_form(a1_pair[1]))
            a2 = dot3(a1_pair, a1_right)
            a2_pair = split(a2)
            a2_right = (right_form(a2_pair[0]), right_form(a2_pair[1]))
            a3 = dot3(a1_pair, a2_right)
            a4 = dot3(a2_pair, a2_right)
            s = eye + (a1 + (a2 + a3))
            x = s + dot3(split(s), right_pair(a4))
            re, im = x[:, :n], x[:, n:]
            out_ref[2 * p] = qre * re - qim * im
            out_ref[2 * p + 1] = qre * im + qim * re


def chain_kernel(layers, *refs):
    in_slots, out_slots = refs[:layers], refs[layers : 2 * layers]
    g_ref, bond_ref = refs[2 * layers :]
    _, per, _, n, _ = g_ref.shape
    for peer, in_slot in zip(peers(layers), in_slots):
        for p in range(per):
            g_ref[peer, p] = in_slot[2 * p : 2 * p + 2]
        bond_ref[peer] = in_slot[2 * per]
    bonds = [None] + [bond_ref[l] for l in range(1, layers)]
    bonds_t = [None] + [b.T for b in bonds[1:]]
    for p in range(per):
        g = [jnp.concatenate([g_ref[l, p, 0], g_ref[l, p, 1]], axis=1) for l in range(layers)]
        down = [None] * layers
        up = [None] * layers
        for l in range(layers):
            high, low = split(g[l])
            tall = (
                jnp.concatenate([high[:, :n], high[:, n:]], axis=0),
                jnp.concatenate([low[:, :n], low[:, n:]], axis=0),
            )
            wide = (high, low)
            if l > 0:
                u = dot3(tall, split(bonds[l]))
                v = dot3(split(bonds_t[l]), wide)
                down[l] = (split(jnp.concatenate([u[:n], u[n:]], axis=1)), right_pair(v))
            if l + 1 < layers:
                u = dot3(tall, split(bonds_t[l + 1]))
                v = dot3(split(bonds[l + 1]), wide)
                up[l] = (split(jnp.concatenate([u[:n], u[n:]], axis=1)), right_pair(v))
        green = list(g)
        gleft = g[0]
        gright = g[layers - 1]
        for step in range(1, layers):
            l = step
            u, v = down[l]
            term = dot3(split(dot3(u, right_pair(gleft))), v)
            green[l] = green[l] + term
            gleft = g[l] + term
            l = layers - 1 - step
            u, v = up[l]
            term = dot3(split(dot3(u, right_pair(gright))), v)
            green[l] = green[l] + term
            gright = g[l] + term
        for l in range(layers):
            near = [green[m] for m in (l - 1, l + 1) if 0 <= m < layers]
            y = green[l] + 0.5 * sum(near[1:], near[0]) if near else green[l]
            g_ref[l, p, 0] = y[:, :n]
            g_ref[l, p, 1] = y[:, n:]
    for peer, out_slot in zip(peers(layers), out_slots):
        out_slot[...] = g_ref[peer]


def momentum_kernel(momentum, layers, *refs):
    core = lax.axis_index("mom")
    here = lax.axis_index("len")
    out_ref = refs[-1]
    per = refs[0].shape[0]
    masks = [0] + orders(layers)[momentum]

    def place(slots):
        for mask, slot in zip(masks, slots):
            for p in range(per):
                out_ref[(here ^ mask) * per + p] = slot[p]

    @pl.when(core == momentum)
    def _():
        place(refs[:layers])

    @pl.when(core != momentum)
    def _():
        place(refs[layers : 2 * layers])


def occupation(pos, total, n):
    return 1.0 / (1.0 + jnp.exp(8.0 * jnp.full((1, n), pos, jnp.int32).astype(F32) / total - 4.0))


def mix_kernel(total, items, first, last, shift_ref, weight_ref, *refs):
    count = len(items)
    inputs = count + (0 if first else 2)
    sums_in = refs[count:inputs]
    results = refs[inputs : inputs + 2]
    targets = refs[inputs + 2 : inputs + 4] if last else results
    local_e, _, n, _ = refs[0].shape
    phonons = shift_ref.shape[0]
    start = lax.axis_index("energy") * local_e
    core = lax.axis_index("mom")
    shifts = [shift_ref[m] for m in range(phonons)]
    weights = [weight_ref[m] for m in range(phonons)]

    def coefficient(t):
        value = 0.0
        for s, w in zip(shifts, weights):
            value = value + jnp.where(s == t, w, 0.0)
        return value

    def copy_out(i, a):
        return pltpu.make_async_copy(targets[i].at[a], results[i].at[a], refs[-1].at[i, a])

    def body(here):
        most = total // 2
        coefficients = {}
        terms = [[] for _ in range(local_e)]
        for i, (momentum, d) in enumerate(items):
            sign, factor = (-1, 1.0) if momentum == here else (1, 0.5)
            for b in range(local_e):
                occ = occupation(start + sign * d * local_e + b, total, n)
                for a in range(local_e):
                    t = d * local_e + sign * (b - a)
                    if 1 <= t <= most:
                        if t not in coefficients:
                            coefficients[t] = coefficient(t)
                        terms[a].append((refs[i], b, coefficients[t] * factor, occ))
        for i in range(2):
            for a in range(local_e):
                sums = [jnp.zeros((n, n), F32) if first else sums_in[i][a, c] for c in range(2)]
                for source, b, w, occ in terms[a]:
                    weight = w if i == 0 else w * occ
                    sums = [sums[c] + weight * source[b, c] for c in range(2)]
                if last and i == 1:
                    sums = [sums[0] - sums[0].T, sums[1] + sums[1].T]
                for c in range(2):
                    targets[i][a, c] = sums[c]
                if last:
                    copy_out(i, a).start()

    @pl.when(core == 0)
    def _():
        body(0)

    @pl.when(core != 0)
    def _():
        body(1)

    if last:
        for a in range(local_e):
            copy_out(0, a).wait()
            copy_out(1, a).wait()


def whole(count):
    return [pl.BlockSpec(memory_space=pltpu.VMEM)] * count


def params():
    return pltpu.CompilerParams(vmem_limit_bytes=VMEM_LIMIT)


def shards(hamiltonian, sigma_prev, coupling, coupling_pattern, phonon_shift, phonon_weight):
    local_e, _, n, _ = sigma_prev.shape[2:]
    layers = lax.axis_size("len")
    count = lax.axis_size("energy")
    moms = lax.axis_size("mom")
    total = local_e * count
    per = local_e // layers
    block = jax.ShapeDtypeStruct((local_e, 2, n, n), F32)
    first, second = orders(layers)

    def exchange(slots, i):
        if i == 0:
            return slots[0]
        pairs = []
        for l in range(layers):
            for k in range(moms):
                peer = l ^ (first, second)[k][i - 1]
                pairs.append((l * moms + k, peer * moms + k))
        return lax.ppermute(slots[i], ("len", "mom"), pairs)

    anywhere = pl.BlockSpec(memory_space=pltpu.HBM)
    inputs = (hamiltonian[0, 0], sigma_prev[0, 0], coupling[0], coupling_pattern)
    inputs = [pltpu.with_memory_space_constraint(value, pltpu.HBM) for value in inputs]

    def inverse(slots):
        return pl.pallas_call(
            functools.partial(inverse_kernel, total, layers, slots),
            out_shape=[jax.ShapeDtypeStruct((2 * per + 1, n, n), F32)] * len(slots),
            in_specs=[anywhere] * 4,
            out_specs=whole(len(slots)),
            scratch_shapes=[
                pltpu.VMEM((2, n, n), F32),
                pltpu.VMEM((len(slots), per, 2, n, n), F32),
                pltpu.VMEM((n, n), F32),
                pltpu.VMEM((n, n), jnp.int32),
                pltpu.SemaphoreType.DMA((3 + len(slots),)),
            ],
            compiler_params=params(),
            cost_estimate=pl.CostEstimate(
                flops=len(slots) * per * 96 * n**3, bytes_accessed=len(slots) * 8 * n * n, transcendentals=0
            ),
            name="inverse",
        )(*inputs)

    half = (layers + 1) // 2
    early = tuple(range(1, half + 1))
    late = tuple(range(half + 1, layers)) + (0,)
    sent = dict(zip(early, inverse(early))) | dict(zip(late, inverse(late)))
    part = jax.ShapeDtypeStruct((per, 2, n, n), F32)
    sent = pl.pallas_call(
        functools.partial(chain_kernel, layers),
        out_shape=[part] * layers,
        in_specs=whole(layers),
        out_specs=whole(layers),
        scratch_shapes=[pltpu.VMEM((layers, per, 2, n, n), F32), pltpu.VMEM((layers, n, n), F32)],
        compiler_params=params(),
        name="chains",
    )(*[exchange(sent, i) for i in range(layers)])
    own = [exchange(sent, i) for i in range(layers)]
    both_ways = [(k, moms - 1 - k) for k in range(moms)]
    other = [lax.ppermute(v, "mom", both_ways) for v in own]
    zero, one = (
        pl.pallas_call(
            functools.partial(momentum_kernel, momentum, layers),
            out_shape=block,
            in_specs=whole(2 * layers),
            out_specs=whole(1)[0],
            compiler_params=params(),
            name="momentum",
        )(*own, *other)
        for momentum in range(2)
    )

    reach = -(-(total // 2) // local_e)

    def hop(value, d, role):
        pairs = []
        for z in range(count - 1):
            low, high = z * moms, (z + 1) * moms
            if z >= d - 1:
                pairs.append((low + role, high + role))
            if z <= count - 1 - d:
                pairs.append((high + 1 - role, low + 1 - role))
        return lax.ppermute(value, ("energy", "mom"), pairs)

    smem = pl.BlockSpec(memory_space=pltpu.SMEM)

    def mix(items, blocks, sums, last=False):
        scratch = [pltpu.VMEM(block.shape, F32)] * 2 + [pltpu.SemaphoreType.DMA((2, local_e))]
        return pl.pallas_call(
            functools.partial(mix_kernel, total, items, not sums, last),
            out_shape=[block] * 2,
            in_specs=[smem, smem] + whole(len(blocks) + len(sums)),
            out_specs=[pl.BlockSpec(memory_space=pl.ANY)] * 2 if last else whole(2),
            scratch_shapes=scratch if last else [],
            compiler_params=params(),
            name="mix",
        )(phonon_shift, phonon_weight, *blocks, *sums)

    sums = mix([(0, 0), (1, 0)], [zero, one], [])
    one, _ = lax.optimization_barrier((one, sums))
    for d in range(1, reach + 1):
        zero = hop(zero, d, 0)
        one = hop(one, d, 1)
        if d < reach:
            sums = mix([(0, d), (1, d)], [zero, one], sums)
    sums = mix([(0, reach)], [zero], sums)
    sums = mix([(1, reach)], [one], sums, last=True)
    retarded, lesser = sums
    return (retarded[None, None], lesser[None, None])


def solution(mesh):
    in_specs = (
        P("mom", "len", None, None, None),
        P("mom", "len", "energy", None, None, None),
        P("len", None, None),
        P(),
        P(),
        P(),
    )
    out_specs = (
        P("mom", "len", "energy", None, None, None),
        P("mom", "len", "energy", None, None, None),
    )
    return jax.shard_map(shards, mesh=mesh, in_specs=in_specs, out_specs=out_specs, check_vma=False)
```

```python
import functools

import jax
import jax.numpy as jnp
from jax import lax
from jax.experimental import pallas as pl
from jax.experimental.pallas import tpu as pltpu
from jax.sharding import PartitionSpec as P

F32 = jnp.float32
BF16 = jnp.bfloat16
VMEM_LIMIT = 16 * 1024 * 1024


def split(x):
    high = x.astype(BF16)
    return high, (x - high.astype(F32)).astype(BF16)


def dot(a, b):
    return jnp.dot(a, b, preferred_element_type=F32)


def dot3(a, b):
    rows = a[0].shape[0]
    both = dot(jnp.concatenate([a[0], a[1]], axis=0), b[0])
    return both[:rows] + (both[rows:] + dot(a[0], b[1]))


def right_form(m):
    n = m.shape[0]
    re, im = m[:, :n], m[:, n:]
    return jnp.concatenate([m, jnp.concatenate([-im, re], axis=1)], axis=0)


def right_pair(m):
    high, low = split(m)
    return right_form(high), right_form(low)


def identity(n):
    rows = lax.broadcasted_iota(jnp.int32, (n, 2 * n), 0)
    cols = lax.broadcasted_iota(jnp.int32, (n, 2 * n), 1)
    return (rows == cols).astype(F32)


def orders(layers):
    first = [layers - 1] + list(range(1, layers - 1))
    second = list(first)
    if layers > 3:
        second[1], second[2] = second[2], second[1]
    return first, second


def peers(layers):
    here = lax.axis_index("len")
    core = lax.axis_index("mom")
    first, second = orders(layers)
    return [here] + [here ^ jnp.where(core == 0, a, b) for a, b in zip(first, second)]


def inverse_kernel(total, layers, slots, ham_any, sig_any, coupling_any, pattern_any, *refs):
    out_refs = refs[: len(slots)]
    ham_ref, sig_ref, coupling_ref, pattern_ref, sems = refs[len(slots) :]
    _, per, _, n, _ = sig_ref.shape
    towards = [peers(layers)[slot] for slot in slots]
    copies = [
        pltpu.make_async_copy(ham_any, ham_ref, sems.at[0]),
        pltpu.make_async_copy(coupling_any, coupling_ref, sems.at[1]),
        pltpu.make_async_copy(pattern_any, pattern_ref, sems.at[2]),
    ]
    for i, peer in enumerate(towards):
        group = sig_any.at[pl.ds(peer * per, per)]
        copies.append(pltpu.make_async_copy(group, sig_ref.at[i], sems.at[3 + i]))
    for copy in copies:
        copy.start()
    for copy in copies:
        copy.wait()
    start = lax.axis_index("energy") * (layers * per)
    eye = identity(n)
    bond = coupling_ref[...] * pattern_ref[...].astype(F32)
    for i, (peer, out_ref) in enumerate(zip(towards, out_refs)):
        out_ref[2 * per] = bond
        for p in range(per):
            pos = jnp.full((1, n), start + peer * per + p, jnp.int32).astype(F32)
            zre = 5.0 + 2.0 * pos / total
            mag = zre * zre + 1.0
            qre = zre / mag
            qim = -1.0 / mag
            sre = ham_ref[0] + sig_ref[i, p, 0]
            sim = ham_ref[1] + sig_ref[i, p, 1]
            a1 = jnp.concatenate([qre * sre - qim * sim, qre * sim + qim * sre], axis=1)
            a1_pair = split(a1)
            a1_right = (right_form(a1_pair[0]), right_form(a1_pair[1]))
            a2 = dot3(a1_pair, a1_right)
            a2_pair = split(a2)
            a2_right = (right_form(a2_pair[0]), right_form(a2_pair[1]))
            a3 = dot3(a1_pair, a2_right)
            a4 = dot3(a2_pair, a2_right)
            s = eye + (a1 + (a2 + a3))
            x = s + dot3(split(s), right_pair(a4))
            re, im = x[:, :n], x[:, n:]
            out_ref[2 * p] = qre * re - qim * im
            out_ref[2 * p + 1] = qre * im + qim * re


def chain_kernel(layers, *refs):
    in_slots, out_slots = refs[:layers], refs[layers : 2 * layers]
    g_ref, bond_ref = refs[2 * layers :]
    _, per, _, n, _ = g_ref.shape
    for peer, in_slot in zip(peers(layers), in_slots):
        for p in range(per):
            g_ref[peer, p] = in_slot[2 * p : 2 * p + 2]
        bond_ref[peer] = in_slot[2 * per]
    bonds = [None] + [bond_ref[l] for l in range(1, layers)]
    bonds_t = [None] + [b.T for b in bonds[1:]]
    for p in range(per):
        g = [jnp.concatenate([g_ref[l, p, 0], g_ref[l, p, 1]], axis=1) for l in range(layers)]
        down = [None] * layers
        up = [None] * layers
        for l in range(layers):
            high, low = split(g[l])
            tall = (
                jnp.concatenate([high[:, :n], high[:, n:]], axis=0),
                jnp.concatenate([low[:, :n], low[:, n:]], axis=0),
            )
            wide = (high, low)
            if l > 0:
                u = dot3(tall, split(bonds[l]))
                v = dot3(split(bonds_t[l]), wide)
                down[l] = (split(jnp.concatenate([u[:n], u[n:]], axis=1)), right_pair(v))
            if l + 1 < layers:
                u = dot3(tall, split(bonds_t[l + 1]))
                v = dot3(split(bonds[l + 1]), wide)
                up[l] = (split(jnp.concatenate([u[:n], u[n:]], axis=1)), right_pair(v))
        green = list(g)
        gleft = g[0]
        gright = g[layers - 1]
        for step in range(1, layers):
            l = step
            u, v = down[l]
            term = dot3(split(dot3(u, right_pair(gleft))), v)
            green[l] = green[l] + term
            gleft = g[l] + term
            l = layers - 1 - step
            u, v = up[l]
            term = dot3(split(dot3(u, right_pair(gright))), v)
            green[l] = green[l] + term
            gright = g[l] + term
        for l in range(layers):
            near = [green[m] for m in (l - 1, l + 1) if 0 <= m < layers]
            y = green[l] + 0.5 * sum(near[1:], near[0]) if near else green[l]
            g_ref[l, p, 0] = y[:, :n]
            g_ref[l, p, 1] = y[:, n:]
    for peer, out_slot in zip(peers(layers), out_slots):
        out_slot[...] = g_ref[peer]


def momentum_kernel(momentum, layers, *refs):
    core = lax.axis_index("mom")
    here = lax.axis_index("len")
    out_ref = refs[-1]
    per = refs[0].shape[0]
    masks = [0] + orders(layers)[momentum]

    def place(slots):
        for mask, slot in zip(masks, slots):
            for p in range(per):
                out_ref[(here ^ mask) * per + p] = slot[p]

    @pl.when(core == momentum)
    def _():
        place(refs[:layers])

    @pl.when(core != momentum)
    def _():
        place(refs[layers : 2 * layers])


def occupation(pos, total, n):
    return 1.0 / (1.0 + jnp.exp(8.0 * jnp.full((1, n), pos, jnp.int32).astype(F32) / total - 4.0))


def mix_kernel(total, items, first, last, shift_ref, weight_ref, *refs):
    count = len(items)
    inputs = count + (0 if first else 3 if last else 2)
    sums_in = refs[count:inputs]
    results = refs[inputs : inputs + 2]
    targets = refs[inputs + 2 : inputs + 4] if last else results
    local_e, _, n, _ = refs[0].shape
    phonons = shift_ref.shape[0]
    place = lax.axis_index("energy")
    start = place * local_e
    core = lax.axis_index("mom")
    shifts = [shift_ref[m] for m in range(phonons)]
    weights = [weight_ref[m] for m in range(phonons)]

    def coefficient(t):
        value = 0.0
        for s, w in zip(shifts, weights):
            value = value + jnp.where(s == t, w, 0.0)
        return value

    def copy_out(i, a):
        return pltpu.make_async_copy(targets[i].at[a], results[i].at[a], refs[-1].at[i, a])

    def body(here, some):
        most = total // 2
        coefficients = {}
        terms = [[] for _ in range(local_e)]
        for i, (momentum, d) in enumerate(items):
            sign, factor = (-1, 1.0) if momentum == here else (1, 0.5)
            for b in range(local_e):
                occ = occupation(start + sign * d * local_e + b, total, n)
                for a in range(local_e):
                    t = d * local_e + sign * (b - a)
                    if some and 1 <= t <= most:
                        if t not in coefficients:
                            coefficients[t] = coefficient(t)
                        terms[a].append((refs[i], b, coefficients[t] * factor, occ))
        for i in range(2):
            for a in range(local_e):
                if first:
                    sums = [jnp.zeros((n, n), F32)] * 2
                else:
                    sums = [sums_in[i][a, c] for c in range(2)]
                for source, b, w, occ in terms[a]:
                    weight = w if i == 0 else w * occ
                    sums = [sums[c] + weight * source[b, c] for c in range(2)]
                if (first or last) and i == 1:
                    sums = [sums[0] - sums[0].T, sums[1] + sums[1].T]
                    if last:
                        sums = [sums[c] + sums_in[2][a, c] for c in range(2)]
                for c in range(2):
                    targets[i][a, c] = sums[c]
                if last:
                    copy_out(i, a).start()

    for here in range(2):
        if len(items) > 1:
            pl.when(core == here)(functools.partial(body, here, True))
            continue
        [(momentum, d)] = items
        if momentum == here:
            some = place >= d
        else:
            some = place + d < lax.axis_size("energy")
        pl.when((core == here) & some)(functools.partial(body, here, True))
        if last:
            pl.when((core == here) & ~some)(functools.partial(body, here, False))

    if last:
        for a in range(local_e):
            copy_out(0, a).wait()
            copy_out(1, a).wait()


def whole(count):
    return [pl.BlockSpec(memory_space=pltpu.VMEM)] * count


def params():
    return pltpu.CompilerParams(vmem_limit_bytes=VMEM_LIMIT)


def shards(hamiltonian, sigma_prev, coupling, coupling_pattern, phonon_shift, phonon_weight):
    local_e, _, n, _ = sigma_prev.shape[2:]
    layers = lax.axis_size("len")
    count = lax.axis_size("energy")
    moms = lax.axis_size("mom")
    total = local_e * count
    per = local_e // layers
    block = jax.ShapeDtypeStruct((local_e, 2, n, n), F32)
    first, second = orders(layers)

    def exchange(slots, i):
        if i == 0:
            return slots[0]
        pairs = []
        for l in range(layers):
            for k in range(moms):
                peer = l ^ (first, second)[k][i - 1]
                pairs.append((l * moms + k, peer * moms + k))
        return lax.ppermute(slots[i], ("len", "mom"), pairs)

    anywhere = pl.BlockSpec(memory_space=pltpu.HBM)
    inputs = (hamiltonian[0, 0], sigma_prev[0, 0], coupling[0], coupling_pattern)
    inputs = [pltpu.with_memory_space_constraint(value, pltpu.HBM) for value in inputs]

    def inverse(slots):
        return pl.pallas_call(
            functools.partial(inverse_kernel, total, layers, slots),
            out_shape=[jax.ShapeDtypeStruct((2 * per + 1, n, n), F32)] * len(slots),
            in_specs=[anywhere] * 4,
            out_specs=whole(len(slots)),
            scratch_shapes=[
                pltpu.VMEM((2, n, n), F32),
                pltpu.VMEM((len(slots), per, 2, n, n), F32),
                pltpu.VMEM((n, n), F32),
                pltpu.VMEM((n, n), jnp.int32),
                pltpu.SemaphoreType.DMA((3 + len(slots),)),
            ],
            compiler_params=params(),
            cost_estimate=pl.CostEstimate(
                flops=len(slots) * per * 96 * n**3, bytes_accessed=len(slots) * 8 * n * n, transcendentals=0
            ),
            name="inverse",
        )(*inputs)

    half = (layers + 1) // 2
    early = tuple(range(1, half + 1))
    late = tuple(range(half + 1, layers)) + (0,)
    sent = dict(zip(early, inverse(early))) | dict(zip(late, inverse(late)))
    part = jax.ShapeDtypeStruct((per, 2, n, n), F32)
    sent = pl.pallas_call(
        functools.partial(chain_kernel, layers),
        out_shape=[part] * layers,
        in_specs=whole(layers),
        out_specs=whole(layers),
        scratch_shapes=[pltpu.VMEM((layers, per, 2, n, n), F32), pltpu.VMEM((layers, n, n), F32)],
        compiler_params=params(),
        name="chains",
    )(*[exchange(sent, i) for i in range(layers)])
    own = [exchange(sent, i) for i in range(layers)]
    both_ways = [(k, moms - 1 - k) for k in range(moms)]
    other = [lax.ppermute(v, "mom", both_ways) for v in own]
    zero, one = (
        pl.pallas_call(
            functools.partial(momentum_kernel, momentum, layers),
            out_shape=block,
            in_specs=whole(2 * layers),
            out_specs=whole(1)[0],
            compiler_params=params(),
            name="momentum",
        )(*own, *other)
        for momentum in range(2)
    )

    reach = -(-(total // 2) // local_e)

    def hop(value, d, role):
        pairs = []
        for z in range(count - 1):
            low, high = z * moms, (z + 1) * moms
            if z >= d - 1:
                pairs.append((low + role, high + role))
            if z <= count - 1 - d:
                pairs.append((high + 1 - role, low + 1 - role))
        return lax.ppermute(value, ("energy", "mom"), pairs)

    smem = pl.BlockSpec(memory_space=pltpu.SMEM)

    def mix(items, blocks, sums, first=False, last=False):
        scratch = [pltpu.VMEM(block.shape, F32)] * 2 + [pltpu.SemaphoreType.DMA((2, local_e))]
        count = 2 + len(blocks)
        in_place = len(items) == 1 and not last
        return pl.pallas_call(
            functools.partial(mix_kernel, total, items, first, last),
            out_shape=[block] * 2,
            in_specs=[smem, smem] + whole(len(blocks) + len(sums)),
            out_specs=[pl.BlockSpec(memory_space=pl.ANY)] * 2 if last else whole(2),
            scratch_shapes=scratch if last else [],
            input_output_aliases={count: 0, count + 1: 1} if in_place else {},
            compiler_params=params(),
            name="mix",
        )(phonon_shift, phonon_weight, *blocks, *sums)

    retarded, local_lesser = mix([(0, 0), (1, 0)], [zero, one], [], first=True)
    one, _ = lax.optimization_barrier((one, local_lesser))
    sums = [retarded, jnp.zeros_like(local_lesser)]
    for d in range(1, reach + 1):
        zero = hop(zero, d, 0)
        one = hop(one, d, 1)
        if d < reach:
            sums = mix([(0, d), (1, d)], [zero, one], sums)
    sums = mix([(0, reach)], [zero], sums)
    sums = mix([(1, reach)], [one], [*sums, local_lesser], last=True)
    retarded, lesser = sums
    return (retarded[None, None], lesser[None, None])


def solution(mesh):
    in_specs = (
        P("mom", "len", None, None, None),
        P("mom", "len", "energy", None, None, None),
        P("len", None, None),
        P(),
        P(),
        P(),
    )
    out_specs = (
        P("mom", "len", "energy", None, None, None),
        P("mom", "len", "energy", None, None, None),
    )
    return jax.shard_map(shards, mesh=mesh, in_specs=in_specs, out_specs=out_specs, check_vma=False)
```

```python
import functools

import jax
import jax.numpy as jnp
from jax import lax
from jax.experimental import pallas as pl
from jax.experimental.pallas import tpu as pltpu
from jax.sharding import PartitionSpec as P

F32 = jnp.float32
BF16 = jnp.bfloat16
VMEM_LIMIT = 16 * 1024 * 1024


def split(x):
    high = x.astype(BF16)
    return high, (x - high.astype(F32)).astype(BF16)


def dot(a, b):
    return jnp.dot(a, b, preferred_element_type=F32)


def dot3(a, b):
    rows = a[0].shape[0]
    both = dot(jnp.concatenate([a[0], a[1]], axis=0), b[0])
    return both[:rows] + (both[rows:] + dot(a[0], b[1]))


def right_form(m):
    n = m.shape[0]
    re, im = m[:, :n], m[:, n:]
    return jnp.concatenate([m, jnp.concatenate([-im, re], axis=1)], axis=0)


def right_pair(m):
    high, low = split(m)
    return right_form(high), right_form(low)


def identity(n):
    rows = lax.broadcasted_iota(jnp.int32, (n, 2 * n), 0)
    cols = lax.broadcasted_iota(jnp.int32, (n, 2 * n), 1)
    return (rows == cols).astype(F32)


def orders(layers):
    first = [layers - 1] + list(range(1, layers - 1))
    second = list(first)
    if layers > 3:
        second[1], second[2] = second[2], second[1]
    return first, second


def peers(layers):
    here = lax.axis_index("len")
    core = lax.axis_index("mom")
    first, second = orders(layers)
    return [here] + [here ^ jnp.where(core == 0, a, b) for a, b in zip(first, second)]


def inverse_kernel(total, layers, slots, ham_any, sig_any, coupling_any, pattern_any, *refs):
    out_refs = refs[: len(slots)]
    ham_ref, sig_ref, coupling_ref, pattern_ref, sems = refs[len(slots) :]
    _, per, _, n, _ = sig_ref.shape
    towards = [peers(layers)[slot] for slot in slots]
    copies = [
        pltpu.make_async_copy(ham_any, ham_ref, sems.at[0]),
        pltpu.make_async_copy(coupling_any, coupling_ref, sems.at[1]),
        pltpu.make_async_copy(pattern_any, pattern_ref, sems.at[2]),
    ]
    for i, peer in enumerate(towards):
        group = sig_any.at[pl.ds(peer * per, per)]
        copies.append(pltpu.make_async_copy(group, sig_ref.at[i], sems.at[3 + i]))
    for copy in copies:
        copy.start()
    for copy in copies:
        copy.wait()
    start = lax.axis_index("energy") * (layers * per)
    eye = identity(n)
    bond = coupling_ref[...] * pattern_ref[...].astype(F32)
    for i, (peer, out_ref) in enumerate(zip(towards, out_refs)):
        out_ref[2 * per] = bond
        for p in range(per):
            pos = jnp.full((1, n), start + peer * per + p, jnp.int32).astype(F32)
            zre = 5.0 + 2.0 * pos / total
            mag = zre * zre + 1.0
            qre = zre / mag
            qim = -1.0 / mag
            sre = ham_ref[0] + sig_ref[i, p, 0]
            sim = ham_ref[1] + sig_ref[i, p, 1]
            a1 = jnp.concatenate([qre * sre - qim * sim, qre * sim + qim * sre], axis=1)
            a1_pair = split(a1)
            a1_right = (right_form(a1_pair[0]), right_form(a1_pair[1]))
            a2 = dot3(a1_pair, a1_right)
            a2_pair = split(a2)
            a2_right = (right_form(a2_pair[0]), right_form(a2_pair[1]))
            a3 = dot3(a1_pair, a2_right)
            a4 = dot3(a2_pair, a2_right)
            s = eye + (a1 + (a2 + a3))
            x = s + dot3(split(s), right_pair(a4))
            re, im = x[:, :n], x[:, n:]
            out_ref[2 * p] = qre * re - qim * im
            out_ref[2 * p + 1] = qre * im + qim * re


def chain_kernel(layers, *refs):
    in_slots, out_slots = refs[:layers], refs[layers : 2 * layers]
    g_ref, bond_ref = refs[2 * layers :]
    _, per, _, n, _ = g_ref.shape
    for peer, in_slot in zip(peers(layers), in_slots):
        for p in range(per):
            g_ref[peer, p] = in_slot[2 * p : 2 * p + 2]
        bond_ref[peer] = in_slot[2 * per]
    bonds = [None] + [bond_ref[l] for l in range(1, layers)]
    bonds_t = [None] + [b.T for b in bonds[1:]]
    for p in range(per):
        g = [jnp.concatenate([g_ref[l, p, 0], g_ref[l, p, 1]], axis=1) for l in range(layers)]
        down = [None] * layers
        up = [None] * layers
        for l in range(layers):
            high, low = split(g[l])
            tall = (
                jnp.concatenate([high[:, :n], high[:, n:]], axis=0),
                jnp.concatenate([low[:, :n], low[:, n:]], axis=0),
            )
            wide = (high, low)
            if l > 0:
                u = dot3(tall, split(bonds[l]))
                v = dot3(split(bonds_t[l]), wide)
                down[l] = (split(jnp.concatenate([u[:n], u[n:]], axis=1)), right_pair(v))
            if l + 1 < layers:
                u = dot3(tall, split(bonds_t[l + 1]))
                v = dot3(split(bonds[l + 1]), wide)
                up[l] = (split(jnp.concatenate([u[:n], u[n:]], axis=1)), right_pair(v))
        green = list(g)
        gleft = g[0]
        gright = g[layers - 1]
        for step in range(1, layers):
            l = step
            u, v = down[l]
            term = dot3(split(dot3(u, right_pair(gleft))), v)
            green[l] = green[l] + term
            gleft = g[l] + term
            l = layers - 1 - step
            u, v = up[l]
            term = dot3(split(dot3(u, right_pair(gright))), v)
            green[l] = green[l] + term
            gright = g[l] + term
        for l in range(layers):
            near = [green[m] for m in (l - 1, l + 1) if 0 <= m < layers]
            y = green[l] + 0.5 * sum(near[1:], near[0]) if near else green[l]
            g_ref[l, p, 0] = y[:, :n]
            g_ref[l, p, 1] = y[:, n:]
    for peer, out_slot in zip(peers(layers), out_slots):
        out_slot[...] = g_ref[peer]


def momentum_kernel(momentum, layers, *refs):
    core = lax.axis_index("mom")
    here = lax.axis_index("len")
    out_ref = refs[-1]
    per = refs[0].shape[0]
    masks = [0] + orders(layers)[momentum]

    def place(slots):
        for mask, slot in zip(masks, slots):
            for p in range(per):
                out_ref[(here ^ mask) * per + p] = slot[p]

    @pl.when(core == momentum)
    def _():
        place(refs[:layers])

    @pl.when(core != momentum)
    def _():
        place(refs[layers : 2 * layers])


def occupation(pos, total, n):
    return 1.0 / (1.0 + jnp.exp(8.0 * jnp.full((1, n), pos, jnp.int32).astype(F32) / total - 4.0))


def local_kernel(total, shift_ref, weight_ref, zero_ref, one_ref, ret_ref, les_ref, table_ref):
    n = table_ref.shape[1]
    phonons = shift_ref.shape[0]
    for t in range(1, total // 2 + 1):
        value = 0.0
        for m in range(phonons):
            value = value + jnp.where(shift_ref[m] == t, weight_ref[m], 0.0)
        table_ref[t : t + 1] = jnp.full((1, n), value, F32)
    items = [(0, 0), (1, 0)]
    mix_kernel(total, items, True, False, table_ref, zero_ref, one_ref, ret_ref, les_ref)


def mix_kernel(total, items, first, last, table_ref, *refs):
    count = len(items)
    inputs = count + (0 if first else 3 if last else 2)
    sums_in = refs[count:inputs]
    results = refs[inputs : inputs + 2]
    targets = refs[inputs + 2 : inputs + 4] if last else results
    local_e, _, n, _ = refs[0].shape
    place = lax.axis_index("energy")
    places = lax.axis_size("energy")
    core = lax.axis_index("mom")

    def copy_out(i, a):
        return pltpu.make_async_copy(targets[i].at[a], results[i].at[a], refs[-1].at[i, a])

    def body(here, some):
        most = total // 2
        terms = [[] for _ in range(local_e)]
        for i, (momentum, d) in enumerate(items):
            sign, factor = (-1, 1.0) if momentum == here else (1, 0.5)
            source = place + sign * d
            factor = jnp.where((source >= 0) & (source < places), factor, 0.0)
            for b in range(local_e):
                occ = occupation(source * local_e + b, total, n)
                for a in range(local_e):
                    t = d * local_e + sign * (b - a)
                    if some and 1 <= t <= most:
                        weight = table_ref[t : t + 1] * factor
                        terms[a].append((refs[i], b, weight, weight * occ))
        for i in range(2):
            for a in range(local_e):
                if first:
                    sums = [jnp.zeros((n, n), F32)] * 2
                else:
                    sums = [sums_in[i][a, c] for c in range(2)]
                for source, b, *weights in terms[a]:
                    sums = [sums[c] + weights[i] * source[b, c] for c in range(2)]
                if (first or last) and i == 1:
                    sums = [sums[0] - sums[0].T, sums[1] + sums[1].T]
                    if last:
                        sums = [sums[c] + sums_in[2][a, c] for c in range(2)]
                for c in range(2):
                    targets[i][a, c] = sums[c]
                if last:
                    copy_out(i, a).start()

    for here in range(2):
        if len(items) > 1:
            pl.when(core == here)(functools.partial(body, here, True))
            continue
        [(momentum, d)] = items
        some = place >= d if momentum == here else place + d < places
        pl.when((core == here) & some)(functools.partial(body, here, True))
        if last:
            pl.when((core == here) & ~some)(functools.partial(body, here, False))

    if last:
        for a in range(local_e):
            copy_out(0, a).wait()
            copy_out(1, a).wait()


def whole(count):
    return [pl.BlockSpec(memory_space=pltpu.VMEM)] * count


def params():
    return pltpu.CompilerParams(vmem_limit_bytes=VMEM_LIMIT)


def shards(hamiltonian, sigma_prev, coupling, coupling_pattern, phonon_shift, phonon_weight):
    local_e, _, n, _ = sigma_prev.shape[2:]
    layers = lax.axis_size("len")
    count = lax.axis_size("energy")
    moms = lax.axis_size("mom")
    total = local_e * count
    per = local_e // layers
    block = jax.ShapeDtypeStruct((local_e, 2, n, n), F32)
    first, second = orders(layers)

    def exchange(slots, i):
        if i == 0:
            return slots[0]
        pairs = []
        for l in range(layers):
            for k in range(moms):
                peer = l ^ (first, second)[k][i - 1]
                pairs.append((l * moms + k, peer * moms + k))
        return lax.ppermute(slots[i], ("len", "mom"), pairs)

    anywhere = pl.BlockSpec(memory_space=pltpu.HBM)
    inputs = (hamiltonian[0, 0], sigma_prev[0, 0], coupling[0], coupling_pattern)
    inputs = [pltpu.with_memory_space_constraint(value, pltpu.HBM) for value in inputs]

    def inverse(slots):
        return pl.pallas_call(
            functools.partial(inverse_kernel, total, layers, slots),
            out_shape=[jax.ShapeDtypeStruct((2 * per + 1, n, n), F32)] * len(slots),
            in_specs=[anywhere] * 4,
            out_specs=whole(len(slots)),
            scratch_shapes=[
                pltpu.VMEM((2, n, n), F32),
                pltpu.VMEM((len(slots), per, 2, n, n), F32),
                pltpu.VMEM((n, n), F32),
                pltpu.VMEM((n, n), jnp.int32),
                pltpu.SemaphoreType.DMA((3 + len(slots),)),
            ],
            compiler_params=params(),
            cost_estimate=pl.CostEstimate(
                flops=len(slots) * per * 96 * n**3, bytes_accessed=len(slots) * 8 * n * n, transcendentals=0
            ),
            name="inverse",
        )(*inputs)

    half = (layers + 1) // 2
    early = tuple(range(1, half + 1))
    late = tuple(range(half + 1, layers)) + (0,)
    sent = dict(zip(early, inverse(early))) | dict(zip(late, inverse(late)))
    part = jax.ShapeDtypeStruct((per, 2, n, n), F32)
    sent = pl.pallas_call(
        functools.partial(chain_kernel, layers),
        out_shape=[part] * layers,
        in_specs=whole(layers),
        out_specs=whole(layers),
        scratch_shapes=[pltpu.VMEM((layers, per, 2, n, n), F32), pltpu.VMEM((layers, n, n), F32)],
        compiler_params=params(),
        name="chains",
    )(*[exchange(sent, i) for i in range(layers)])
    own = [exchange(sent, i) for i in range(layers)]
    both_ways = [(k, moms - 1 - k) for k in range(moms)]
    other = [lax.ppermute(v, "mom", both_ways) for v in own]
    zero, one = (
        pl.pallas_call(
            functools.partial(momentum_kernel, momentum, layers),
            out_shape=block,
            in_specs=whole(2 * layers),
            out_specs=whole(1)[0],
            compiler_params=params(),
            name="momentum",
        )(*own, *other)
        for momentum in range(2)
    )

    reach = -(-(total // 2) // local_e)

    ring = [z * moms for z in range(count)] + [z * moms + 1 for z in reversed(range(count))]
    ring = list(zip(ring, ring[1:] + ring[:1]))
    ways = ring, [(target, source) for source, target in ring]

    def hop(value, role):
        return lax.ppermute(value, ("energy", "mom"), ways[role])

    smem = pl.BlockSpec(memory_space=pltpu.SMEM)

    retarded, local_lesser, table = pl.pallas_call(
        functools.partial(local_kernel, total),
        out_shape=[block] * 2 + [jax.ShapeDtypeStruct((total // 2 + 8, n), F32)],
        in_specs=[smem, smem] + whole(2),
        out_specs=whole(3),
        compiler_params=params(),
        name="local",
    )(phonon_shift, phonon_weight, zero, one)

    def mix(items, blocks, sums, last=False):
        scratch = [pltpu.VMEM(block.shape, F32)] * 2 + [pltpu.SemaphoreType.DMA((2, local_e))]
        count = 1 + len(blocks)
        in_place = len(items) == 1 and not last
        return pl.pallas_call(
            functools.partial(mix_kernel, total, items, False, last),
            out_shape=[block] * 2,
            in_specs=whole(1 + len(blocks) + len(sums)),
            out_specs=[pl.BlockSpec(memory_space=pl.ANY)] * 2 if last else whole(2),
            scratch_shapes=scratch if last else [],
            input_output_aliases={count: 0, count + 1: 1} if in_place else {},
            compiler_params=params(),
            name="mix",
        )(table, *blocks, *sums)

    one, _ = lax.optimization_barrier((one, local_lesser))
    sums = [retarded, jnp.zeros_like(local_lesser)]
    for d in range(1, reach + 1):
        zero = hop(zero, 0)
        one = hop(one, 1)
        if d < reach:
            sums = mix([(0, d), (1, d)], [zero, one], sums)
    sums = mix([(0, reach)], [zero], sums)
    sums = mix([(1, reach)], [one], [*sums, local_lesser], last=True)
    retarded, lesser = sums
    return (retarded[None, None], lesser[None, None])


def solution(mesh):
    in_specs = (
        P("mom", "len", None, None, None),
        P("mom", "len", "energy", None, None, None),
        P("len", None, None),
        P(),
        P(),
        P(),
    )
    out_specs = (
        P("mom", "len", "energy", None, None, None),
        P("mom", "len", "energy", None, None, None),
    )
    return jax.shard_map(shards, mesh=mesh, in_specs=in_specs, out_specs=out_specs, check_vma=False)
```

```python
import functools

import jax
import jax.numpy as jnp
from jax import lax
from jax.experimental import pallas as pl
from jax.experimental.pallas import tpu as pltpu
from jax.sharding import PartitionSpec as P

F32 = jnp.float32
BF16 = jnp.bfloat16
VMEM_LIMIT = 16 * 1024 * 1024


def split(x):
    high = x.astype(BF16)
    return high, (x - high.astype(F32)).astype(BF16)


def dot(a, b):
    return jnp.dot(a, b, preferred_element_type=F32)


def dot3(a, b):
    rows = a[0].shape[0]
    both = dot(jnp.concatenate([a[0], a[1]], axis=0), b[0])
    return both[:rows] + (both[rows:] + dot(a[0], b[1]))


def right_form(m):
    n = m.shape[0]
    re, im = m[:, :n], m[:, n:]
    return jnp.concatenate([m, jnp.concatenate([-im, re], axis=1)], axis=0)


def right_pair(m):
    high, low = split(m)
    return right_form(high), right_form(low)


def identity(n):
    rows = lax.broadcasted_iota(jnp.int32, (n, 2 * n), 0)
    cols = lax.broadcasted_iota(jnp.int32, (n, 2 * n), 1)
    return (rows == cols).astype(F32)


def orders(layers):
    first = [layers - 1] + list(range(1, layers - 1))
    second = list(first)
    if layers > 3:
        second[1], second[2] = second[2], second[1]
    return first, second


def peers(layers):
    here = lax.axis_index("len")
    core = lax.axis_index("mom")
    first, second = orders(layers)
    return [here] + [here ^ jnp.where(core == 0, a, b) for a, b in zip(first, second)]


def inverse_kernel(total, layers, slots, ham_any, sig_any, coupling_any, pattern_any, *refs):
    out_refs = refs[: len(slots)]
    ham_ref, sig_ref, coupling_ref, pattern_ref, sems = refs[len(slots) :]
    _, per, _, n, _ = sig_ref.shape
    towards = [peers(layers)[slot] for slot in slots]
    copies = [
        pltpu.make_async_copy(ham_any, ham_ref, sems.at[0]),
        pltpu.make_async_copy(coupling_any, coupling_ref, sems.at[1]),
        pltpu.make_async_copy(pattern_any, pattern_ref, sems.at[2]),
    ]
    for i, peer in enumerate(towards):
        group = sig_any.at[pl.ds(peer * per, per)]
        copies.append(pltpu.make_async_copy(group, sig_ref.at[i], sems.at[3 + i]))
    for copy in copies:
        copy.start()
    for copy in copies:
        copy.wait()
    start = lax.axis_index("energy") * (layers * per)
    eye = identity(n)
    bond = coupling_ref[...] * pattern_ref[...].astype(F32)
    for i, (peer, out_ref) in enumerate(zip(towards, out_refs)):
        out_ref[2 * per] = bond
        for p in range(per):
            pos = jnp.full((1, n), start + peer * per + p, jnp.int32).astype(F32)
            zre = 5.0 + 2.0 * pos / total
            mag = zre * zre + 1.0
            qre = zre / mag
            qim = -1.0 / mag
            sre = ham_ref[0] + sig_ref[i, p, 0]
            sim = ham_ref[1] + sig_ref[i, p, 1]
            a1 = jnp.concatenate([qre * sre - qim * sim, qre * sim + qim * sre], axis=1)
            a1_pair = split(a1)
            a1_right = (right_form(a1_pair[0]), right_form(a1_pair[1]))
            a2 = dot3(a1_pair, a1_right)
            a2_pair = split(a2)
            a2_right = (right_form(a2_pair[0]), right_form(a2_pair[1]))
            a3 = dot3(a1_pair, a2_right)
            a4 = dot3(a2_pair, a2_right)
            s = eye + (a1 + (a2 + a3))
            x = s + dot3(split(s), right_pair(a4))
            re, im = x[:, :n], x[:, n:]
            out_ref[2 * p] = qre * re - qim * im
            out_ref[2 * p + 1] = qre * im + qim * re


def chain_kernel(layers, *refs):
    in_slots, out_slots = refs[:layers], refs[layers : 2 * layers]
    g_ref, bond_ref = refs[2 * layers :]
    _, per, _, n, _ = g_ref.shape
    for peer, in_slot in zip(peers(layers), in_slots):
        for p in range(per):
            g_ref[peer, p] = in_slot[2 * p : 2 * p + 2]
        bond_ref[peer] = in_slot[2 * per]
    bonds = [None] + [bond_ref[l] for l in range(1, layers)]
    bonds_t = [None] + [b.T for b in bonds[1:]]
    for p in range(per):
        g = [jnp.concatenate([g_ref[l, p, 0], g_ref[l, p, 1]], axis=1) for l in range(layers)]
        down = [None] * layers
        up = [None] * layers
        for l in range(layers):
            high, low = split(g[l])
            tall = (
                jnp.concatenate([high[:, :n], high[:, n:]], axis=0),
                jnp.concatenate([low[:, :n], low[:, n:]], axis=0),
            )
            wide = (high, low)
            if l > 0:
                u = dot3(tall, split(bonds[l]))
                v = dot3(split(bonds_t[l]), wide)
                down[l] = (split(jnp.concatenate([u[:n], u[n:]], axis=1)), right_pair(v))
            if l + 1 < layers:
                u = dot3(tall, split(bonds_t[l + 1]))
                v = dot3(split(bonds[l + 1]), wide)
                up[l] = (split(jnp.concatenate([u[:n], u[n:]], axis=1)), right_pair(v))
        green = list(g)
        gleft = g[0]
        gright = g[layers - 1]
        for step in range(1, layers):
            l = step
            u, v = down[l]
            term = dot3(split(dot3(u, right_pair(gleft))), v)
            green[l] = green[l] + term
            gleft = g[l] + term
            l = layers - 1 - step
            u, v = up[l]
            term = dot3(split(dot3(u, right_pair(gright))), v)
            green[l] = green[l] + term
            gright = g[l] + term
        for l in range(layers):
            near = [green[m] for m in (l - 1, l + 1) if 0 <= m < layers]
            y = green[l] + 0.5 * sum(near[1:], near[0]) if near else green[l]
            g_ref[l, p, 0] = y[:, :n]
            g_ref[l, p, 1] = y[:, n:]
    for peer, out_slot in zip(peers(layers), out_slots):
        out_slot[...] = g_ref[peer]


def momentum_kernel(momentum, slots, *refs):
    core = lax.axis_index("mom")
    out_ref = refs[-1]
    per = refs[0].shape[0]

    def place(blocks):
        for i, block in enumerate(blocks):
            out_ref[i * per : (i + 1) * per] = block[...]

    @pl.when(core == momentum)
    def _():
        place(refs[:slots])

    @pl.when(core != momentum)
    def _():
        place(refs[slots : 2 * slots])


def join_kernel(*refs):
    out_ref = refs[-1]
    start = 0
    for part in refs[:-1]:
        out_ref[start : start + part.shape[0]] = part[...]
        start += part.shape[0]


def by_energy_kernel(momentum, layers, order, *refs):
    here = lax.axis_index("len")
    parts, out_ref = refs[:-1], refs[-1]
    per = out_ref.shape[0] // layers
    masks = [0] + orders(layers)[momentum]
    slots = [(part, i) for part in parts for i in range(part.shape[0] // per)]
    for slot, (part, i) in zip(order, slots):
        for p in range(per):
            out_ref[(here ^ masks[slot]) * per + p] = part[i * per + p]


def occupation(pos, total, n):
    return 1.0 / (1.0 + jnp.exp(8.0 * jnp.full((1, n), pos, jnp.int32).astype(F32) / total - 4.0))


def local_kernel(total, shift_ref, weight_ref, zero_ref, one_ref, ret_ref, les_ref, table_ref):
    n = table_ref.shape[1]
    phonons = shift_ref.shape[0]
    for t in range(1, total // 2 + 1):
        value = 0.0
        for m in range(phonons):
            value = value + jnp.where(shift_ref[m] == t, weight_ref[m], 0.0)
        table_ref[t : t + 1] = jnp.full((1, n), value, F32)
    items = [(0, 0), (1, 0)]
    mix_kernel(total, items, True, False, table_ref, zero_ref, one_ref, ret_ref, les_ref)


def mix_kernel(total, items, first, last, table_ref, *refs):
    count = len(items)
    inputs = count + (0 if first else 3 if last else 2)
    sums_in = refs[count:inputs]
    results = refs[inputs : inputs + 2]
    targets = refs[inputs + 2 : inputs + 4] if last else results
    local_e, _, n, _ = refs[0].shape
    place = lax.axis_index("energy")
    places = lax.axis_size("energy")
    core = lax.axis_index("mom")

    def copy_out(i, a):
        return pltpu.make_async_copy(targets[i].at[a], results[i].at[a], refs[-1].at[i, a])

    def body(here, some):
        most = total // 2
        terms = [[] for _ in range(local_e)]
        for i, (momentum, d) in enumerate(items):
            sign, factor = (-1, 1.0) if momentum == here else (1, 0.5)
            source = place + sign * d
            factor = jnp.where((source >= 0) & (source < places), factor, 0.0)
            for b in range(local_e):
                occ = occupation(source * local_e + b, total, n)
                for a in range(local_e):
                    t = d * local_e + sign * (b - a)
                    if some and 1 <= t <= most:
                        weight = table_ref[t : t + 1] * factor
                        terms[a].append((refs[i], b, weight, weight * occ))
        for i in range(2):
            for a in range(local_e):
                if first:
                    sums = [jnp.zeros((n, n), F32)] * 2
                else:
                    sums = [sums_in[i][a, c] for c in range(2)]
                for source, b, *weights in terms[a]:
                    sums = [sums[c] + weights[i] * source[b, c] for c in range(2)]
                if (first or last) and i == 1:
                    sums = [sums[0] - sums[0].T, sums[1] + sums[1].T]
                    if last:
                        sums = [sums[c] + sums_in[2][a, c] for c in range(2)]
                for c in range(2):
                    targets[i][a, c] = sums[c]
                if last:
                    copy_out(i, a).start()

    for here in range(2):
        if len(items) > 1:
            pl.when(core == here)(functools.partial(body, here, True))
            continue
        [(momentum, d)] = items
        some = place >= d if momentum == here else place + d < places
        pl.when((core == here) & some)(functools.partial(body, here, True))
        if last:
            pl.when((core == here) & ~some)(functools.partial(body, here, False))

    if last:
        for a in range(local_e):
            copy_out(0, a).wait()
            copy_out(1, a).wait()


def whole(count):
    return [pl.BlockSpec(memory_space=pltpu.VMEM)] * count


def params():
    return pltpu.CompilerParams(vmem_limit_bytes=VMEM_LIMIT)


def shards(hamiltonian, sigma_prev, coupling, coupling_pattern, phonon_shift, phonon_weight):
    local_e, _, n, _ = sigma_prev.shape[2:]
    layers = lax.axis_size("len")
    count = lax.axis_size("energy")
    moms = lax.axis_size("mom")
    total = local_e * count
    per = local_e // layers
    block = jax.ShapeDtypeStruct((local_e, 2, n, n), F32)
    first, second = orders(layers)

    def exchange(slots, i):
        if i == 0:
            return slots[0]
        pairs = []
        for l in range(layers):
            for k in range(moms):
                peer = l ^ (first, second)[k][i - 1]
                pairs.append((l * moms + k, peer * moms + k))
        return lax.ppermute(slots[i], ("len", "mom"), pairs)

    anywhere = pl.BlockSpec(memory_space=pltpu.HBM)
    inputs = (hamiltonian[0, 0], sigma_prev[0, 0], coupling[0], coupling_pattern)
    inputs = [pltpu.with_memory_space_constraint(value, pltpu.HBM) for value in inputs]

    def inverse(slots):
        return pl.pallas_call(
            functools.partial(inverse_kernel, total, layers, slots),
            out_shape=[jax.ShapeDtypeStruct((2 * per + 1, n, n), F32)] * len(slots),
            in_specs=[anywhere] * 4,
            out_specs=whole(len(slots)),
            scratch_shapes=[
                pltpu.VMEM((2, n, n), F32),
                pltpu.VMEM((len(slots), per, 2, n, n), F32),
                pltpu.VMEM((n, n), F32),
                pltpu.VMEM((n, n), jnp.int32),
                pltpu.SemaphoreType.DMA((3 + len(slots),)),
            ],
            compiler_params=params(),
            cost_estimate=pl.CostEstimate(
                flops=len(slots) * per * 96 * n**3, bytes_accessed=len(slots) * 8 * n * n, transcendentals=0
            ),
            name="inverse",
        )(*inputs)

    half = (layers + 1) // 2
    early = tuple(range(1, half + 1))
    late = tuple(range(half + 1, layers)) + (0,)
    sent = dict(zip(early, inverse(early))) | dict(zip(late, inverse(late)))
    part = jax.ShapeDtypeStruct((per, 2, n, n), F32)
    sent = pl.pallas_call(
        functools.partial(chain_kernel, layers),
        out_shape=[part] * layers,
        in_specs=whole(layers),
        out_specs=whole(layers),
        scratch_shapes=[pltpu.VMEM((layers, per, 2, n, n), F32), pltpu.VMEM((layers, n, n), F32)],
        compiler_params=params(),
        name="chains",
    )(*[exchange(sent, i) for i in range(layers)])
    own = [exchange(sent, i) for i in range(layers)]
    both_ways = [(k, moms - 1 - k) for k in range(moms)]
    little = pl.CostEstimate(flops=0, bytes_accessed=8 * n, transcendentals=0)

    def call(kernel, shape, *operands, name):
        return pl.pallas_call(
            kernel,
            out_shape=jax.ShapeDtypeStruct((shape, 2, n, n), F32),
            in_specs=whole(len(operands)),
            out_specs=whole(1)[0],
            compiler_params=params(),
            cost_estimate=little,
            name=name,
        )(*operands)

    def of_momentum(momentum, own, other):
        kernel = functools.partial(momentum_kernel, momentum, len(own))
        return call(kernel, len(own) * per, *own, *other, name="momentum")

    def by_energy(momentum, parts):
        kernel = functools.partial(by_energy_kernel, momentum, layers, sum(chunks, []))
        return call(kernel, local_e, *parts, name="by_energy")

    def join(parts):
        return call(join_kernel, sum(p.shape[0] for p in parts), *parts, name="join")

    reach = -(-(total // 2) // local_e)

    ring = [z * moms for z in range(count)] + [z * moms + 1 for z in reversed(range(count))]
    ring = list(zip(ring, ring[1:] + ring[:1]))
    ways = ring, [(target, source) for source, target in ring]

    def hop(value, role):
        return lax.ppermute(value, ("energy", "mom"), ways[role])

    chunks = [[0], [layers - 1], list(range(1, layers - 1))]
    fields = [[], []]
    hops = [[], []]
    for c in chunks:
        held = [own[i] for i in c]
        if hops[0]:
            held, _ = lax.optimization_barrier((held, [steps[0] for steps in hops]))
        other = [lax.ppermute(v, "mom", both_ways) for v in held]
        for m in range(2):
            fields[m].append(of_momentum(m, held, other))
            hops[m].append(hop(fields[m][-1], m))
    zero, one = (by_energy(m, fields[m]) for m in range(2))
    smem = pl.BlockSpec(memory_space=pltpu.SMEM)
    retarded, local_lesser, table = pl.pallas_call(
        functools.partial(local_kernel, total),
        out_shape=[block] * 2 + [jax.ShapeDtypeStruct((total // 2 + 8, n), F32)],
        in_specs=[smem, smem] + whole(2),
        out_specs=whole(3),
        compiler_params=params(),
        name="local",
    )(phonon_shift, phonon_weight, zero, one)

    def mix(items, blocks, sums, last=False):
        scratch = [pltpu.VMEM(block.shape, F32)] * 2 + [pltpu.SemaphoreType.DMA((2, local_e))]
        count = 1 + len(blocks)
        in_place = len(items) == 1 and not last
        return pl.pallas_call(
            functools.partial(mix_kernel, total, items, False, last),
            out_shape=[block] * 2,
            in_specs=whole(1 + len(blocks) + len(sums)),
            out_specs=[pl.BlockSpec(memory_space=pl.ANY)] * 2 if last else whole(2),
            scratch_shapes=scratch if last else [],
            input_output_aliases={count: 0, count + 1: 1} if in_place else {},
            compiler_params=params(),
            name="mix",
        )(table, *blocks, *sums)

    sums = [retarded, jnp.zeros_like(local_lesser)]
    for d in range(1, reach + 1):
        fields = hops if d == 1 else [[hop(part, m) for part in fields[m]] for m in range(2)]
        zero, one = (by_energy(m, fields[m]) for m in range(2))
        if d == 1:
            fields = [[join(parts[:-1]), parts[-1]] for parts in fields]
        if d < reach:
            sums = mix([(0, d), (1, d)], [zero, one], sums)
    sums = mix([(0, reach)], [zero], sums)
    sums = mix([(1, reach)], [one], [*sums, local_lesser], last=True)
    retarded, lesser = sums
    return (retarded[None, None], lesser[None, None])


def solution(mesh):
    in_specs = (
        P("mom", "len", None, None, None),
        P("mom", "len", "energy", None, None, None),
        P("len", None, None),
        P(),
        P(),
        P(),
    )
    out_specs = (
        P("mom", "len", "energy", None, None, None),
        P("mom", "len", "energy", None, None, None),
    )
    return jax.shard_map(shards, mesh=mesh, in_specs=in_specs, out_specs=out_specs, check_vma=False)
```

```python
import functools

import jax
import jax.numpy as jnp
from jax import lax
from jax.experimental import pallas as pl
from jax.experimental.pallas import tpu as pltpu
from jax.sharding import PartitionSpec as P

F32 = jnp.float32
BF16 = jnp.bfloat16
VMEM_LIMIT = 16 * 1024 * 1024


def split(x):
    high = x.astype(BF16)
    return high, (x - high.astype(F32)).astype(BF16)


def dot(a, b):
    return jnp.dot(a, b, preferred_element_type=F32)


def dot3(a, b):
    rows = a[0].shape[0]
    both = dot(jnp.concatenate([a[0], a[1]], axis=0), b[0])
    return both[:rows] + (both[rows:] + dot(a[0], b[1]))


def right_form(m):
    n = m.shape[0]
    re, im = m[:, :n], m[:, n:]
    return jnp.concatenate([m, jnp.concatenate([-im, re], axis=1)], axis=0)


def right_pair(m):
    high, low = split(m)
    return right_form(high), right_form(low)


def identity(n):
    rows = lax.broadcasted_iota(jnp.int32, (n, 2 * n), 0)
    cols = lax.broadcasted_iota(jnp.int32, (n, 2 * n), 1)
    return (rows == cols).astype(F32)


def orders(layers):
    first = [layers - 1] + list(range(1, layers - 1))
    second = list(first)
    if layers > 3:
        second[1], second[2] = second[2], second[1]
    return first, second


def peers(layers):
    here = lax.axis_index("len")
    core = lax.axis_index("mom")
    first, second = orders(layers)
    return [here] + [here ^ jnp.where(core == 0, a, b) for a, b in zip(first, second)]


def inverse_kernel(total, layers, slots, ham_any, sig_any, coupling_any, pattern_any, *refs):
    out_refs = refs[: len(slots)]
    ham_ref, sig_ref, coupling_ref, pattern_ref, sems = refs[len(slots) :]
    _, per, _, n, _ = sig_ref.shape
    towards = [peers(layers)[slot] for slot in slots]
    copies = [
        pltpu.make_async_copy(ham_any, ham_ref, sems.at[0]),
        pltpu.make_async_copy(coupling_any, coupling_ref, sems.at[1]),
        pltpu.make_async_copy(pattern_any, pattern_ref, sems.at[2]),
    ]
    for i, peer in enumerate(towards):
        group = sig_any.at[pl.ds(peer * per, per)]
        copies.append(pltpu.make_async_copy(group, sig_ref.at[i], sems.at[3 + i]))
    for copy in copies:
        copy.start()
    for copy in copies:
        copy.wait()
    start = lax.axis_index("energy") * (layers * per)
    eye = identity(n)
    bond = coupling_ref[...] * pattern_ref[...].astype(F32)
    for i, (peer, out_ref) in enumerate(zip(towards, out_refs)):
        out_ref[2 * per] = bond
        for p in range(per):
            pos = jnp.full((1, n), start + peer * per + p, jnp.int32).astype(F32)
            zre = 5.0 + 2.0 * pos / total
            mag = zre * zre + 1.0
            qre = zre / mag
            qim = -1.0 / mag
            sre = ham_ref[0] + sig_ref[i, p, 0]
            sim = ham_ref[1] + sig_ref[i, p, 1]
            a1 = jnp.concatenate([qre * sre - qim * sim, qre * sim + qim * sre], axis=1)
            a1_pair = split(a1)
            a1_right = (right_form(a1_pair[0]), right_form(a1_pair[1]))
            a2 = dot3(a1_pair, a1_right)
            a2_pair = split(a2)
            a2_right = (right_form(a2_pair[0]), right_form(a2_pair[1]))
            a3 = dot3(a1_pair, a2_right)
            a4 = dot3(a2_pair, a2_right)
            s = eye + (a1 + (a2 + a3))
            x = s + dot3(split(s), right_pair(a4))
            re, im = x[:, :n], x[:, n:]
            out_ref[2 * p] = qre * re - qim * im
            out_ref[2 * p + 1] = qre * im + qim * re


def chain_kernel(layers, *refs):
    in_slots, out_slots = refs[:layers], refs[layers : 2 * layers]
    g_ref, bond_ref = refs[2 * layers :]
    _, per, _, n, _ = g_ref.shape
    for peer, in_slot in zip(peers(layers), in_slots):
        for p in range(per):
            g_ref[peer, p] = in_slot[2 * p : 2 * p + 2]
        bond_ref[peer] = in_slot[2 * per]
    bonds = [None] + [bond_ref[l] for l in range(1, layers)]
    bonds_t = [None] + [b.T for b in bonds[1:]]
    for p in range(per):
        g = [jnp.concatenate([g_ref[l, p, 0], g_ref[l, p, 1]], axis=1) for l in range(layers)]
        down = [None] * layers
        up = [None] * layers
        for l in range(layers):
            high, low = split(g[l])
            tall = (
                jnp.concatenate([high[:, :n], high[:, n:]], axis=0),
                jnp.concatenate([low[:, :n], low[:, n:]], axis=0),
            )
            wide = (high, low)
            if l > 0:
                u = dot3(tall, split(bonds[l]))
                v = dot3(split(bonds_t[l]), wide)
                down[l] = (split(jnp.concatenate([u[:n], u[n:]], axis=1)), right_pair(v))
            if l + 1 < layers:
                u = dot3(tall, split(bonds_t[l + 1]))
                v = dot3(split(bonds[l + 1]), wide)
                up[l] = (split(jnp.concatenate([u[:n], u[n:]], axis=1)), right_pair(v))
        green = list(g)
        gleft = g[0]
        gright = g[layers - 1]
        for step in range(1, layers):
            l = step
            u, v = down[l]
            term = dot3(split(dot3(u, right_pair(gleft))), v)
            green[l] = green[l] + term
            gleft = g[l] + term
            l = layers - 1 - step
            u, v = up[l]
            term = dot3(split(dot3(u, right_pair(gright))), v)
            green[l] = green[l] + term
            gright = g[l] + term
        for l in range(layers):
            near = [green[m] for m in (l - 1, l + 1) if 0 <= m < layers]
            y = green[l] + 0.5 * sum(near[1:], near[0]) if near else green[l]
            g_ref[l, p, 0] = y[:, :n]
            g_ref[l, p, 1] = y[:, n:]
    for peer, out_slot in zip(peers(layers), out_slots):
        out_slot[...] = g_ref[peer]


def momentum_kernel(momentum, slots, *refs):
    core = lax.axis_index("mom")
    out_ref = refs[-1]
    per = refs[0].shape[0]

    def place(blocks):
        for i, block in enumerate(blocks):
            out_ref[i * per : (i + 1) * per] = block[...]

    @pl.when(core == momentum)
    def _():
        place(refs[:slots])

    @pl.when(core != momentum)
    def _():
        place(refs[slots : 2 * slots])


def by_energy_kernel(momentum, layers, order, *refs):
    here = lax.axis_index("len")
    parts, out_ref = refs[:-1], refs[-1]
    per = out_ref.shape[0] // layers
    masks = [0] + orders(layers)[momentum]
    slots = [(part, i) for part in parts for i in range(part.shape[0] // per)]
    for slot, (part, i) in zip(order, slots):
        for p in range(per):
            out_ref[(here ^ masks[slot]) * per + p] = part[i * per + p]


def occupation(pos, total, n):
    return 1.0 / (1.0 + jnp.exp(8.0 * jnp.full((1, n), pos, jnp.int32).astype(F32) / total - 4.0))


def local_kernel(total, shift_ref, weight_ref, zero_ref, one_ref, ret_ref, les_ref, table_ref):
    n = table_ref.shape[1]
    phonons = shift_ref.shape[0]
    for t in range(1, total // 2 + 1):
        value = 0.0
        for m in range(phonons):
            value = value + jnp.where(shift_ref[m] == t, weight_ref[m], 0.0)
        table_ref[t : t + 1] = jnp.full((1, n), value, F32)
    items = [(0, 0), (1, 0)]
    mix_kernel(total, items, True, False, table_ref, zero_ref, one_ref, ret_ref, les_ref)


def mix_kernel(total, items, first, last, table_ref, *refs):
    count = len(items)
    inputs = count + (0 if first else 3 if last else 2)
    sums_in = refs[count:inputs]
    results = refs[inputs : inputs + 2]
    targets = refs[inputs + 2 : inputs + 4] if last else results
    local_e, _, n, _ = refs[0].shape
    place = lax.axis_index("energy")
    places = lax.axis_size("energy")
    core = lax.axis_index("mom")

    def copy_out(i, a):
        return pltpu.make_async_copy(targets[i].at[a], results[i].at[a], refs[-1].at[i, a])

    def body(here, some):
        most = total // 2
        terms = [[] for _ in range(local_e)]
        for i, (momentum, d) in enumerate(items):
            sign, factor = (-1, 1.0) if momentum == here else (1, 0.5)
            source = place + sign * d
            factor = jnp.where((source >= 0) & (source < places), factor, 0.0)
            for b in range(local_e):
                occ = occupation(source * local_e + b, total, n)
                for a in range(local_e):
                    t = d * local_e + sign * (b - a)
                    if some and 1 <= t <= most:
                        weight = table_ref[t : t + 1] * factor
                        terms[a].append((refs[i], b, weight, weight * occ))
        for i in range(2):
            for a in range(local_e):
                if first:
                    sums = [jnp.zeros((n, n), F32)] * 2
                else:
                    sums = [sums_in[i][a, c] for c in range(2)]
                for source, b, *weights in terms[a]:
                    sums = [sums[c] + weights[i] * source[b, c] for c in range(2)]
                if (first or last) and i == 1:
                    sums = [sums[0] - sums[0].T, sums[1] + sums[1].T]
                    if last:
                        sums = [sums[c] + sums_in[2][a, c] for c in range(2)]
                for c in range(2):
                    targets[i][a, c] = sums[c]
                if last:
                    copy_out(i, a).start()

    for here in range(2):
        if len(items) > 1:
            pl.when(core == here)(functools.partial(body, here, True))
            continue
        [(momentum, d)] = items
        some = place >= d if momentum == here else place + d < places
        pl.when((core == here) & some)(functools.partial(body, here, True))
        if last:
            pl.when((core == here) & ~some)(functools.partial(body, here, False))

    if last:
        for a in range(local_e):
            copy_out(0, a).wait()
            copy_out(1, a).wait()


def whole(count):
    return [pl.BlockSpec(memory_space=pltpu.VMEM)] * count


def params():
    return pltpu.CompilerParams(vmem_limit_bytes=VMEM_LIMIT)


def shards(hamiltonian, sigma_prev, coupling, coupling_pattern, phonon_shift, phonon_weight):
    local_e, _, n, _ = sigma_prev.shape[2:]
    layers = lax.axis_size("len")
    count = lax.axis_size("energy")
    moms = lax.axis_size("mom")
    total = local_e * count
    per = local_e // layers
    block = jax.ShapeDtypeStruct((local_e, 2, n, n), F32)
    first, second = orders(layers)

    def exchange(slots, i):
        if i == 0:
            return slots[0]
        pairs = []
        for l in range(layers):
            for k in range(moms):
                peer = l ^ (first, second)[k][i - 1]
                pairs.append((l * moms + k, peer * moms + k))
        return lax.ppermute(slots[i], ("len", "mom"), pairs)

    anywhere = pl.BlockSpec(memory_space=pltpu.HBM)
    inputs = (hamiltonian[0, 0], sigma_prev[0, 0], coupling[0], coupling_pattern)
    inputs = [pltpu.with_memory_space_constraint(value, pltpu.HBM) for value in inputs]

    def inverse(slots):
        return pl.pallas_call(
            functools.partial(inverse_kernel, total, layers, slots),
            out_shape=[jax.ShapeDtypeStruct((2 * per + 1, n, n), F32)] * len(slots),
            in_specs=[anywhere] * 4,
            out_specs=whole(len(slots)),
            scratch_shapes=[
                pltpu.VMEM((2, n, n), F32),
                pltpu.VMEM((len(slots), per, 2, n, n), F32),
                pltpu.VMEM((n, n), F32),
                pltpu.VMEM((n, n), jnp.int32),
                pltpu.SemaphoreType.DMA((3 + len(slots),)),
            ],
            compiler_params=params(),
            cost_estimate=pl.CostEstimate(
                flops=len(slots) * per * 96 * n**3, bytes_accessed=len(slots) * 8 * n * n, transcendentals=0
            ),
            name="inverse",
        )(*inputs)

    half = (layers + 1) // 2
    early = tuple(range(1, half + 1))
    late = tuple(range(half + 1, layers)) + (0,)
    sent = dict(zip(early, inverse(early))) | dict(zip(late, inverse(late)))
    part = jax.ShapeDtypeStruct((per, 2, n, n), F32)
    sent = pl.pallas_call(
        functools.partial(chain_kernel, layers),
        out_shape=[part] * layers,
        in_specs=whole(layers),
        out_specs=whole(layers),
        scratch_shapes=[pltpu.VMEM((layers, per, 2, n, n), F32), pltpu.VMEM((layers, n, n), F32)],
        compiler_params=params(),
        name="chains",
    )(*[exchange(sent, i) for i in range(layers)])
    own = [exchange(sent, i) for i in range(layers)]
    both_ways = [(k, moms - 1 - k) for k in range(moms)]
    little = pl.CostEstimate(flops=0, bytes_accessed=8 * n, transcendentals=0)

    def call(kernel, shape, *operands, name):
        return pl.pallas_call(
            kernel,
            out_shape=jax.ShapeDtypeStruct((shape, 2, n, n), F32),
            in_specs=whole(len(operands)),
            out_specs=whole(1)[0],
            compiler_params=params(),
            cost_estimate=little,
            name=name,
        )(*operands)

    def of_momentum(momentum, own, other):
        kernel = functools.partial(momentum_kernel, momentum, len(own))
        return call(kernel, len(own) * per, *own, *other, name="momentum")

    def by_energy(momentum, parts):
        kernel = functools.partial(by_energy_kernel, momentum, layers, sum(chunks, []))
        return call(kernel, local_e, *parts, name="by_energy")

    reach = -(-(total // 2) // local_e)

    ring = [z * moms for z in range(count)] + [z * moms + 1 for z in reversed(range(count))]
    ring = list(zip(ring, ring[1:] + ring[:1]))
    ways = ring, [(target, source) for source, target in ring]

    def hop(value, role):
        return lax.ppermute(value, ("energy", "mom"), ways[role])

    chunks = [[0], list(range(1, layers))]
    fields = [[], []]
    hops = [[], []]
    for c in chunks:
        held = [own[i] for i in c]
        if hops[0]:
            held, _ = lax.optimization_barrier((held, [steps[0] for steps in hops]))
        other = [lax.ppermute(v, "mom", both_ways) for v in held]
        for m in range(2):
            part = of_momentum(m, held, other)
            fields[m].append(part)
            if m == 1 and c == chunks[-1]:
                ahead = [hop(steps[0], k) for k, steps in enumerate(hops)]
                part, _ = lax.optimization_barrier((part, ahead))
            hops[m].append(hop(part, m))
    zero, one = (by_energy(m, fields[m]) for m in range(2))
    smem = pl.BlockSpec(memory_space=pltpu.SMEM)
    retarded, local_lesser, table = pl.pallas_call(
        functools.partial(local_kernel, total),
        out_shape=[block] * 2 + [jax.ShapeDtypeStruct((total // 2 + 8, n), F32)],
        in_specs=[smem, smem] + whole(2),
        out_specs=whole(3),
        compiler_params=params(),
        name="local",
    )(phonon_shift, phonon_weight, zero, one)

    def mix(items, blocks, sums, last=False):
        scratch = [pltpu.VMEM(block.shape, F32)] * 2 + [pltpu.SemaphoreType.DMA((2, local_e))]
        count = 1 + len(blocks)
        in_place = len(items) == 1 and not last
        return pl.pallas_call(
            functools.partial(mix_kernel, total, items, False, last),
            out_shape=[block] * 2,
            in_specs=whole(1 + len(blocks) + len(sums)),
            out_specs=[pl.BlockSpec(memory_space=pl.ANY)] * 2 if last else whole(2),
            scratch_shapes=scratch if last else [],
            input_output_aliases={count: 0, count + 1: 1} if in_place else {},
            compiler_params=params(),
            name="mix",
        )(table, *blocks, *sums)

    sums = [retarded, jnp.zeros_like(local_lesser)]
    for d in range(1, reach + 1):
        if d == 1:
            fields = hops
        elif d == 2:
            fields = [[ahead[m]] + [hop(part, m) for part in fields[m][1:]] for m in range(2)]
        else:
            fields = [[hop(part, m) for part in fields[m]] for m in range(2)]
        zero, one = (by_energy(m, fields[m]) for m in range(2))
        if d < reach:
            sums = mix([(0, d), (1, d)], [zero, one], sums)
    sums = mix([(0, reach)], [zero], sums)
    sums = mix([(1, reach)], [one], [*sums, local_lesser], last=True)
    retarded, lesser = sums
    return (retarded[None, None], lesser[None, None])


def solution(mesh):
    in_specs = (
        P("mom", "len", None, None, None),
        P("mom", "len", "energy", None, None, None),
        P("len", None, None),
        P(),
        P(),
        P(),
    )
    out_specs = (
        P("mom", "len", "energy", None, None, None),
        P("mom", "len", "energy", None, None, None),
    )
    return jax.shard_map(shards, mesh=mesh, in_specs=in_specs, out_specs=out_specs, check_vma=False)
```

```python
import functools

import jax
import jax.numpy as jnp
from jax import lax
from jax.experimental import pallas as pl
from jax.experimental.pallas import tpu as pltpu
from jax.sharding import PartitionSpec as P

F32 = jnp.float32
BF16 = jnp.bfloat16
VMEM_LIMIT = 16 * 1024 * 1024


def split(x):
    high = x.astype(BF16)
    return high, (x - high.astype(F32)).astype(BF16)


def dot(a, b):
    return jnp.dot(a, b, preferred_element_type=F32)


def dot3(a, b):
    rows = a[0].shape[0]
    both = dot(jnp.concatenate([a[0], a[1]], axis=0), b[0])
    return both[:rows] + (both[rows:] + dot(a[0], b[1]))


def right_form(m):
    n = m.shape[0]
    re, im = m[:, :n], m[:, n:]
    return jnp.concatenate([m, jnp.concatenate([-im, re], axis=1)], axis=0)


def right_pair(m):
    high, low = split(m)
    return right_form(high), right_form(low)


def identity(n):
    rows = lax.broadcasted_iota(jnp.int32, (n, 2 * n), 0)
    cols = lax.broadcasted_iota(jnp.int32, (n, 2 * n), 1)
    return (rows == cols).astype(F32)


def orders(layers):
    first = [layers - 1] + list(range(1, layers - 1))
    second = list(first)
    if layers > 3:
        second[1], second[2] = second[2], second[1]
    return first, second


def peers(layers):
    here = lax.axis_index("len")
    core = lax.axis_index("mom")
    first, second = orders(layers)
    return [here] + [here ^ jnp.where(core == 0, a, b) for a, b in zip(first, second)]


def inverse_kernel(total, layers, slots, ham_any, sig_any, coupling_any, pattern_any, *refs):
    out_refs = refs[: len(slots)]
    ham_ref, sig_ref, coupling_ref, pattern_ref, sems = refs[len(slots) :]
    _, per, _, n, _ = sig_ref.shape
    towards = [peers(layers)[slot] for slot in slots]
    copies = [
        pltpu.make_async_copy(ham_any, ham_ref, sems.at[0]),
        pltpu.make_async_copy(coupling_any, coupling_ref, sems.at[1]),
        pltpu.make_async_copy(pattern_any, pattern_ref, sems.at[2]),
    ]
    for i, peer in enumerate(towards):
        group = sig_any.at[pl.ds(peer * per, per)]
        copies.append(pltpu.make_async_copy(group, sig_ref.at[i], sems.at[3 + i]))
    for copy in copies:
        copy.start()
    for copy in copies:
        copy.wait()
    start = lax.axis_index("energy") * (layers * per)
    eye = identity(n)
    bond = coupling_ref[...] * pattern_ref[...].astype(F32)
    for i, (peer, out_ref) in enumerate(zip(towards, out_refs)):
        out_ref[2 * per] = bond
        for p in range(per):
            pos = jnp.full((1, n), start + peer * per + p, jnp.int32).astype(F32)
            zre = 5.0 + 2.0 * pos / total
            mag = zre * zre + 1.0
            qre = zre / mag
            qim = -1.0 / mag
            sre = ham_ref[0] + sig_ref[i, p, 0]
            sim = ham_ref[1] + sig_ref[i, p, 1]
            a1 = jnp.concatenate([qre * sre - qim * sim, qre * sim + qim * sre], axis=1)
            a1_pair = split(a1)
            a1_right = (right_form(a1_pair[0]), right_form(a1_pair[1]))
            a2 = dot3(a1_pair, a1_right)
            a2_pair = split(a2)
            a2_right = (right_form(a2_pair[0]), right_form(a2_pair[1]))
            a3 = dot3(a1_pair, a2_right)
            a4 = dot3(a2_pair, a2_right)
            s = eye + (a1 + (a2 + a3))
            x = s + dot3(split(s), right_pair(a4))
            re, im = x[:, :n], x[:, n:]
            out_ref[2 * p] = qre * re - qim * im
            out_ref[2 * p + 1] = qre * im + qim * re


def chain_kernel(layers, *refs):
    in_slots, out_slots = refs[:layers], refs[layers : 2 * layers]
    g_ref, bond_ref = refs[2 * layers :]
    _, per, _, n, _ = g_ref.shape
    for peer, in_slot in zip(peers(layers), in_slots):
        for p in range(per):
            g_ref[peer, p] = in_slot[2 * p : 2 * p + 2]
        bond_ref[peer] = in_slot[2 * per]
    bonds = [None] + [bond_ref[l] for l in range(1, layers)]
    bonds_t = [None] + [b.T for b in bonds[1:]]
    for p in range(per):
        g = [jnp.concatenate([g_ref[l, p, 0], g_ref[l, p, 1]], axis=1) for l in range(layers)]
        down = [None] * layers
        up = [None] * layers
        for l in range(layers):
            high, low = split(g[l])
            tall = (
                jnp.concatenate([high[:, :n], high[:, n:]], axis=0),
                jnp.concatenate([low[:, :n], low[:, n:]], axis=0),
            )
            wide = (high, low)
            if l > 0:
                u = dot3(tall, split(bonds[l]))
                v = dot3(split(bonds_t[l]), wide)
                down[l] = (split(jnp.concatenate([u[:n], u[n:]], axis=1)), right_pair(v))
            if l + 1 < layers:
                u = dot3(tall, split(bonds_t[l + 1]))
                v = dot3(split(bonds[l + 1]), wide)
                up[l] = (split(jnp.concatenate([u[:n], u[n:]], axis=1)), right_pair(v))
        green = list(g)
        gleft = g[0]
        gright = g[layers - 1]
        for step in range(1, layers):
            l = step
            u, v = down[l]
            term = dot3(split(dot3(u, right_pair(gleft))), v)
            green[l] = green[l] + term
            gleft = g[l] + term
            l = layers - 1 - step
            u, v = up[l]
            term = dot3(split(dot3(u, right_pair(gright))), v)
            green[l] = green[l] + term
            gright = g[l] + term
        for l in range(layers):
            near = [green[m] for m in (l - 1, l + 1) if 0 <= m < layers]
            y = green[l] + 0.5 * sum(near[1:], near[0]) if near else green[l]
            g_ref[l, p, 0] = y[:, :n]
            g_ref[l, p, 1] = y[:, n:]
    for peer, out_slot in zip(peers(layers), out_slots):
        out_slot[...] = g_ref[peer]


def momentum_kernel(momentum, slots, *refs):
    core = lax.axis_index("mom")
    out_ref = refs[-1]
    per = refs[0].shape[0]

    def place(blocks):
        for i, block in enumerate(blocks):
            out_ref[i * per : (i + 1) * per] = block[...]

    @pl.when(core == momentum)
    def _():
        place(refs[:slots])

    @pl.when(core != momentum)
    def _():
        place(refs[slots : 2 * slots])


def by_energy_kernel(momentum, layers, order, *refs):
    here = lax.axis_index("len")
    parts, out_ref = refs[:-1], refs[-1]
    per = out_ref.shape[0] // layers
    masks = [0] + orders(layers)[momentum]
    slots = [(part, i) for part in parts for i in range(part.shape[0] // per)]
    for slot, (part, i) in zip(order, slots):
        for p in range(per):
            out_ref[(here ^ masks[slot]) * per + p] = part[i * per + p]


def occupation(pos, total, n):
    return 1.0 / (1.0 + jnp.exp(8.0 * jnp.full((1, n), pos, jnp.int32).astype(F32) / total - 4.0))


def local_kernel(total, shift_ref, weight_ref, zero_ref, one_ref, ret_ref, les_ref, table_ref):
    n = table_ref.shape[1]
    phonons = shift_ref.shape[0]
    for t in range(1, total // 2 + 1):
        value = 0.0
        for m in range(phonons):
            value = value + jnp.where(shift_ref[m] == t, weight_ref[m], 0.0)
        table_ref[t : t + 1] = jnp.full((1, n), value, F32)
    items = [(0, 0), (1, 0)]
    mix_kernel(total, items, True, False, table_ref, zero_ref, one_ref, ret_ref, les_ref)


def mix_kernel(total, items, first, last, table_ref, *refs):
    count = len(items)
    inputs = count + (0 if first else 3 if last else 2)
    sums_in = refs[count:inputs]
    results = refs[inputs : inputs + 2]
    targets = refs[inputs + 2 : inputs + 4] if last else results
    local_e, _, n, _ = refs[0].shape
    place = lax.axis_index("energy")
    places = lax.axis_size("energy")
    core = lax.axis_index("mom")

    def copy_out(i, a):
        return pltpu.make_async_copy(targets[i].at[a], results[i].at[a], refs[-1].at[i, a])

    def body(here, some):
        most = total // 2
        terms = [[] for _ in range(local_e)]
        for i, (momentum, d) in enumerate(items):
            sign, factor = (-1, 1.0) if momentum == here else (1, 0.5)
            source = place + sign * d
            factor = jnp.where((source >= 0) & (source < places), factor, 0.0)
            for b in range(local_e):
                occ = occupation(source * local_e + b, total, n)
                for a in range(local_e):
                    t = d * local_e + sign * (b - a)
                    if some and 1 <= t <= most:
                        weight = table_ref[t : t + 1] * factor
                        terms[a].append((refs[i], b, weight, weight * occ))
        for i in range(2):
            for a in range(local_e):
                if first:
                    sums = [jnp.zeros((n, n), F32)] * 2
                else:
                    sums = [sums_in[i][a, c] for c in range(2)]
                for source, b, *weights in terms[a]:
                    sums = [sums[c] + weights[i] * source[b, c] for c in range(2)]
                if (first or last) and i == 1:
                    sums = [sums[0] - sums[0].T, sums[1] + sums[1].T]
                    if last:
                        sums = [sums[c] + sums_in[2][a, c] for c in range(2)]
                for c in range(2):
                    targets[i][a, c] = sums[c]
                if last:
                    copy_out(i, a).start()

    for here in range(2):
        if len(items) > 1:
            pl.when(core == here)(functools.partial(body, here, True))
            continue
        [(momentum, d)] = items
        some = place >= d if momentum == here else place + d < places
        pl.when((core == here) & some)(functools.partial(body, here, True))
        if last:
            pl.when((core == here) & ~some)(functools.partial(body, here, False))

    if last:
        for a in range(local_e):
            copy_out(0, a).wait()
            copy_out(1, a).wait()


def whole(count):
    return [pl.BlockSpec(memory_space=pltpu.VMEM)] * count


def params():
    return pltpu.CompilerParams(vmem_limit_bytes=VMEM_LIMIT)


def shards(hamiltonian, sigma_prev, coupling, coupling_pattern, phonon_shift, phonon_weight):
    local_e, _, n, _ = sigma_prev.shape[2:]
    layers = lax.axis_size("len")
    count = lax.axis_size("energy")
    moms = lax.axis_size("mom")
    total = local_e * count
    per = local_e // layers
    block = jax.ShapeDtypeStruct((local_e, 2, n, n), F32)
    first, second = orders(layers)

    def exchange(slots, i):
        if i == 0:
            return slots[0]
        pairs = []
        for l in range(layers):
            for k in range(moms):
                peer = l ^ (first, second)[k][i - 1]
                pairs.append((l * moms + k, peer * moms + k))
        return lax.ppermute(slots[i], ("len", "mom"), pairs)

    anywhere = pl.BlockSpec(memory_space=pltpu.HBM)
    inputs = (hamiltonian[0, 0], sigma_prev[0, 0], coupling[0], coupling_pattern)
    inputs = [pltpu.with_memory_space_constraint(value, pltpu.HBM) for value in inputs]

    def inverse(slots):
        return pl.pallas_call(
            functools.partial(inverse_kernel, total, layers, slots),
            out_shape=[jax.ShapeDtypeStruct((2 * per + 1, n, n), F32)] * len(slots),
            in_specs=[anywhere] * 4,
            out_specs=whole(len(slots)),
            scratch_shapes=[
                pltpu.VMEM((2, n, n), F32),
                pltpu.VMEM((len(slots), per, 2, n, n), F32),
                pltpu.VMEM((n, n), F32),
                pltpu.VMEM((n, n), jnp.int32),
                pltpu.SemaphoreType.DMA((3 + len(slots),)),
            ],
            compiler_params=params(),
            cost_estimate=pl.CostEstimate(
                flops=len(slots) * per * 96 * n**3, bytes_accessed=len(slots) * 8 * n * n, transcendentals=0
            ),
            name="inverse",
        )(*inputs)

    half = (layers + 1) // 2
    early = tuple(range(1, half + 1))
    late = tuple(range(half + 1, layers)) + (0,)
    sent = dict(zip(early, inverse(early))) | dict(zip(late, inverse(late)))
    part = jax.ShapeDtypeStruct((per, 2, n, n), F32)
    sent = pl.pallas_call(
        functools.partial(chain_kernel, layers),
        out_shape=[part] * layers,
        in_specs=whole(layers),
        out_specs=whole(layers),
        scratch_shapes=[pltpu.VMEM((layers, per, 2, n, n), F32), pltpu.VMEM((layers, n, n), F32)],
        compiler_params=params(),
        name="chains",
    )(*[exchange(sent, i) for i in range(layers)])
    own = [exchange(sent, i) for i in range(layers)]
    both_ways = [(k, moms - 1 - k) for k in range(moms)]
    little = pl.CostEstimate(flops=0, bytes_accessed=8 * n, transcendentals=0)

    def call(kernel, shape, *operands, name):
        return pl.pallas_call(
            kernel,
            out_shape=jax.ShapeDtypeStruct((shape, 2, n, n), F32),
            in_specs=whole(len(operands)),
            out_specs=whole(1)[0],
            compiler_params=params(),
            cost_estimate=little,
            name=name,
        )(*operands)

    def of_momentum(momentum, own, other):
        kernel = functools.partial(momentum_kernel, momentum, len(own))
        return call(kernel, len(own) * per, *own, *other, name="momentum")

    def by_energy(momentum, parts):
        kernel = functools.partial(by_energy_kernel, momentum, layers, sum(chunks, []))
        return call(kernel, local_e, *parts, name="by_energy")

    reach = -(-(total // 2) // local_e)

    ring = [z * moms for z in range(count)] + [z * moms + 1 for z in reversed(range(count))]
    ring = list(zip(ring, ring[1:] + ring[:1]))
    ways = ring, [(target, source) for source, target in ring]

    def hop(value, role):
        return lax.ppermute(value, ("energy", "mom"), ways[role])

    chunks = [[0], [layers - 1], list(range(1, layers - 1))]
    fields = [[], []]
    hops = [[], []]
    for c in chunks:
        if len(hops[0]) == 1:
            own, _ = lax.optimization_barrier((own, hops))
        held = [own[i] for i in c]
        other = [lax.ppermute(v, "mom", both_ways) for v in held]
        for m in range(2):
            fields[m].append(of_momentum(m, held, other))
            hops[m].append(hop(fields[m][-1], m))
    zero, one = (by_energy(m, fields[m]) for m in range(2))
    smem = pl.BlockSpec(memory_space=pltpu.SMEM)
    retarded, local_lesser, table = pl.pallas_call(
        functools.partial(local_kernel, total),
        out_shape=[block] * 2 + [jax.ShapeDtypeStruct((total // 2 + 8, n), F32)],
        in_specs=[smem, smem] + whole(2),
        out_specs=whole(3),
        compiler_params=params(),
        name="local",
    )(phonon_shift, phonon_weight, zero, one)

    def mix(items, blocks, sums, last=False):
        scratch = [pltpu.VMEM(block.shape, F32)] * 2 + [pltpu.SemaphoreType.DMA((2, local_e))]
        count = 1 + len(blocks)
        in_place = len(items) == 1 and not last
        return pl.pallas_call(
            functools.partial(mix_kernel, total, items, False, last),
            out_shape=[block] * 2,
            in_specs=whole(1 + len(blocks) + len(sums)),
            out_specs=[pl.BlockSpec(memory_space=pl.ANY)] * 2 if last else whole(2),
            scratch_shapes=scratch if last else [],
            input_output_aliases={count: 0, count + 1: 1} if in_place else {},
            compiler_params=params(),
            name="mix",
        )(table, *blocks, *sums)

    sums = [retarded, jnp.zeros_like(local_lesser)]
    for d in range(1, reach + 1):
        if d == 1:
            fields = hops
        elif d == 2:
            ahead = [hop(fields[m][0], m) for m in range(2)]
            held = [lax.optimization_barrier((fields[m][1], ahead[m]))[0] for m in range(2)]
            big, _ = lax.optimization_barrier((fields[0][2], fields[1][1]))
            fields = [[ahead[m], hop(held[m], m), hop([big, fields[1][2]][m], m)] for m in range(2)]
        else:
            fields = [[hop(part, m) for part in fields[m]] for m in range(2)]
        zero, one = (by_energy(m, fields[m]) for m in range(2))
        if d < reach:
            sums = mix([(0, d), (1, d)], [zero, one], sums)
    sums = mix([(0, reach)], [zero], sums)
    sums = mix([(1, reach)], [one], [*sums, local_lesser], last=True)
    retarded, lesser = sums
    return (retarded[None, None], lesser[None, None])


def solution(mesh):
    in_specs = (
        P("mom", "len", None, None, None),
        P("mom", "len", "energy", None, None, None),
        P("len", None, None),
        P(),
        P(),
        P(),
    )
    out_specs = (
        P("mom", "len", "energy", None, None, None),
        P("mom", "len", "energy", None, None, None),
    )
    return jax.shard_map(shards, mesh=mesh, in_specs=in_specs, out_specs=out_specs, check_vma=False)
```

```python
import functools
import itertools

import jax
import jax.numpy as jnp
from jax import lax
from jax.experimental import pallas as pl
from jax.experimental.pallas import tpu as pltpu
from jax.sharding import PartitionSpec as P

F32 = jnp.float32
BF16 = jnp.bfloat16
VMEM_LIMIT = 16 * 1024 * 1024


def split(x):
    high = x.astype(BF16)
    return high, (x - high.astype(F32)).astype(BF16)


def dot(a, b):
    return jnp.dot(a, b, preferred_element_type=F32)


def dot3(a, b):
    rows = a[0].shape[0]
    both = dot(jnp.concatenate([a[0], a[1]], axis=0), b[0])
    return both[:rows] + (both[rows:] + dot(a[0], b[1]))


def right_form(m):
    n = m.shape[0]
    re, im = m[:, :n], m[:, n:]
    return jnp.concatenate([m, jnp.concatenate([-im, re], axis=1)], axis=0)


def right_pair(m):
    high, low = split(m)
    return right_form(high), right_form(low)


def identity(n):
    rows = lax.broadcasted_iota(jnp.int32, (n, 2 * n), 0)
    cols = lax.broadcasted_iota(jnp.int32, (n, 2 * n), 1)
    return (rows == cols).astype(F32)


def orders(layers):
    first = [layers - 1] + list(range(1, layers - 1))
    second = list(first)
    if layers > 3:
        second[1], second[2] = second[2], second[1]
    return first, second


def peers(layers):
    here = lax.axis_index("len")
    core = lax.axis_index("mom")
    first, second = orders(layers)
    return [here] + [here ^ jnp.where(core == 0, a, b) for a, b in zip(first, second)]


def inverse_kernel(total, layers, slots, ham_any, sig_any, coupling_any, pattern_any, *refs):
    out_refs = refs[: len(slots)]
    ham_ref, sig_ref, coupling_ref, pattern_ref, sems = refs[len(slots) :]
    _, per, _, n, _ = sig_ref.shape
    towards = [peers(layers)[slot] for slot in slots]
    copies = [
        pltpu.make_async_copy(ham_any, ham_ref, sems.at[0]),
        pltpu.make_async_copy(coupling_any, coupling_ref, sems.at[1]),
        pltpu.make_async_copy(pattern_any, pattern_ref, sems.at[2]),
    ]
    for i, peer in enumerate(towards):
        group = sig_any.at[pl.ds(peer * per, per)]
        copies.append(pltpu.make_async_copy(group, sig_ref.at[i], sems.at[3 + i]))
    for copy in copies:
        copy.start()
    for copy in copies:
        copy.wait()
    start = lax.axis_index("energy") * (layers * per)
    eye = identity(n)
    bond = coupling_ref[...] * pattern_ref[...].astype(F32)
    for i, (peer, out_ref) in enumerate(zip(towards, out_refs)):
        out_ref[2 * per] = bond
        for p in range(per):
            pos = jnp.full((1, n), start + peer * per + p, jnp.int32).astype(F32)
            zre = 5.0 + 2.0 * pos / total
            mag = zre * zre + 1.0
            qre = zre / mag
            qim = -1.0 / mag
            sre = ham_ref[0] + sig_ref[i, p, 0]
            sim = ham_ref[1] + sig_ref[i, p, 1]
            a1 = jnp.concatenate([qre * sre - qim * sim, qre * sim + qim * sre], axis=1)
            a1_pair = split(a1)
            a1_right = (right_form(a1_pair[0]), right_form(a1_pair[1]))
            a2 = dot3(a1_pair, a1_right)
            a2_pair = split(a2)
            a2_right = (right_form(a2_pair[0]), right_form(a2_pair[1]))
            a3 = dot3(a1_pair, a2_right)
            a4 = dot3(a2_pair, a2_right)
            s = eye + (a1 + (a2 + a3))
            x = s + dot3(split(s), right_pair(a4))
            re, im = x[:, :n], x[:, n:]
            out_ref[2 * p] = qre * re - qim * im
            out_ref[2 * p + 1] = qre * im + qim * re


def chain_kernel(layers, *refs):
    in_slots, out_slots = refs[:layers], refs[layers : 2 * layers]
    g_ref, bond_ref = refs[2 * layers :]
    _, per, _, n, _ = g_ref.shape
    for peer, in_slot in zip(peers(layers), in_slots):
        for p in range(per):
            g_ref[peer, p] = in_slot[2 * p : 2 * p + 2]
        bond_ref[peer] = in_slot[2 * per]
    bonds = [None] + [bond_ref[l] for l in range(1, layers)]
    bonds_t = [None] + [b.T for b in bonds[1:]]
    for p in range(per):
        g = [jnp.concatenate([g_ref[l, p, 0], g_ref[l, p, 1]], axis=1) for l in range(layers)]
        down = [None] * layers
        up = [None] * layers
        for l in range(layers):
            high, low = split(g[l])
            tall = (
                jnp.concatenate([high[:, :n], high[:, n:]], axis=0),
                jnp.concatenate([low[:, :n], low[:, n:]], axis=0),
            )
            wide = (high, low)
            if l > 0:
                u = dot3(tall, split(bonds[l]))
                v = dot3(split(bonds_t[l]), wide)
                down[l] = (split(jnp.concatenate([u[:n], u[n:]], axis=1)), right_pair(v))
            if l + 1 < layers:
                u = dot3(tall, split(bonds_t[l + 1]))
                v = dot3(split(bonds[l + 1]), wide)
                up[l] = (split(jnp.concatenate([u[:n], u[n:]], axis=1)), right_pair(v))
        green = list(g)
        gleft = g[0]
        gright = g[layers - 1]
        for step in range(1, layers):
            l = step
            u, v = down[l]
            term = dot3(split(dot3(u, right_pair(gleft))), v)
            green[l] = green[l] + term
            gleft = g[l] + term
            l = layers - 1 - step
            u, v = up[l]
            term = dot3(split(dot3(u, right_pair(gright))), v)
            green[l] = green[l] + term
            gright = g[l] + term
        for l in range(layers):
            near = [green[m] for m in (l - 1, l + 1) if 0 <= m < layers]
            y = green[l] + 0.5 * sum(near[1:], near[0]) if near else green[l]
            g_ref[l, p, 0] = y[:, :n]
            g_ref[l, p, 1] = y[:, n:]
    for peer, out_slot in zip(peers(layers), out_slots):
        out_slot[...] = g_ref[peer]


def momentum_kernel(momentum, slots, *refs):
    core = lax.axis_index("mom")
    out_ref = refs[-1]
    per = refs[0].shape[0]

    def place(blocks):
        for i, block in enumerate(blocks):
            out_ref[i * per : (i + 1) * per] = block[...]

    @pl.when(core == momentum)
    def _():
        place(refs[:slots])

    @pl.when(core != momentum)
    def _():
        place(refs[slots : 2 * slots])


def by_energy_kernel(momentum, layers, order, *refs):
    here = lax.axis_index("len")
    parts, out_ref = refs[:-1], refs[-1]
    per = out_ref.shape[0] // layers
    masks = [0] + orders(layers)[momentum]
    slots = [(part, i) for part in parts for i in range(part.shape[0] // per)]
    for slot, (part, i) in zip(order, slots):
        for p in range(per):
            out_ref[(here ^ masks[slot]) * per + p] = part[i * per + p]


def occupation(pos, total, n):
    return 1.0 / (1.0 + jnp.exp(8.0 * jnp.full((1, n), pos, jnp.int32).astype(F32) / total - 4.0))


def local_kernel(total, shift_ref, weight_ref, zero_ref, one_ref, ret_ref, les_ref, table_ref):
    n = table_ref.shape[1]
    phonons = shift_ref.shape[0]
    for t in range(1, total // 2 + 1):
        value = 0.0
        for m in range(phonons):
            value = value + jnp.where(shift_ref[m] == t, weight_ref[m], 0.0)
        table_ref[t : t + 1] = jnp.full((1, n), value, F32)
    items = [(0, 0), (1, 0)]
    mix_kernel(total, items, True, False, table_ref, zero_ref, one_ref, ret_ref, les_ref)


def mix_kernel(total, items, first, last, table_ref, *refs):
    count = len(items)
    inputs = count + (0 if first else 3 if last else 2)
    sums_in = refs[count:inputs]
    results = refs[inputs : inputs + 2]
    targets = refs[inputs + 2 : inputs + 4] if last else results
    local_e, _, n, _ = refs[0].shape
    place = lax.axis_index("energy")
    places = lax.axis_size("energy")
    core = lax.axis_index("mom")

    def copy_out(i, a):
        return pltpu.make_async_copy(targets[i].at[a], results[i].at[a], refs[-1].at[i, a])

    def body(here, some):
        most = total // 2
        terms = [[] for _ in range(local_e)]
        for i, (momentum, d) in enumerate(items):
            sign, factor = (-1, 1.0) if momentum == here else (1, 0.5)
            source = place + sign * d
            factor = jnp.where((source >= 0) & (source < places), factor, 0.0)
            for b in range(local_e):
                occ = occupation(source * local_e + b, total, n)
                for a in range(local_e):
                    t = d * local_e + sign * (b - a)
                    if some[i] and 1 <= t <= most:
                        weight = table_ref[t : t + 1] * factor
                        terms[a].append((refs[i], b, weight, weight * occ))
        for i in range(2):
            for a in range(local_e):
                if first:
                    sums = [jnp.zeros((n, n), F32)] * 2
                else:
                    sums = [sums_in[i][a, c] for c in range(2)]
                for source, b, *weights in terms[a]:
                    sums = [sums[c] + weights[i] * source[b, c] for c in range(2)]
                if (first or last) and i == 1:
                    sums = [sums[0] - sums[0].T, sums[1] + sums[1].T]
                    if last:
                        sums = [sums[c] + sums_in[2][a, c] for c in range(2)]
                for c in range(2):
                    targets[i][a, c] = sums[c]
                if last:
                    copy_out(i, a).start()

    def present(here, momentum, d):
        return place >= d if momentum == here else place + d < places

    for here in range(2):
        if not last:
            pl.when(core == here)(functools.partial(body, here, [True] * count))
            continue
        for some in itertools.product([False, True], repeat=count):
            fits = core == here
            for (momentum, d), there in zip(items, some):
                fits = fits & (present(here, momentum, d) == there)
            pl.when(fits)(functools.partial(body, here, some))

    if last:
        for a in range(local_e):
            copy_out(0, a).wait()
            copy_out(1, a).wait()


def whole(count):
    return [pl.BlockSpec(memory_space=pltpu.VMEM)] * count


def params():
    return pltpu.CompilerParams(vmem_limit_bytes=VMEM_LIMIT)


def shards(hamiltonian, sigma_prev, coupling, coupling_pattern, phonon_shift, phonon_weight):
    local_e, _, n, _ = sigma_prev.shape[2:]
    layers = lax.axis_size("len")
    count = lax.axis_size("energy")
    moms = lax.axis_size("mom")
    total = local_e * count
    per = local_e // layers
    block = jax.ShapeDtypeStruct((local_e, 2, n, n), F32)
    first, second = orders(layers)

    def exchange(slots, i):
        if i == 0:
            return slots[0]
        pairs = []
        for l in range(layers):
            for k in range(moms):
                peer = l ^ (first, second)[k][i - 1]
                pairs.append((l * moms + k, peer * moms + k))
        return lax.ppermute(slots[i], ("len", "mom"), pairs)

    anywhere = pl.BlockSpec(memory_space=pltpu.HBM)
    inputs = (hamiltonian[0, 0], sigma_prev[0, 0], coupling[0], coupling_pattern)
    inputs = [pltpu.with_memory_space_constraint(value, pltpu.HBM) for value in inputs]

    def inverse(slots):
        return pl.pallas_call(
            functools.partial(inverse_kernel, total, layers, slots),
            out_shape=[jax.ShapeDtypeStruct((2 * per + 1, n, n), F32)] * len(slots),
            in_specs=[anywhere] * 4,
            out_specs=whole(len(slots)),
            scratch_shapes=[
                pltpu.VMEM((2, n, n), F32),
                pltpu.VMEM((len(slots), per, 2, n, n), F32),
                pltpu.VMEM((n, n), F32),
                pltpu.VMEM((n, n), jnp.int32),
                pltpu.SemaphoreType.DMA((3 + len(slots),)),
            ],
            compiler_params=params(),
            cost_estimate=pl.CostEstimate(
                flops=len(slots) * per * 96 * n**3, bytes_accessed=len(slots) * 8 * n * n, transcendentals=0
            ),
            name="inverse",
        )(*inputs)

    half = (layers + 1) // 2
    early = tuple(range(1, half + 1))
    late = tuple(range(half + 1, layers)) + (0,)
    sent = dict(zip(early, inverse(early))) | dict(zip(late, inverse(late)))
    part = jax.ShapeDtypeStruct((per, 2, n, n), F32)
    sent = pl.pallas_call(
        functools.partial(chain_kernel, layers),
        out_shape=[part] * layers,
        in_specs=whole(layers),
        out_specs=whole(layers),
        scratch_shapes=[pltpu.VMEM((layers, per, 2, n, n), F32), pltpu.VMEM((layers, n, n), F32)],
        compiler_params=params(),
        name="chains",
    )(*[exchange(sent, i) for i in range(layers)])
    own = [exchange(sent, i) for i in range(layers)]
    both_ways = [(k, moms - 1 - k) for k in range(moms)]
    little = pl.CostEstimate(flops=0, bytes_accessed=8 * n, transcendentals=0)

    def call(kernel, shape, *operands, name):
        return pl.pallas_call(
            kernel,
            out_shape=jax.ShapeDtypeStruct((shape, 2, n, n), F32),
            in_specs=whole(len(operands)),
            out_specs=whole(1)[0],
            compiler_params=params(),
            cost_estimate=little,
            name=name,
        )(*operands)

    def of_momentum(momentum, own, other):
        kernel = functools.partial(momentum_kernel, momentum, len(own))
        return call(kernel, len(own) * per, *own, *other, name="momentum")

    def by_energy(momentum, parts):
        kernel = functools.partial(by_energy_kernel, momentum, layers, sum(chunks, []))
        return call(kernel, local_e, *parts, name="by_energy")

    reach = -(-(total // 2) // local_e)

    ring = [z * moms for z in range(count)] + [z * moms + 1 for z in reversed(range(count))]
    ring = list(zip(ring, ring[1:] + ring[:1]))
    ways = ring, [(target, source) for source, target in ring]

    def hop(value, role):
        return lax.ppermute(value, ("energy", "mom"), ways[role])

    chunks = [[0], [layers - 1], list(range(1, layers - 1))]
    fields = [[], []]
    hops = [[], []]
    for c in chunks:
        if len(hops[0]) == 1:
            own, _ = lax.optimization_barrier((own, hops))
        held = [own[i] for i in c]
        other = [lax.ppermute(v, "mom", both_ways) for v in held]
        for m in range(2):
            fields[m].append(of_momentum(m, held, other))
            hops[m].append(hop(fields[m][-1], m))
    zero, one = (by_energy(m, fields[m]) for m in range(2))
    smem = pl.BlockSpec(memory_space=pltpu.SMEM)
    retarded, local_lesser, table = pl.pallas_call(
        functools.partial(local_kernel, total),
        out_shape=[block] * 2 + [jax.ShapeDtypeStruct((total // 2 + 8, n), F32)],
        in_specs=[smem, smem] + whole(2),
        out_specs=whole(3),
        compiler_params=params(),
        name="local",
    )(phonon_shift, phonon_weight, zero, one)

    def mix(items, blocks, sums, last=False):
        scratch = [pltpu.VMEM(block.shape, F32)] * 2 + [pltpu.SemaphoreType.DMA((2, local_e))]
        return pl.pallas_call(
            functools.partial(mix_kernel, total, items, False, last),
            out_shape=[block] * 2,
            in_specs=whole(1 + len(blocks) + len(sums)),
            out_specs=[pl.BlockSpec(memory_space=pl.ANY)] * 2 if last else whole(2),
            scratch_shapes=scratch if last else [],
            compiler_params=params(),
            name="mix",
        )(table, *blocks, *sums)

    sums = [retarded, jnp.zeros_like(local_lesser)]
    for d in range(1, reach + 1):
        if d == 1:
            fields = hops
        elif d == 2:
            ahead = [hop(fields[m][0], m) for m in range(2)]
            held = [lax.optimization_barrier((fields[m][1], ahead[m]))[0] for m in range(2)]
            big, _ = lax.optimization_barrier((fields[0][2], fields[1][1]))
            fields = [[ahead[m], hop(held[m], m), hop([big, fields[1][2]][m], m)] for m in range(2)]
        else:
            fields = [[hop(part, m) for part in fields[m]] for m in range(2)]
        zero, one = (by_energy(m, fields[m]) for m in range(2))
        if d < reach:
            sums = mix([(0, d), (1, d)], [zero, one], sums)
    sums = mix([(0, reach), (1, reach)], [zero, one], [*sums, local_lesser], last=True)
    retarded, lesser = sums
    return (retarded[None, None], lesser[None, None])


def solution(mesh):
    in_specs = (
        P("mom", "len", None, None, None),
        P("mom", "len", "energy", None, None, None),
        P("len", None, None),
        P(),
        P(),
        P(),
    )
    out_specs = (
        P("mom", "len", "energy", None, None, None),
        P("mom", "len", "energy", None, None, None),
    )
    return jax.shard_map(shards, mesh=mesh, in_specs=in_specs, out_specs=out_specs, check_vma=False)
```

```python
import functools
import itertools

import jax
import jax.numpy as jnp
from jax import lax
from jax.experimental import pallas as pl
from jax.experimental.pallas import tpu as pltpu
from jax.sharding import PartitionSpec as P

F32 = jnp.float32
BF16 = jnp.bfloat16
VMEM_LIMIT = 16 * 1024 * 1024


def split(x):
    high = x.astype(BF16)
    return high, (x - high.astype(F32)).astype(BF16)


def dot(a, b):
    return jnp.dot(a, b, preferred_element_type=F32)


def dot3(a, b):
    rows = a[0].shape[0]
    both = dot(jnp.concatenate([a[0], a[1]], axis=0), b[0])
    return both[:rows] + (both[rows:] + dot(a[0], b[1]))


def right_form(m):
    n = m.shape[0]
    re, im = m[:, :n], m[:, n:]
    return jnp.concatenate([m, jnp.concatenate([-im, re], axis=1)], axis=0)


def right_pair(m):
    high, low = split(m)
    return right_form(high), right_form(low)


def identity(n):
    rows = lax.broadcasted_iota(jnp.int32, (n, 2 * n), 0)
    cols = lax.broadcasted_iota(jnp.int32, (n, 2 * n), 1)
    return (rows == cols).astype(F32)


def orders(layers):
    first = [layers - 1] + list(range(1, layers - 1))
    second = list(first)
    if layers > 3:
        second[1], second[2] = second[2], second[1]
    return first, second


def peers(layers):
    here = lax.axis_index("len")
    core = lax.axis_index("mom")
    first, second = orders(layers)
    return [here] + [here ^ jnp.where(core == 0, a, b) for a, b in zip(first, second)]


def inverse_kernel(total, layers, slots, ham_any, sig_any, coupling_any, pattern_any, *refs):
    out_refs = refs[: len(slots)]
    ham_ref, sig_ref, coupling_ref, pattern_ref, sems = refs[len(slots) :]
    _, per, _, n, _ = sig_ref.shape
    towards = [peers(layers)[slot] for slot in slots]
    copies = [
        pltpu.make_async_copy(ham_any, ham_ref, sems.at[0]),
        pltpu.make_async_copy(coupling_any, coupling_ref, sems.at[1]),
        pltpu.make_async_copy(pattern_any, pattern_ref, sems.at[2]),
    ]
    for i, peer in enumerate(towards):
        group = sig_any.at[pl.ds(peer * per, per)]
        copies.append(pltpu.make_async_copy(group, sig_ref.at[i], sems.at[3 + i]))
    for copy in copies:
        copy.start()
    for copy in copies:
        copy.wait()
    start = lax.axis_index("energy") * (layers * per)
    eye = identity(n)
    bond = coupling_ref[...] * pattern_ref[...].astype(F32)
    for i, (peer, out_ref) in enumerate(zip(towards, out_refs)):
        out_ref[2 * per] = bond
        for p in range(per):
            pos = jnp.full((1, n), start + peer * per + p, jnp.int32).astype(F32)
            zre = 5.0 + 2.0 * pos / total
            mag = zre * zre + 1.0
            qre = zre / mag
            qim = -1.0 / mag
            sre = ham_ref[0] + sig_ref[i, p, 0]
            sim = ham_ref[1] + sig_ref[i, p, 1]
            a1 = jnp.concatenate([qre * sre - qim * sim, qre * sim + qim * sre], axis=1)
            a1_pair = split(a1)
            a1_right = (right_form(a1_pair[0]), right_form(a1_pair[1]))
            a2 = dot3(a1_pair, a1_right)
            a2_pair = split(a2)
            a2_right = (right_form(a2_pair[0]), right_form(a2_pair[1]))
            a3 = dot3(a1_pair, a2_right)
            a4 = dot3(a2_pair, a2_right)
            s = eye + (a1 + (a2 + a3))
            x = s + dot3(split(s), right_pair(a4))
            re, im = x[:, :n], x[:, n:]
            out_ref[2 * p] = qre * re - qim * im
            out_ref[2 * p + 1] = qre * im + qim * re


def chain_kernel(layers, *refs):
    in_slots, out_slots = refs[:layers], refs[layers : 2 * layers]
    g_ref, bond_ref = refs[2 * layers :]
    _, per, _, n, _ = g_ref.shape
    for peer, in_slot in zip(peers(layers), in_slots):
        for p in range(per):
            g_ref[peer, p] = in_slot[2 * p : 2 * p + 2]
        bond_ref[peer] = in_slot[2 * per]
    bonds = [None] + [bond_ref[l] for l in range(1, layers)]
    bonds_t = [None] + [b.T for b in bonds[1:]]
    for p in range(per):
        g = [jnp.concatenate([g_ref[l, p, 0], g_ref[l, p, 1]], axis=1) for l in range(layers)]
        down = [None] * layers
        up = [None] * layers
        for l in range(layers):
            high, low = split(g[l])
            tall = (
                jnp.concatenate([high[:, :n], high[:, n:]], axis=0),
                jnp.concatenate([low[:, :n], low[:, n:]], axis=0),
            )
            wide = (high, low)
            if l > 0:
                u = dot3(tall, split(bonds[l]))
                v = dot3(split(bonds_t[l]), wide)
                down[l] = (split(jnp.concatenate([u[:n], u[n:]], axis=1)), right_pair(v))
            if l + 1 < layers:
                u = dot3(tall, split(bonds_t[l + 1]))
                v = dot3(split(bonds[l + 1]), wide)
                up[l] = (split(jnp.concatenate([u[:n], u[n:]], axis=1)), right_pair(v))
        green = list(g)
        gleft = g[0]
        gright = g[layers - 1]
        for step in range(1, layers):
            l = step
            u, v = down[l]
            term = dot3(split(dot3(u, right_pair(gleft))), v)
            green[l] = green[l] + term
            gleft = g[l] + term
            l = layers - 1 - step
            u, v = up[l]
            term = dot3(split(dot3(u, right_pair(gright))), v)
            green[l] = green[l] + term
            gright = g[l] + term
        for l in range(layers):
            near = [green[m] for m in (l - 1, l + 1) if 0 <= m < layers]
            y = green[l] + 0.5 * sum(near[1:], near[0]) if near else green[l]
            g_ref[l, p, 0] = y[:, :n]
            g_ref[l, p, 1] = y[:, n:]
    for peer, out_slot in zip(peers(layers), out_slots):
        out_slot[...] = g_ref[peer]


def momentum_kernel(momentum, slots, *refs):
    core = lax.axis_index("mom")
    out_ref = refs[-1]
    per = refs[0].shape[0]

    def place(blocks):
        for i, block in enumerate(blocks):
            out_ref[i * per : (i + 1) * per] = block[...]

    @pl.when(core == momentum)
    def _():
        place(refs[:slots])

    @pl.when(core != momentum)
    def _():
        place(refs[slots : 2 * slots])


def by_energy_kernel(momentum, layers, order, *refs):
    here = lax.axis_index("len")
    parts, out_ref = refs[:-1], refs[-1]
    per = out_ref.shape[0] // layers
    masks = [0] + orders(layers)[momentum]
    slots = [(part, i) for part in parts for i in range(part.shape[0] // per)]
    for slot, (part, i) in zip(order, slots):
        for p in range(per):
            out_ref[(here ^ masks[slot]) * per + p] = part[i * per + p]


def occupation(pos, total, n):
    return 1.0 / (1.0 + jnp.exp(8.0 * jnp.full((1, n), pos, jnp.int32).astype(F32) / total - 4.0))


def local_kernel(total, shift_ref, weight_ref, zero_ref, one_ref, ret_ref, les_ref, table_ref):
    n = table_ref.shape[1]
    phonons = shift_ref.shape[0]
    for t in range(1, total // 2 + 1):
        value = 0.0
        for m in range(phonons):
            value = value + jnp.where(shift_ref[m] == t, weight_ref[m], 0.0)
        table_ref[t : t + 1] = jnp.full((1, n), value, F32)
    items = [(0, 0), (1, 0)]
    mix_kernel(total, items, True, False, table_ref, zero_ref, one_ref, ret_ref, les_ref)


def mix_kernel(total, items, first, last, table_ref, *refs):
    count = len(items)
    inputs = count + (0 if first else 3 if last else 2)
    sums_in = refs[count:inputs]
    results = refs[inputs : inputs + 2]
    targets = refs[inputs + 2 : inputs + 4] if last else results
    local_e, _, n, _ = refs[0].shape
    place = lax.axis_index("energy")
    places = lax.axis_size("energy")
    core = lax.axis_index("mom")

    def copy_out(i, a):
        return pltpu.make_async_copy(targets[i].at[a], results[i].at[a], refs[-1].at[i, a])

    def body(here, some):
        most = total // 2
        terms = [[] for _ in range(local_e)]
        for i, (momentum, d) in enumerate(items):
            sign, factor = (-1, 1.0) if momentum == here else (1, 0.5)
            source = place + sign * d
            factor = jnp.where((source >= 0) & (source < places), factor, 0.0)
            for b in range(local_e):
                occ = occupation(source * local_e + b, total, n)
                for a in range(local_e):
                    t = d * local_e + sign * (b - a)
                    if some[i] and 1 <= t <= most:
                        weight = table_ref[t : t + 1] * factor
                        terms[a].append((refs[i], b, weight, weight * occ))
        for i in range(2):
            for a in range(local_e):
                if first:
                    sums = [jnp.zeros((n, n), F32)] * 2
                else:
                    sums = [sums_in[i][a, c] for c in range(2)]
                for source, b, *weights in terms[a]:
                    sums = [sums[c] + weights[i] * source[b, c] for c in range(2)]
                if (first or last) and i == 1:
                    sums = [sums[0] - sums[0].T, sums[1] + sums[1].T]
                    if last:
                        sums = [sums[c] + sums_in[2][a, c] for c in range(2)]
                for c in range(2):
                    targets[i][a, c] = sums[c]
                if last:
                    copy_out(i, a).start()

    def present(here, momentum, d):
        return place >= d if momentum == here else place + d < places

    for here in range(2):
        if not last:
            pl.when(core == here)(functools.partial(body, here, [True] * count))
            continue
        for some in itertools.product([False, True], repeat=count):
            fits = core == here
            for (momentum, d), there in zip(items, some):
                fits = fits & (present(here, momentum, d) == there)
            pl.when(fits)(functools.partial(body, here, some))

    if last:
        for a in range(local_e):
            copy_out(0, a).wait()
            copy_out(1, a).wait()


def whole(count):
    return [pl.BlockSpec(memory_space=pltpu.VMEM)] * count


def params():
    return pltpu.CompilerParams(vmem_limit_bytes=VMEM_LIMIT)


def shards(hamiltonian, sigma_prev, coupling, coupling_pattern, phonon_shift, phonon_weight):
    local_e, _, n, _ = sigma_prev.shape[2:]
    layers = lax.axis_size("len")
    count = lax.axis_size("energy")
    moms = lax.axis_size("mom")
    total = local_e * count
    per = local_e // layers
    block = jax.ShapeDtypeStruct((local_e, 2, n, n), F32)
    first, second = orders(layers)

    def exchange(slots, i):
        if i == 0:
            return slots[0]
        pairs = []
        for l in range(layers):
            for k in range(moms):
                peer = l ^ (first, second)[k][i - 1]
                pairs.append((l * moms + k, peer * moms + k))
        return lax.ppermute(slots[i], ("len", "mom"), pairs)

    anywhere = pl.BlockSpec(memory_space=pltpu.HBM)
    inputs = (hamiltonian[0, 0], sigma_prev[0, 0], coupling[0], coupling_pattern)
    inputs = [pltpu.with_memory_space_constraint(value, pltpu.HBM) for value in inputs]

    def inverse(slots):
        return pl.pallas_call(
            functools.partial(inverse_kernel, total, layers, slots),
            out_shape=[jax.ShapeDtypeStruct((2 * per + 1, n, n), F32)] * len(slots),
            in_specs=[anywhere] * 4,
            out_specs=whole(len(slots)),
            scratch_shapes=[
                pltpu.VMEM((2, n, n), F32),
                pltpu.VMEM((len(slots), per, 2, n, n), F32),
                pltpu.VMEM((n, n), F32),
                pltpu.VMEM((n, n), jnp.int32),
                pltpu.SemaphoreType.DMA((3 + len(slots),)),
            ],
            compiler_params=params(),
            cost_estimate=pl.CostEstimate(
                flops=len(slots) * per * 96 * n**3, bytes_accessed=len(slots) * 8 * n * n, transcendentals=0
            ),
            name="inverse",
        )(*inputs)

    half = (layers + 1) // 2
    early = tuple(range(1, half + 1))
    late = tuple(range(half + 1, layers)) + (0,)
    sent = dict(zip(early, inverse(early))) | dict(zip(late, inverse(late)))
    part = jax.ShapeDtypeStruct((per, 2, n, n), F32)
    sent = pl.pallas_call(
        functools.partial(chain_kernel, layers),
        out_shape=[part] * layers,
        in_specs=whole(layers),
        out_specs=whole(layers),
        scratch_shapes=[pltpu.VMEM((layers, per, 2, n, n), F32), pltpu.VMEM((layers, n, n), F32)],
        compiler_params=params(),
        name="chains",
    )(*[exchange(sent, i) for i in range(layers)])
    own = [exchange(sent, i) for i in range(layers)]
    both_ways = [(k, moms - 1 - k) for k in range(moms)]
    little = pl.CostEstimate(flops=0, bytes_accessed=8 * n, transcendentals=0)

    def call(kernel, shape, *operands, name):
        return pl.pallas_call(
            kernel,
            out_shape=jax.ShapeDtypeStruct((shape, 2, n, n), F32),
            in_specs=whole(len(operands)),
            out_specs=whole(1)[0],
            compiler_params=params(),
            cost_estimate=little,
            name=name,
        )(*operands)

    def of_momentum(momentum, own, other):
        kernel = functools.partial(momentum_kernel, momentum, len(own))
        return call(kernel, len(own) * per, *own, *other, name="momentum")

    def by_energy(momentum, parts):
        kernel = functools.partial(by_energy_kernel, momentum, layers, sum(chunks, []))
        return call(kernel, local_e, *parts, name="by_energy")

    reach = -(-(total // 2) // local_e)

    ring = [z * moms for z in range(count)] + [z * moms + 1 for z in reversed(range(count))]
    ring = list(zip(ring, ring[1:] + ring[:1]))
    ways = ring, [(target, source) for source, target in ring]

    def hop(value, role):
        return lax.ppermute(value, ("energy", "mom"), ways[role])

    chunks = [[0], list(range(1, layers - 1)), [layers - 1]]
    fields = [[], []]
    hops = [[], []]
    for c in chunks:
        if len(hops[0]) == 1:
            own, _ = lax.optimization_barrier((own, hops))
            ahead = [hop(hops[m][0], m) for m in range(2)]
        held = [own[i] for i in c]
        if len(hops[0]) == 2:
            held, _ = lax.optimization_barrier((held, ahead))
        other = [lax.ppermute(v, "mom", both_ways) for v in held]
        for m in range(2):
            fields[m].append(of_momentum(m, held, other))
            hops[m].append(hop(fields[m][-1], m))
    zero, one = (by_energy(m, fields[m]) for m in range(2))
    smem = pl.BlockSpec(memory_space=pltpu.SMEM)
    retarded, local_lesser, table = pl.pallas_call(
        functools.partial(local_kernel, total),
        out_shape=[block] * 2 + [jax.ShapeDtypeStruct((total // 2 + 8, n), F32)],
        in_specs=[smem, smem] + whole(2),
        out_specs=whole(3),
        compiler_params=params(),
        name="local",
    )(phonon_shift, phonon_weight, zero, one)

    def mix(items, blocks, sums, last=False):
        scratch = [pltpu.VMEM(block.shape, F32)] * 2 + [pltpu.SemaphoreType.DMA((2, local_e))]
        return pl.pallas_call(
            functools.partial(mix_kernel, total, items, False, last),
            out_shape=[block] * 2,
            in_specs=whole(1 + len(blocks) + len(sums)),
            out_specs=[pl.BlockSpec(memory_space=pl.ANY)] * 2 if last else whole(2),
            scratch_shapes=scratch if last else [],
            compiler_params=params(),
            name="mix",
        )(table, *blocks, *sums)

    sums = [retarded, jnp.zeros_like(local_lesser)]
    for d in range(1, reach + 1):
        if d == 1:
            fields = hops
        elif d == 2:
            big, _ = lax.optimization_barrier((fields[0][1], fields[1][2]))
            fields = [[ahead[m], hop([big, fields[1][1]][m], m), hop(fields[m][2], m)] for m in range(2)]
        else:
            fields = [[hop(part, m) for part in fields[m]] for m in range(2)]
        zero, one = (by_energy(m, fields[m]) for m in range(2))
        if d < reach:
            sums = mix([(0, d), (1, d)], [zero, one], sums)
    sums = mix([(0, reach), (1, reach)], [zero, one], [*sums, local_lesser], last=True)
    retarded, lesser = sums
    return (retarded[None, None], lesser[None, None])


def solution(mesh):
    in_specs = (
        P("mom", "len", None, None, None),
        P("mom", "len", "energy", None, None, None),
        P("len", None, None),
        P(),
        P(),
        P(),
    )
    out_specs = (
        P("mom", "len", "energy", None, None, None),
        P("mom", "len", "energy", None, None, None),
    )
    return jax.shard_map(shards, mesh=mesh, in_specs=in_specs, out_specs=out_specs, check_vma=False)
```

```python
import functools

import jax
import jax.numpy as jnp
from jax import lax
from jax.experimental import pallas as pl
from jax.experimental.pallas import tpu as pltpu
from jax.sharding import PartitionSpec as P

F32 = jnp.float32
BF16 = jnp.bfloat16
VMEM_LIMIT = 16 * 1024 * 1024


def split(x):
    high = x.astype(BF16)
    return high, (x - high.astype(F32)).astype(BF16)


def dot(a, b):
    return jnp.dot(a, b, preferred_element_type=F32)


def dot3(a, b):
    rows = a[0].shape[0]
    both = dot(jnp.concatenate([a[0], a[1]], axis=0), b[0])
    return both[:rows] + (both[rows:] + dot(a[0], b[1]))


def right_form(m):
    n = m.shape[0]
    re, im = m[:, :n], m[:, n:]
    return jnp.concatenate([m, jnp.concatenate([-im, re], axis=1)], axis=0)


def right_pair(m):
    high, low = split(m)
    return right_form(high), right_form(low)


def identity(n):
    rows = lax.broadcasted_iota(jnp.int32, (n, 2 * n), 0)
    cols = lax.broadcasted_iota(jnp.int32, (n, 2 * n), 1)
    return (rows == cols).astype(F32)


def orders(layers):
    first = [layers - 1] + list(range(1, layers - 1))
    second = list(first)
    if layers > 3:
        second[1], second[2] = second[2], second[1]
    return first, second


def peers(layers):
    here = lax.axis_index("len")
    core = lax.axis_index("mom")
    first, second = orders(layers)
    return [here] + [here ^ jnp.where(core == 0, a, b) for a, b in zip(first, second)]


def inverse_kernel(total, layers, slots, ham_any, sig_any, coupling_any, pattern_any, *refs):
    out_refs = refs[: len(slots)]
    ham_ref, sig_ref, coupling_ref, pattern_ref, sems = refs[len(slots) :]
    _, per, _, n, _ = sig_ref.shape
    towards = [peers(layers)[slot] for slot in slots]
    copies = [
        pltpu.make_async_copy(ham_any, ham_ref, sems.at[0]),
        pltpu.make_async_copy(coupling_any, coupling_ref, sems.at[1]),
        pltpu.make_async_copy(pattern_any, pattern_ref, sems.at[2]),
    ]
    for i, peer in enumerate(towards):
        group = sig_any.at[pl.ds(peer * per, per)]
        copies.append(pltpu.make_async_copy(group, sig_ref.at[i], sems.at[3 + i]))
    for copy in copies:
        copy.start()
    for copy in copies:
        copy.wait()
    start = lax.axis_index("energy") * (layers * per)
    eye = identity(n)
    bond = coupling_ref[...] * pattern_ref[...].astype(F32)
    for i, (peer, out_ref) in enumerate(zip(towards, out_refs)):
        out_ref[2 * per] = bond
        for p in range(per):
            pos = jnp.full((1, n), start + peer * per + p, jnp.int32).astype(F32)
            zre = 5.0 + 2.0 * pos / total
            mag = zre * zre + 1.0
            qre = zre / mag
            qim = -1.0 / mag
            sre = ham_ref[0] + sig_ref[i, p, 0]
            sim = ham_ref[1] + sig_ref[i, p, 1]
            a1 = jnp.concatenate([qre * sre - qim * sim, qre * sim + qim * sre], axis=1)
            a1_pair = split(a1)
            a1_right = (right_form(a1_pair[0]), right_form(a1_pair[1]))
            a2 = dot3(a1_pair, a1_right)
            a2_pair = split(a2)
            a2_right = (right_form(a2_pair[0]), right_form(a2_pair[1]))
            a3 = dot3(a1_pair, a2_right)
            a4 = dot3(a2_pair, a2_right)
            s = eye + (a1 + (a2 + a3))
            x = s + dot3(split(s), right_pair(a4))
            re, im = x[:, :n], x[:, n:]
            out_ref[2 * p] = qre * re - qim * im
            out_ref[2 * p + 1] = qre * im + qim * re


def chain_kernel(layers, *refs):
    in_slots, out_slots = refs[:layers], refs[layers : 2 * layers]
    g_ref, bond_ref = refs[2 * layers :]
    _, per, _, n, _ = g_ref.shape
    for peer, in_slot in zip(peers(layers), in_slots):
        for p in range(per):
            g_ref[peer, p] = in_slot[2 * p : 2 * p + 2]
        bond_ref[peer] = in_slot[2 * per]
    bonds = [None] + [bond_ref[l] for l in range(1, layers)]
    bonds_t = [None] + [b.T for b in bonds[1:]]
    for p in range(per):
        g = [jnp.concatenate([g_ref[l, p, 0], g_ref[l, p, 1]], axis=1) for l in range(layers)]
        down = [None] * layers
        up = [None] * layers
        for l in range(layers):
            high, low = split(g[l])
            tall = (
                jnp.concatenate([high[:, :n], high[:, n:]], axis=0),
                jnp.concatenate([low[:, :n], low[:, n:]], axis=0),
            )
            wide = (high, low)
            if l > 0:
                u = dot3(tall, split(bonds[l]))
                v = dot3(split(bonds_t[l]), wide)
                down[l] = (split(jnp.concatenate([u[:n], u[n:]], axis=1)), right_pair(v))
            if l + 1 < layers:
                u = dot3(tall, split(bonds_t[l + 1]))
                v = dot3(split(bonds[l + 1]), wide)
                up[l] = (split(jnp.concatenate([u[:n], u[n:]], axis=1)), right_pair(v))
        green = list(g)
        gleft = g[0]
        gright = g[layers - 1]
        for step in range(1, layers):
            l = step
            u, v = down[l]
            term = dot3(split(dot3(u, right_pair(gleft))), v)
            green[l] = green[l] + term
            gleft = g[l] + term
            l = layers - 1 - step
            u, v = up[l]
            term = dot3(split(dot3(u, right_pair(gright))), v)
            green[l] = green[l] + term
            gright = g[l] + term
        for l in range(layers):
            near = [green[m] for m in (l - 1, l + 1) if 0 <= m < layers]
            y = green[l] + 0.5 * sum(near[1:], near[0]) if near else green[l]
            g_ref[l, p, 0] = y[:, :n]
            g_ref[l, p, 1] = y[:, n:]
    for peer, out_slot in zip(peers(layers), out_slots):
        out_slot[...] = g_ref[peer]


def momentum_kernel(momentum, slots, *refs):
    core = lax.axis_index("mom")
    out_ref = refs[-1]
    per = refs[0].shape[0]

    def place(blocks):
        for i, block in enumerate(blocks):
            out_ref[i * per : (i + 1) * per] = block[...]

    @pl.when(core == momentum)
    def _():
        place(refs[:slots])

    @pl.when(core != momentum)
    def _():
        place(refs[slots : 2 * slots])


def sender_kernel(momentum, own_ref, passed_ref, out_ref):
    place = lax.axis_index("energy")
    places = lax.axis_size("energy")
    up = lax.axis_index("mom") == momentum
    own = (up & (place < places // 2)) | (~up & (place >= places - places // 2))

    @pl.when(own)
    def _():
        out_ref[...] = own_ref[...]

    @pl.when(~own)
    def _():
        out_ref[...] = passed_ref[...]


def by_energy_kernel(momentum, layers, order, *refs):
    here = lax.axis_index("len")
    parts, out_ref = refs[:-1], refs[-1]
    per = out_ref.shape[0] // layers
    masks = [0] + orders(layers)[momentum]
    slots = [(part, i) for part in parts for i in range(part.shape[0] // per)]
    for slot, (part, i) in zip(order, slots):
        for p in range(per):
            out_ref[(here ^ masks[slot]) * per + p] = part[i * per + p]


def occupation(pos, total, n):
    return 1.0 / (1.0 + jnp.exp(8.0 * jnp.full((1, n), pos, jnp.int32).astype(F32) / total - 4.0))


def local_kernel(total, shift_ref, weight_ref, zero_ref, one_ref, ret_ref, les_ref, table_ref):
    n = table_ref.shape[1]
    phonons = shift_ref.shape[0]
    for t in range(1, total // 2 + 1):
        value = 0.0
        for m in range(phonons):
            value = value + jnp.where(shift_ref[m] == t, weight_ref[m], 0.0)
        table_ref[t : t + 1] = jnp.full((1, n), value, F32)
    items = [(0, 0), (1, 0)]
    mix_kernel(total, items, True, False, table_ref, zero_ref, one_ref, ret_ref, les_ref)


def mix_kernel(total, items, first, last, table_ref, *refs):
    count = len(items)
    inputs = count + (0 if first else 3 if last else 2)
    sums_in = refs[count:inputs]
    results = refs[inputs : inputs + 2]
    targets = refs[inputs + 2 : inputs + 4] if last else results
    local_e, _, n, _ = refs[0].shape
    place = lax.axis_index("energy")
    places = lax.axis_size("energy")
    core = lax.axis_index("mom")

    def copy_out(i, a):
        return pltpu.make_async_copy(targets[i].at[a], results[i].at[a], refs[-1].at[i, a])

    def body(here, some):
        most = total // 2
        terms = [[] for _ in range(local_e)]
        for i, (momentum, d) in enumerate(items):
            sign, factor = (-1, 1.0) if momentum == here else (1, 0.5)
            source = place + sign * d
            factor = jnp.where((source >= 0) & (source < places), factor, 0.0)
            for b in range(local_e):
                occ = occupation(source * local_e + b, total, n)
                for a in range(local_e):
                    t = d * local_e + sign * (b - a)
                    if some and 1 <= t <= most:
                        weight = table_ref[t : t + 1] * factor
                        terms[a].append((refs[i], b, weight, weight * occ))
        for i in range(2):
            for a in range(local_e):
                if first:
                    sums = [jnp.zeros((n, n), F32)] * 2
                else:
                    sums = [sums_in[i][a, c] for c in range(2)]
                for source, b, *weights in terms[a]:
                    sums = [sums[c] + weights[i] * source[b, c] for c in range(2)]
                if (first or last) and i == 1:
                    sums = [sums[0] - sums[0].T, sums[1] + sums[1].T]
                    if last:
                        sums = [sums[c] + sums_in[2][a, c] for c in range(2)]
                for c in range(2):
                    targets[i][a, c] = sums[c]
                if last:
                    copy_out(i, a).start()

    for here in range(2):
        if len(items) > 1:
            pl.when(core == here)(functools.partial(body, here, True))
            continue
        [(momentum, d)] = items
        some = place >= d if momentum == here else place + d < places
        pl.when((core == here) & some)(functools.partial(body, here, True))
        if last:
            pl.when((core == here) & ~some)(functools.partial(body, here, False))

    if last:
        for a in range(local_e):
            copy_out(0, a).wait()
            copy_out(1, a).wait()


def whole(count):
    return [pl.BlockSpec(memory_space=pltpu.VMEM)] * count


def params():
    return pltpu.CompilerParams(vmem_limit_bytes=VMEM_LIMIT)


def shards(hamiltonian, sigma_prev, coupling, coupling_pattern, phonon_shift, phonon_weight):
    local_e, _, n, _ = sigma_prev.shape[2:]
    layers = lax.axis_size("len")
    count = lax.axis_size("energy")
    moms = lax.axis_size("mom")
    total = local_e * count
    per = local_e // layers
    block = jax.ShapeDtypeStruct((local_e, 2, n, n), F32)
    first, second = orders(layers)

    def exchange(slots, i):
        if i == 0:
            return slots[0]
        pairs = []
        for l in range(layers):
            for k in range(moms):
                peer = l ^ (first, second)[k][i - 1]
                pairs.append((l * moms + k, peer * moms + k))
        return lax.ppermute(slots[i], ("len", "mom"), pairs)

    anywhere = pl.BlockSpec(memory_space=pltpu.HBM)
    inputs = (hamiltonian[0, 0], sigma_prev[0, 0], coupling[0], coupling_pattern)
    inputs = [pltpu.with_memory_space_constraint(value, pltpu.HBM) for value in inputs]

    def inverse(slots):
        return pl.pallas_call(
            functools.partial(inverse_kernel, total, layers, slots),
            out_shape=[jax.ShapeDtypeStruct((2 * per + 1, n, n), F32)] * len(slots),
            in_specs=[anywhere] * 4,
            out_specs=whole(len(slots)),
            scratch_shapes=[
                pltpu.VMEM((2, n, n), F32),
                pltpu.VMEM((len(slots), per, 2, n, n), F32),
                pltpu.VMEM((n, n), F32),
                pltpu.VMEM((n, n), jnp.int32),
                pltpu.SemaphoreType.DMA((3 + len(slots),)),
            ],
            compiler_params=params(),
            cost_estimate=pl.CostEstimate(
                flops=len(slots) * per * 96 * n**3, bytes_accessed=len(slots) * 8 * n * n, transcendentals=0
            ),
            name="inverse",
        )(*inputs)

    half = (layers + 1) // 2
    early = tuple(range(1, half + 1))
    late = tuple(range(half + 1, layers)) + (0,)
    sent = dict(zip(early, inverse(early))) | dict(zip(late, inverse(late)))
    part = jax.ShapeDtypeStruct((per, 2, n, n), F32)
    sent = pl.pallas_call(
        functools.partial(chain_kernel, layers),
        out_shape=[part] * layers,
        in_specs=whole(layers),
        out_specs=whole(layers),
        scratch_shapes=[pltpu.VMEM((layers, per, 2, n, n), F32), pltpu.VMEM((layers, n, n), F32)],
        compiler_params=params(),
        name="chains",
    )(*[exchange(sent, i) for i in range(layers)])
    own = [exchange(sent, i) for i in range(layers)]
    both_ways = [(k, moms - 1 - k) for k in range(moms)]
    little = pl.CostEstimate(flops=0, bytes_accessed=8 * n, transcendentals=0)

    def call(kernel, shape, *operands, name):
        return pl.pallas_call(
            kernel,
            out_shape=jax.ShapeDtypeStruct((shape, 2, n, n), F32),
            in_specs=whole(len(operands)),
            out_specs=whole(1)[0],
            compiler_params=params(),
            cost_estimate=little,
            name=name,
        )(*operands)

    def of_momentum(momentum, own, other):
        kernel = functools.partial(momentum_kernel, momentum, len(own))
        return call(kernel, len(own) * per, *own, *other, name="momentum")

    def by_energy(momentum, parts):
        kernel = functools.partial(by_energy_kernel, momentum, layers, sum(chunks, []))
        return call(kernel, local_e, *parts, name="by_energy")

    reach = -(-(total // 2) // local_e)

    ring = [z * moms for z in range(count)] + [z * moms + 1 for z in reversed(range(count))]
    ring = list(zip(ring, ring[1:] + ring[:1]))
    ways = ring, [(target, source) for source, target in ring]

    def hop(value, role):
        return lax.ppermute(value, ("energy", "mom"), ways[role])

    last, middle = count - 1, count // 2
    up = [(z, z + 2) for z in range(middle - 1)] + [(z, z + 1) for z in range(middle, last)]
    up += [(middle - 1, 1)]
    far_ways = []
    for m in range(2):
        pairs = [(z * moms + m, target * moms + m) for z, target in up]
        pairs += [((last - z) * moms + 1 - m, (last - target) * moms + 1 - m) for z, target in up]
        far_ways.append(pairs + [(last * moms + m, last * moms + 1 - m), (1 - m, m)])

    def second_hop(own, passed, m):
        kernel = functools.partial(sender_kernel, m)
        value = call(kernel, own.shape[0], own, passed, name="sender")
        return lax.ppermute(value, ("energy", "mom"), far_ways[m])

    chunks = [[0], list(range(1, layers))]
    fields = [[], []]
    hops = [[], []]
    for c in chunks:
        if len(hops[0]) == 1:
            own, _ = lax.optimization_barrier((own, hops))
        held = [own[i] for i in c]
        other = [lax.ppermute(v, "mom", both_ways) for v in held]
        for m in range(2):
            fields[m].append(of_momentum(m, held, other))
            hops[m].append(hop(fields[m][-1], m))
    zero, one = (by_energy(m, fields[m]) for m in range(2))
    smem = pl.BlockSpec(memory_space=pltpu.SMEM)
    retarded, local_lesser, table = pl.pallas_call(
        functools.partial(local_kernel, total),
        out_shape=[block] * 2 + [jax.ShapeDtypeStruct((total // 2 + 8, n), F32)],
        in_specs=[smem, smem] + whole(2),
        out_specs=whole(3),
        compiler_params=params(),
        name="local",
    )(phonon_shift, phonon_weight, zero, one)

    def mix(items, blocks, sums, last=False):
        scratch = [pltpu.VMEM(block.shape, F32)] * 2 + [pltpu.SemaphoreType.DMA((2, local_e))]
        count = 1 + len(blocks)
        in_place = len(items) == 1 and not last
        return pl.pallas_call(
            functools.partial(mix_kernel, total, items, False, last),
            out_shape=[block] * 2,
            in_specs=whole(1 + len(blocks) + len(sums)),
            out_specs=[pl.BlockSpec(memory_space=pl.ANY)] * 2 if last else whole(2),
            scratch_shapes=scratch if last else [],
            input_output_aliases={count: 0, count + 1: 1} if in_place else {},
            compiler_params=params(),
            name="mix",
        )(table, *blocks, *sums)

    sums = [retarded, jnp.zeros_like(local_lesser)]
    for d in range(1, reach + 1):
        if d == 1:
            starts, fields = fields, hops
        elif d == 2:
            ahead = [second_hop(starts[m][0], fields[m][0], m) for m in range(2)]
            held, _ = lax.optimization_barrier((fields[0][1], ahead))
            fields = [[ahead[m], second_hop(starts[m][1], (held, fields[1][1])[m], m)] for m in range(2)]
        else:
            fields = [[hop(part, m) for part in fields[m]] for m in range(2)]
        zero, one = (by_energy(m, fields[m]) for m in range(2))
        if d < reach:
            sums = mix([(0, d), (1, d)], [zero, one], sums)
    sums = mix([(0, reach)], [zero], sums)
    sums = mix([(1, reach)], [one], [*sums, local_lesser], last=True)
    retarded, lesser = sums
    return (retarded[None, None], lesser[None, None])


def solution(mesh):
    in_specs = (
        P("mom", "len", None, None, None),
        P("mom", "len", "energy", None, None, None),
        P("len", None, None),
        P(),
        P(),
        P(),
    )
    out_specs = (
        P("mom", "len", "energy", None, None, None),
        P("mom", "len", "energy", None, None, None),
    )
    return jax.shard_map(shards, mesh=mesh, in_specs=in_specs, out_specs=out_specs, check_vma=False)
```

```python
import functools
import itertools

import jax
import jax.numpy as jnp
from jax import lax
from jax.experimental import pallas as pl
from jax.experimental.pallas import tpu as pltpu
from jax.sharding import PartitionSpec as P

F32 = jnp.float32
BF16 = jnp.bfloat16
VMEM_LIMIT = 16 * 1024 * 1024


def split(x):
    high = x.astype(BF16)
    return high, (x - high.astype(F32)).astype(BF16)


def dot(a, b):
    return jnp.dot(a, b, preferred_element_type=F32)


def dot3(a, b):
    rows = a[0].shape[0]
    both = dot(jnp.concatenate([a[0], a[1]], axis=0), b[0])
    return both[:rows] + (both[rows:] + dot(a[0], b[1]))


def right_form(m):
    n = m.shape[0]
    re, im = m[:, :n], m[:, n:]
    return jnp.concatenate([m, jnp.concatenate([-im, re], axis=1)], axis=0)


def right_pair(m):
    high, low = split(m)
    return right_form(high), right_form(low)


def identity(n):
    rows = lax.broadcasted_iota(jnp.int32, (n, 2 * n), 0)
    cols = lax.broadcasted_iota(jnp.int32, (n, 2 * n), 1)
    return (rows == cols).astype(F32)


def orders(layers):
    first = [layers - 1] + list(range(1, layers - 1))
    second = list(first)
    if layers > 3:
        second[1], second[2] = second[2], second[1]
    return first, second


def peers(layers):
    here = lax.axis_index("len")
    core = lax.axis_index("mom")
    first, second = orders(layers)
    return [here] + [here ^ jnp.where(core == 0, a, b) for a, b in zip(first, second)]


def inverse_kernel(total, layers, slots, ham_any, sig_any, coupling_any, pattern_any, *refs):
    out_refs = refs[: len(slots)]
    ham_ref, sig_ref, coupling_ref, pattern_ref, sems = refs[len(slots) :]
    _, per, _, n, _ = sig_ref.shape
    towards = [peers(layers)[slot] for slot in slots]
    copies = [
        pltpu.make_async_copy(ham_any, ham_ref, sems.at[0]),
        pltpu.make_async_copy(coupling_any, coupling_ref, sems.at[1]),
        pltpu.make_async_copy(pattern_any, pattern_ref, sems.at[2]),
    ]
    for i, peer in enumerate(towards):
        group = sig_any.at[pl.ds(peer * per, per)]
        copies.append(pltpu.make_async_copy(group, sig_ref.at[i], sems.at[3 + i]))
    for copy in copies:
        copy.start()
    for copy in copies:
        copy.wait()
    start = lax.axis_index("energy") * (layers * per)
    eye = identity(n)
    bond = coupling_ref[...] * pattern_ref[...].astype(F32)
    for i, (peer, out_ref) in enumerate(zip(towards, out_refs)):
        out_ref[2 * per] = bond
        for p in range(per):
            pos = jnp.full((1, n), start + peer * per + p, jnp.int32).astype(F32)
            zre = 5.0 + 2.0 * pos / total
            mag = zre * zre + 1.0
            qre = zre / mag
            qim = -1.0 / mag
            sre = ham_ref[0] + sig_ref[i, p, 0]
            sim = ham_ref[1] + sig_ref[i, p, 1]
            a1 = jnp.concatenate([qre * sre - qim * sim, qre * sim + qim * sre], axis=1)
            a1_pair = split(a1)
            a1_right = (right_form(a1_pair[0]), right_form(a1_pair[1]))
            a2 = dot3(a1_pair, a1_right)
            a2_pair = split(a2)
            a2_right = (right_form(a2_pair[0]), right_form(a2_pair[1]))
            a3 = dot3(a1_pair, a2_right)
            a4 = dot3(a2_pair, a2_right)
            s = eye + (a1 + (a2 + a3))
            x = s + dot3(split(s), right_pair(a4))
            re, im = x[:, :n], x[:, n:]
            out_ref[2 * p] = qre * re - qim * im
            out_ref[2 * p + 1] = qre * im + qim * re


def chain_kernel(layers, *refs):
    in_slots, out_slots = refs[:layers], refs[layers : 2 * layers]
    g_ref, bond_ref = refs[2 * layers :]
    _, per, _, n, _ = g_ref.shape
    for peer, in_slot in zip(peers(layers), in_slots):
        for p in range(per):
            g_ref[peer, p] = in_slot[2 * p : 2 * p + 2]
        bond_ref[peer] = in_slot[2 * per]
    bonds = [None] + [bond_ref[l] for l in range(1, layers)]
    bonds_t = [None] + [b.T for b in bonds[1:]]
    for p in range(per):
        g = [jnp.concatenate([g_ref[l, p, 0], g_ref[l, p, 1]], axis=1) for l in range(layers)]
        down = [None] * layers
        up = [None] * layers
        for l in range(layers):
            high, low = split(g[l])
            tall = (
                jnp.concatenate([high[:, :n], high[:, n:]], axis=0),
                jnp.concatenate([low[:, :n], low[:, n:]], axis=0),
            )
            wide = (high, low)
            if l > 0:
                u = dot3(tall, split(bonds[l]))
                v = dot3(split(bonds_t[l]), wide)
                down[l] = (split(jnp.concatenate([u[:n], u[n:]], axis=1)), right_pair(v))
            if l + 1 < layers:
                u = dot3(tall, split(bonds_t[l + 1]))
                v = dot3(split(bonds[l + 1]), wide)
                up[l] = (split(jnp.concatenate([u[:n], u[n:]], axis=1)), right_pair(v))
        green = list(g)
        gleft = g[0]
        gright = g[layers - 1]
        for step in range(1, layers):
            l = step
            u, v = down[l]
            term = dot3(split(dot3(u, right_pair(gleft))), v)
            green[l] = green[l] + term
            gleft = g[l] + term
            l = layers - 1 - step
            u, v = up[l]
            term = dot3(split(dot3(u, right_pair(gright))), v)
            green[l] = green[l] + term
            gright = g[l] + term
        for l in range(layers):
            near = [green[m] for m in (l - 1, l + 1) if 0 <= m < layers]
            y = green[l] + 0.5 * sum(near[1:], near[0]) if near else green[l]
            g_ref[l, p, 0] = y[:, :n]
            g_ref[l, p, 1] = y[:, n:]
    for peer, out_slot in zip(peers(layers), out_slots):
        out_slot[...] = g_ref[peer]


def momentum_kernel(momentum, slots, *refs):
    core = lax.axis_index("mom")
    out_ref = refs[-1]
    per = refs[0].shape[0]

    def place(blocks):
        for i, block in enumerate(blocks):
            out_ref[i * per : (i + 1) * per] = block[...]

    @pl.when(core == momentum)
    def _():
        place(refs[:slots])

    @pl.when(core != momentum)
    def _():
        place(refs[slots : 2 * slots])


def by_energy_kernel(momentum, layers, order, *refs):
    here = lax.axis_index("len")
    parts, out_ref = refs[:-1], refs[-1]
    per = out_ref.shape[0] // layers
    masks = [0] + orders(layers)[momentum]
    slots = [(part, i) for part in parts for i in range(part.shape[0] // per)]
    for slot, (part, i) in zip(order, slots):
        for p in range(per):
            out_ref[(here ^ masks[slot]) * per + p] = part[i * per + p]


def occupation(pos, total, n):
    return 1.0 / (1.0 + jnp.exp(8.0 * jnp.full((1, n), pos, jnp.int32).astype(F32) / total - 4.0))


def local_kernel(total, shift_ref, weight_ref, zero_ref, one_ref, ret_ref, les_ref, table_ref):
    n = table_ref.shape[1]
    phonons = shift_ref.shape[0]
    for t in range(1, total // 2 + 1):
        value = 0.0
        for m in range(phonons):
            value = value + jnp.where(shift_ref[m] == t, weight_ref[m], 0.0)
        table_ref[t : t + 1] = jnp.full((1, n), value, F32)
    items = [(0, 0), (1, 0)]
    mix_kernel(total, items, True, False, table_ref, zero_ref, one_ref, ret_ref, les_ref)


def mix_kernel(total, items, first, last, table_ref, *refs):
    count = len(items)
    inputs = count + (0 if first else 3 if last else 2)
    sums_in = refs[count:inputs]
    results = refs[inputs : inputs + 2]
    targets = refs[inputs + 2 : inputs + 4] if last else results
    local_e, _, n, _ = refs[0].shape
    place = lax.axis_index("energy")
    places = lax.axis_size("energy")
    core = lax.axis_index("mom")

    def copy_out(i, a):
        return pltpu.make_async_copy(targets[i].at[a], results[i].at[a], refs[-1].at[i, a])

    def body(here, some):
        most = total // 2
        terms = [[] for _ in range(local_e)]
        for i, (momentum, d) in enumerate(items):
            sign, factor = (-1, 1.0) if momentum == here else (1, 0.5)
            source = place + sign * d
            factor = jnp.where((source >= 0) & (source < places), factor, 0.0)
            for b in range(local_e):
                occ = occupation(source * local_e + b, total, n)
                for a in range(local_e):
                    t = d * local_e + sign * (b - a)
                    if some[i] and 1 <= t <= most:
                        weight = table_ref[t : t + 1] * factor
                        terms[a].append((refs[i], b, weight, weight * occ))
        for i in range(2):
            for a in range(local_e):
                if first:
                    sums = [jnp.zeros((n, n), F32)] * 2
                else:
                    sums = [sums_in[i][a, c] for c in range(2)]
                for source, b, *weights in terms[a]:
                    sums = [sums[c] + weights[i] * source[b, c] for c in range(2)]
                if (first or last) and i == 1:
                    sums = [sums[0] - sums[0].T, sums[1] + sums[1].T]
                    if last:
                        sums = [sums[c] + sums_in[2][a, c] for c in range(2)]
                for c in range(2):
                    targets[i][a, c] = sums[c]
                if last:
                    copy_out(i, a).start()

    def present(here, momentum, d):
        return place >= d if momentum == here else place + d < places

    for here in range(2):
        if not last:
            pl.when(core == here)(functools.partial(body, here, [True] * count))
            continue
        for some in itertools.product([False, True], repeat=count):
            fits = core == here
            for (momentum, d), there in zip(items, some):
                fits = fits & (present(here, momentum, d) == there)
            pl.when(fits)(functools.partial(body, here, some))

    if last:
        for a in range(local_e):
            copy_out(0, a).wait()
            copy_out(1, a).wait()


def whole(count):
    return [pl.BlockSpec(memory_space=pltpu.VMEM)] * count


def params():
    return pltpu.CompilerParams(vmem_limit_bytes=VMEM_LIMIT)


def shards(hamiltonian, sigma_prev, coupling, coupling_pattern, phonon_shift, phonon_weight):
    local_e, _, n, _ = sigma_prev.shape[2:]
    layers = lax.axis_size("len")
    count = lax.axis_size("energy")
    moms = lax.axis_size("mom")
    total = local_e * count
    per = local_e // layers
    block = jax.ShapeDtypeStruct((local_e, 2, n, n), F32)
    first, second = orders(layers)

    def exchange(slots, i):
        if i == 0:
            return slots[0]
        pairs = []
        for l in range(layers):
            for k in range(moms):
                peer = l ^ (first, second)[k][i - 1]
                pairs.append((l * moms + k, peer * moms + k))
        return lax.ppermute(slots[i], ("len", "mom"), pairs)

    anywhere = pl.BlockSpec(memory_space=pltpu.HBM)
    inputs = (hamiltonian[0, 0], sigma_prev[0, 0], coupling[0], coupling_pattern)
    inputs = [pltpu.with_memory_space_constraint(value, pltpu.HBM) for value in inputs]

    def inverse(slots):
        return pl.pallas_call(
            functools.partial(inverse_kernel, total, layers, slots),
            out_shape=[jax.ShapeDtypeStruct((2 * per + 1, n, n), F32)] * len(slots),
            in_specs=[anywhere] * 4,
            out_specs=whole(len(slots)),
            scratch_shapes=[
                pltpu.VMEM((2, n, n), F32),
                pltpu.VMEM((len(slots), per, 2, n, n), F32),
                pltpu.VMEM((n, n), F32),
                pltpu.VMEM((n, n), jnp.int32),
                pltpu.SemaphoreType.DMA((3 + len(slots),)),
            ],
            compiler_params=params(),
            cost_estimate=pl.CostEstimate(
                flops=len(slots) * per * 96 * n**3, bytes_accessed=len(slots) * 8 * n * n, transcendentals=0
            ),
            name="inverse",
        )(*inputs)

    half = (layers + 1) // 2
    early = tuple(range(1, half + 1))
    late = tuple(range(half + 1, layers)) + (0,)
    sent = dict(zip(early, inverse(early))) | dict(zip(late, inverse(late)))
    part = jax.ShapeDtypeStruct((per, 2, n, n), F32)
    sent = pl.pallas_call(
        functools.partial(chain_kernel, layers),
        out_shape=[part] * layers,
        in_specs=whole(layers),
        out_specs=whole(layers),
        scratch_shapes=[pltpu.VMEM((layers, per, 2, n, n), F32), pltpu.VMEM((layers, n, n), F32)],
        compiler_params=params(),
        name="chains",
    )(*[exchange(sent, i) for i in range(layers)])
    own = [exchange(sent, i) for i in range(layers)]
    both_ways = [(k, moms - 1 - k) for k in range(moms)]
    little = pl.CostEstimate(flops=0, bytes_accessed=8 * n, transcendentals=0)

    def call(kernel, shape, *operands, name):
        return pl.pallas_call(
            kernel,
            out_shape=jax.ShapeDtypeStruct((shape, 2, n, n), F32),
            in_specs=whole(len(operands)),
            out_specs=whole(1)[0],
            compiler_params=params(),
            cost_estimate=little,
            name=name,
        )(*operands)

    def of_momentum(momentum, own, other):
        kernel = functools.partial(momentum_kernel, momentum, len(own))
        return call(kernel, len(own) * per, *own, *other, name="momentum")

    def by_energy(momentum, parts):
        kernel = functools.partial(by_energy_kernel, momentum, layers, sum(chunks, []))
        return call(kernel, local_e, *parts, name="by_energy")

    reach = -(-(total // 2) // local_e)

    ring = [z * moms for z in range(count)] + [z * moms + 1 for z in reversed(range(count))]
    ring = list(zip(ring, ring[1:] + ring[:1]))
    ways = ring, [(target, source) for source, target in ring]

    def hop(value, role):
        return lax.ppermute(value, ("energy", "mom"), ways[role])

    chunks = [[0], list(range(1, layers - 1)), [layers - 1]]
    fields = [[], []]
    hops = [[], []]
    for c in chunks:
        if len(hops[0]) == 1:
            own, _ = lax.optimization_barrier((own, hops))
            ahead = [hop(hops[m][0], m) for m in range(2)]
        held = [own[i] for i in c]
        other = [lax.ppermute(v, "mom", both_ways) for v in held]
        parts = [of_momentum(m, held, other) for m in range(2)]
        for m in range(2):
            fields[m].append(parts[m])
        if len(hops[0]) == 2:
            parts, _ = lax.optimization_barrier((parts, ahead))
        for m in range(2):
            hops[m].append(hop(parts[m], m))
    zero, one = (by_energy(m, fields[m]) for m in range(2))
    smem = pl.BlockSpec(memory_space=pltpu.SMEM)
    retarded, local_lesser, table = pl.pallas_call(
        functools.partial(local_kernel, total),
        out_shape=[block] * 2 + [jax.ShapeDtypeStruct((total // 2 + 8, n), F32)],
        in_specs=[smem, smem] + whole(2),
        out_specs=whole(3),
        compiler_params=params(),
        name="local",
    )(phonon_shift, phonon_weight, zero, one)

    def mix(items, blocks, sums, last=False):
        scratch = [pltpu.VMEM(block.shape, F32)] * 2 + [pltpu.SemaphoreType.DMA((2, local_e))]
        return pl.pallas_call(
            functools.partial(mix_kernel, total, items, False, last),
            out_shape=[block] * 2,
            in_specs=whole(1 + len(blocks) + len(sums)),
            out_specs=[pl.BlockSpec(memory_space=pl.ANY)] * 2 if last else whole(2),
            scratch_shapes=scratch if last else [],
            compiler_params=params(),
            name="mix",
        )(table, *blocks, *sums)

    sums = [retarded, jnp.zeros_like(local_lesser)]
    for d in range(1, reach + 1):
        if d == 1:
            fields = hops
        elif d == 2:
            big, _ = lax.optimization_barrier((fields[0][1], fields[1][2]))
            fields = [[ahead[m], hop([big, fields[1][1]][m], m), hop(fields[m][2], m)] for m in range(2)]
        else:
            fields = [[hop(part, m) for part in fields[m]] for m in range(2)]
        zero, one = (by_energy(m, fields[m]) for m in range(2))
        if d < reach:
            sums = mix([(0, d), (1, d)], [zero, one], sums)
    sums = mix([(0, reach), (1, reach)], [zero, one], [*sums, local_lesser], last=True)
    retarded, lesser = sums
    return (retarded[None, None], lesser[None, None])


def solution(mesh):
    in_specs = (
        P("mom", "len", None, None, None),
        P("mom", "len", "energy", None, None, None),
        P("len", None, None),
        P(),
        P(),
        P(),
    )
    out_specs = (
        P("mom", "len", "energy", None, None, None),
        P("mom", "len", "energy", None, None, None),
    )
    return jax.shard_map(shards, mesh=mesh, in_specs=in_specs, out_specs=out_specs, check_vma=False)
```

```python
import functools
import itertools

import jax
import jax.numpy as jnp
from jax import lax
from jax.experimental import pallas as pl
from jax.experimental.pallas import tpu as pltpu
from jax.sharding import PartitionSpec as P

F32 = jnp.float32
BF16 = jnp.bfloat16
VMEM_LIMIT = 16 * 1024 * 1024


def split(x):
    high = x.astype(BF16)
    return high, (x - high.astype(F32)).astype(BF16)


def dot(a, b):
    return jnp.dot(a, b, preferred_element_type=F32)


def dot3(a, b):
    rows = a[0].shape[0]
    both = dot(jnp.concatenate([a[0], a[1]], axis=0), b[0])
    return both[:rows] + (both[rows:] + dot(a[0], b[1]))


def right_form(m):
    n = m.shape[0]
    re, im = m[:, :n], m[:, n:]
    return jnp.concatenate([m, jnp.concatenate([-im, re], axis=1)], axis=0)


def right_pair(m):
    high, low = split(m)
    return right_form(high), right_form(low)


def identity(n):
    rows = lax.broadcasted_iota(jnp.int32, (n, 2 * n), 0)
    cols = lax.broadcasted_iota(jnp.int32, (n, 2 * n), 1)
    return (rows == cols).astype(F32)


def orders(layers):
    first = [layers - 1] + list(range(1, layers - 1))
    second = list(first)
    if layers > 3:
        second[1], second[2] = second[2], second[1]
    return first, second


def peers(layers):
    here = lax.axis_index("len")
    core = lax.axis_index("mom")
    first, second = orders(layers)
    return [here] + [here ^ jnp.where(core == 0, a, b) for a, b in zip(first, second)]


def inverse_kernel(total, layers, slots, ham_any, sig_any, coupling_any, pattern_any, *refs):
    out_refs = refs[: len(slots)]
    ham_ref, sig_ref, coupling_ref, pattern_ref, sems = refs[len(slots) :]
    _, per, _, n, _ = sig_ref.shape
    towards = [peers(layers)[slot] for slot in slots]
    copies = [
        pltpu.make_async_copy(ham_any, ham_ref, sems.at[0]),
        pltpu.make_async_copy(coupling_any, coupling_ref, sems.at[1]),
        pltpu.make_async_copy(pattern_any, pattern_ref, sems.at[2]),
    ]
    for i, peer in enumerate(towards):
        group = sig_any.at[pl.ds(peer * per, per)]
        copies.append(pltpu.make_async_copy(group, sig_ref.at[i], sems.at[3 + i]))
    for copy in copies:
        copy.start()
    for copy in copies:
        copy.wait()
    start = lax.axis_index("energy") * (layers * per)
    eye = identity(n)
    bond = coupling_ref[...] * pattern_ref[...].astype(F32)
    for i, (peer, out_ref) in enumerate(zip(towards, out_refs)):
        out_ref[2 * per] = bond
        for p in range(per):
            pos = jnp.full((1, n), start + peer * per + p, jnp.int32).astype(F32)
            zre = 5.0 + 2.0 * pos / total
            mag = zre * zre + 1.0
            qre = zre / mag
            qim = -1.0 / mag
            sre = ham_ref[0] + sig_ref[i, p, 0]
            sim = ham_ref[1] + sig_ref[i, p, 1]
            a1 = jnp.concatenate([qre * sre - qim * sim, qre * sim + qim * sre], axis=1)
            a1_pair = split(a1)
            a1_right = (right_form(a1_pair[0]), right_form(a1_pair[1]))
            a2 = dot3(a1_pair, a1_right)
            a2_pair = split(a2)
            a2_right = (right_form(a2_pair[0]), right_form(a2_pair[1]))
            a3 = dot3(a1_pair, a2_right)
            a4 = dot3(a2_pair, a2_right)
            s = eye + (a1 + (a2 + a3))
            x = s + dot3(split(s), right_pair(a4))
            re, im = x[:, :n], x[:, n:]
            out_ref[2 * p] = qre * re - qim * im
            out_ref[2 * p + 1] = qre * im + qim * re


def chain_kernel(layers, *refs):
    in_slots, out_slots = refs[:layers], refs[layers : 2 * layers]
    g_ref, bond_ref = refs[2 * layers :]
    _, per, _, n, _ = g_ref.shape
    for peer, in_slot in zip(peers(layers), in_slots):
        for p in range(per):
            g_ref[peer, p] = in_slot[2 * p : 2 * p + 2]
        bond_ref[peer] = in_slot[2 * per]
    bonds = [None] + [bond_ref[l] for l in range(1, layers)]
    bonds_t = [None] + [b.T for b in bonds[1:]]
    for p in range(per):
        g = [jnp.concatenate([g_ref[l, p, 0], g_ref[l, p, 1]], axis=1) for l in range(layers)]
        down = [None] * layers
        up = [None] * layers
        for l in range(layers):
            high, low = split(g[l])
            tall = (
                jnp.concatenate([high[:, :n], high[:, n:]], axis=0),
                jnp.concatenate([low[:, :n], low[:, n:]], axis=0),
            )
            wide = (high, low)
            if l > 0:
                u = dot3(tall, split(bonds[l]))
                v = dot3(split(bonds_t[l]), wide)
                down[l] = (split(jnp.concatenate([u[:n], u[n:]], axis=1)), right_pair(v))
            if l + 1 < layers:
                u = dot3(tall, split(bonds_t[l + 1]))
                v = dot3(split(bonds[l + 1]), wide)
                up[l] = (split(jnp.concatenate([u[:n], u[n:]], axis=1)), right_pair(v))
        green = list(g)
        gleft = g[0]
        gright = g[layers - 1]
        for step in range(1, layers):
            l = step
            u, v = down[l]
            term = dot3(split(dot3(u, right_pair(gleft))), v)
            green[l] = green[l] + term
            gleft = g[l] + term
            l = layers - 1 - step
            u, v = up[l]
            term = dot3(split(dot3(u, right_pair(gright))), v)
            green[l] = green[l] + term
            gright = g[l] + term
        for l in range(layers):
            near = [green[m] for m in (l - 1, l + 1) if 0 <= m < layers]
            y = green[l] + 0.5 * sum(near[1:], near[0]) if near else green[l]
            g_ref[l, p, 0] = y[:, :n]
            g_ref[l, p, 1] = y[:, n:]
    for peer, out_slot in zip(peers(layers), out_slots):
        out_slot[...] = g_ref[peer]


def momentum_kernel(momentum, slots, *refs):
    core = lax.axis_index("mom")
    out_ref = refs[-1]
    per = refs[0].shape[0]

    def place(blocks):
        for i, block in enumerate(blocks):
            out_ref[i * per : (i + 1) * per] = block[...]

    @pl.when(core == momentum)
    def _():
        place(refs[:slots])

    @pl.when(core != momentum)
    def _():
        place(refs[slots : 2 * slots])


def by_energy_kernel(momentum, layers, order, *refs):
    here = lax.axis_index("len")
    parts, out_ref = refs[:-1], refs[-1]
    per = out_ref.shape[0] // layers
    masks = [0] + orders(layers)[momentum]
    slots = [(part, i) for part in parts for i in range(part.shape[0] // per)]
    for slot, (part, i) in zip(order, slots):
        for p in range(per):
            out_ref[(here ^ masks[slot]) * per + p] = part[i * per + p]


def occupation(pos, total, n):
    return 1.0 / (1.0 + jnp.exp(8.0 * jnp.full((1, n), pos, jnp.int32).astype(F32) / total - 4.0))


def local_kernel(total, shift_ref, weight_ref, zero_ref, one_ref, ret_ref, les_ref, table_ref):
    n = table_ref.shape[1]
    phonons = shift_ref.shape[0]
    for t in range(1, total // 2 + 1):
        value = 0.0
        for m in range(phonons):
            value = value + jnp.where(shift_ref[m] == t, weight_ref[m], 0.0)
        table_ref[t : t + 1] = jnp.full((1, n), value, F32)
    items = [(0, 0), (1, 0)]
    mix_kernel(total, items, True, False, table_ref, zero_ref, one_ref, ret_ref, les_ref)


def mix_kernel(total, items, first, last, table_ref, *refs):
    count = len(items)
    inputs = count + (0 if first else 3 if last else 2)
    sums_in = refs[count:inputs]
    results = refs[inputs : inputs + 2]
    targets = refs[inputs + 2 : inputs + 4] if last else results
    local_e, _, n, _ = refs[0].shape
    place = lax.axis_index("energy")
    places = lax.axis_size("energy")
    core = lax.axis_index("mom")

    def copy_out(i, a):
        return pltpu.make_async_copy(targets[i].at[a], results[i].at[a], refs[-1].at[i, a])

    def body(here, some):
        most = total // 2
        terms = [[] for _ in range(local_e)]
        for i, (momentum, d) in enumerate(items):
            sign, factor = (-1, 1.0) if momentum == here else (1, 0.5)
            source = place + sign * d
            factor = jnp.where((source >= 0) & (source < places), factor, 0.0)
            for b in range(local_e):
                occ = occupation(source * local_e + b, total, n)
                for a in range(local_e):
                    t = d * local_e + sign * (b - a)
                    if some[i] and 1 <= t <= most:
                        weight = table_ref[t : t + 1] * factor
                        terms[a].append((refs[i], b, weight, weight * occ))
        for i in range(2):
            for a in range(local_e):
                if first:
                    sums = [jnp.zeros((n, n), F32)] * 2
                else:
                    sums = [sums_in[i][a, c] for c in range(2)]
                for source, b, *weights in terms[a]:
                    sums = [sums[c] + weights[i] * source[b, c] for c in range(2)]
                if (first or last) and i == 1:
                    sums = [sums[0] - sums[0].T, sums[1] + sums[1].T]
                    if last:
                        sums = [sums[c] + sums_in[2][a, c] for c in range(2)]
                for c in range(2):
                    targets[i][a, c] = sums[c]
                if last:
                    copy_out(i, a).start()

    def present(here, momentum, d):
        return place >= d if momentum == here else place + d < places

    for here in range(2):
        if not last:
            pl.when(core == here)(functools.partial(body, here, [True] * count))
            continue
        for some in itertools.product([False, True], repeat=count):
            fits = core == here
            for (momentum, d), there in zip(items, some):
                fits = fits & (present(here, momentum, d) == there)
            pl.when(fits)(functools.partial(body, here, some))

    if last:
        for a in range(local_e):
            copy_out(0, a).wait()
            copy_out(1, a).wait()


def whole(count):
    return [pl.BlockSpec(memory_space=pltpu.VMEM)] * count


def params():
    return pltpu.CompilerParams(vmem_limit_bytes=VMEM_LIMIT)


def shards(hamiltonian, sigma_prev, coupling, coupling_pattern, phonon_shift, phonon_weight):
    local_e, _, n, _ = sigma_prev.shape[2:]
    layers = lax.axis_size("len")
    count = lax.axis_size("energy")
    moms = lax.axis_size("mom")
    total = local_e * count
    per = local_e // layers
    block = jax.ShapeDtypeStruct((local_e, 2, n, n), F32)
    first, second = orders(layers)

    def exchange(slots, i):
        if i == 0:
            return slots[0]
        pairs = []
        for l in range(layers):
            for k in range(moms):
                peer = l ^ (first, second)[k][i - 1]
                pairs.append((l * moms + k, peer * moms + k))
        return lax.ppermute(slots[i], ("len", "mom"), pairs)

    anywhere = pl.BlockSpec(memory_space=pltpu.HBM)
    inputs = (hamiltonian[0, 0], sigma_prev[0, 0], coupling[0], coupling_pattern)
    inputs = [pltpu.with_memory_space_constraint(value, pltpu.HBM) for value in inputs]

    def inverse(slots):
        return pl.pallas_call(
            functools.partial(inverse_kernel, total, layers, slots),
            out_shape=[jax.ShapeDtypeStruct((2 * per + 1, n, n), F32)] * len(slots),
            in_specs=[anywhere] * 4,
            out_specs=whole(len(slots)),
            scratch_shapes=[
                pltpu.VMEM((2, n, n), F32),
                pltpu.VMEM((len(slots), per, 2, n, n), F32),
                pltpu.VMEM((n, n), F32),
                pltpu.VMEM((n, n), jnp.int32),
                pltpu.SemaphoreType.DMA((3 + len(slots),)),
            ],
            compiler_params=params(),
            cost_estimate=pl.CostEstimate(
                flops=len(slots) * per * 96 * n**3, bytes_accessed=len(slots) * 8 * n * n, transcendentals=0
            ),
            name="inverse",
        )(*inputs)

    half = (layers + 1) // 2
    early = tuple(range(1, half + 1))
    late = tuple(range(half + 1, layers)) + (0,)
    sent = dict(zip(early, inverse(early))) | dict(zip(late, inverse(late)))
    part = jax.ShapeDtypeStruct((per, 2, n, n), F32)
    sent = pl.pallas_call(
        functools.partial(chain_kernel, layers),
        out_shape=[part] * layers,
        in_specs=whole(layers),
        out_specs=whole(layers),
        scratch_shapes=[pltpu.VMEM((layers, per, 2, n, n), F32), pltpu.VMEM((layers, n, n), F32)],
        compiler_params=params(),
        name="chains",
    )(*[exchange(sent, i) for i in range(layers)])
    own = [exchange(sent, i) for i in range(layers)]
    both_ways = [(k, moms - 1 - k) for k in range(moms)]
    little = pl.CostEstimate(flops=0, bytes_accessed=8 * n, transcendentals=0)

    def call(kernel, shape, *operands, name):
        return pl.pallas_call(
            kernel,
            out_shape=jax.ShapeDtypeStruct((shape, 2, n, n), F32),
            in_specs=whole(len(operands)),
            out_specs=whole(1)[0],
            compiler_params=params(),
            cost_estimate=little,
            name=name,
        )(*operands)

    def of_momentum(momentum, own, other):
        kernel = functools.partial(momentum_kernel, momentum, len(own))
        return call(kernel, len(own) * per, *own, *other, name="momentum")

    def by_energy(momentum, parts):
        kernel = functools.partial(by_energy_kernel, momentum, layers, sum(chunks, []))
        return call(kernel, local_e, *parts, name="by_energy")

    reach = -(-(total // 2) // local_e)

    ring = [z * moms for z in range(count)] + [z * moms + 1 for z in reversed(range(count))]
    ring = list(zip(ring, ring[1:] + ring[:1]))
    ways = ring, [(target, source) for source, target in ring]

    def hop(value, role):
        return lax.ppermute(value, ("energy", "mom"), ways[role])

    chunks = [[0], list(range(1, layers - 1)), [layers - 1]]
    fields = [[], []]
    hops = [[], []]
    for c in chunks:
        if len(hops[0]) == 1:
            own, _ = lax.optimization_barrier((own, hops[0]))
            ahead = [hop(hops[m][0], m) for m in range(2)]
        held = [own[i] for i in c]
        other = [lax.ppermute(v, "mom", both_ways) for v in held]
        parts = [of_momentum(m, held, other) for m in range(2)]
        for m in range(2):
            fields[m].append(parts[m])
        if len(hops[0]) == 2:
            parts, _ = lax.optimization_barrier((parts, ahead))
        for m in range(2):
            hops[m].append(hop(parts[m], m))
    zero, one = (by_energy(m, fields[m]) for m in range(2))
    smem = pl.BlockSpec(memory_space=pltpu.SMEM)
    retarded, local_lesser, table = pl.pallas_call(
        functools.partial(local_kernel, total),
        out_shape=[block] * 2 + [jax.ShapeDtypeStruct((total // 2 + 8, n), F32)],
        in_specs=[smem, smem] + whole(2),
        out_specs=whole(3),
        compiler_params=params(),
        name="local",
    )(phonon_shift, phonon_weight, zero, one)

    def mix(items, blocks, sums, last=False):
        scratch = [pltpu.VMEM(block.shape, F32)] * 2 + [pltpu.SemaphoreType.DMA((2, local_e))]
        return pl.pallas_call(
            functools.partial(mix_kernel, total, items, False, last),
            out_shape=[block] * 2,
            in_specs=whole(1 + len(blocks) + len(sums)),
            out_specs=[pl.BlockSpec(memory_space=pl.ANY)] * 2 if last else whole(2),
            scratch_shapes=scratch if last else [],
            compiler_params=params(),
            name="mix",
        )(table, *blocks, *sums)

    sums = [retarded, jnp.zeros_like(local_lesser)]
    for d in range(1, reach + 1):
        if d == 1:
            fields = hops
        elif d == 2:
            big, _ = lax.optimization_barrier((fields[0][1], fields[1][2]))
            fields = [[ahead[m], hop([big, fields[1][1]][m], m), hop(fields[m][2], m)] for m in range(2)]
        else:
            fields = [[hop(part, m) for part in fields[m]] for m in range(2)]
        zero, one = (by_energy(m, fields[m]) for m in range(2))
        if d < reach:
            sums = mix([(0, d), (1, d)], [zero, one], sums)
    sums = mix([(0, reach), (1, reach)], [zero, one], [*sums, local_lesser], last=True)
    retarded, lesser = sums
    return (retarded[None, None], lesser[None, None])


def solution(mesh):
    in_specs = (
        P("mom", "len", None, None, None),
        P("mom", "len", "energy", None, None, None),
        P("len", None, None),
        P(),
        P(),
        P(),
    )
    out_specs = (
        P("mom", "len", "energy", None, None, None),
        P("mom", "len", "energy", None, None, None),
    )
    return jax.shard_map(shards, mesh=mesh, in_specs=in_specs, out_specs=out_specs, check_vma=False)
```

```python
import functools
import itertools

import jax
import jax.numpy as jnp
from jax import lax
from jax.experimental import pallas as pl
from jax.experimental.pallas import tpu as pltpu
from jax.sharding import PartitionSpec as P

F32 = jnp.float32
BF16 = jnp.bfloat16
VMEM_LIMIT = 16 * 1024 * 1024


def split(x):
    high = x.astype(BF16)
    return high, (x - high.astype(F32)).astype(BF16)


def dot(a, b):
    return jnp.dot(a, b, preferred_element_type=F32)


def dot3(a, b):
    rows = a[0].shape[0]
    both = dot(jnp.concatenate([a[0], a[1]], axis=0), b[0])
    return both[:rows] + (both[rows:] + dot(a[0], b[1]))


def right_form(m):
    n = m.shape[0]
    re, im = m[:, :n], m[:, n:]
    return jnp.concatenate([m, jnp.concatenate([-im, re], axis=1)], axis=0)


def right_pair(m):
    high, low = split(m)
    return right_form(high), right_form(low)


def identity(n):
    rows = lax.broadcasted_iota(jnp.int32, (n, 2 * n), 0)
    cols = lax.broadcasted_iota(jnp.int32, (n, 2 * n), 1)
    return (rows == cols).astype(F32)


def orders(layers):
    first = [layers - 1] + list(range(1, layers - 1))
    second = list(first)
    if layers > 3:
        second[1], second[2] = second[2], second[1]
    return first, second


def peers(layers):
    here = lax.axis_index("len")
    core = lax.axis_index("mom")
    first, second = orders(layers)
    return [here] + [here ^ jnp.where(core == 0, a, b) for a, b in zip(first, second)]


def inverse_kernel(total, layers, slots, ham_any, sig_any, coupling_any, pattern_any, *refs):
    out_refs = refs[: len(slots)]
    ham_ref, sig_ref, coupling_ref, pattern_ref, sems = refs[len(slots) :]
    _, per, _, n, _ = sig_ref.shape
    towards = [peers(layers)[slot] for slot in slots]
    copies = [
        pltpu.make_async_copy(ham_any, ham_ref, sems.at[0]),
        pltpu.make_async_copy(coupling_any, coupling_ref, sems.at[1]),
        pltpu.make_async_copy(pattern_any, pattern_ref, sems.at[2]),
    ]
    for i, peer in enumerate(towards):
        group = sig_any.at[pl.ds(peer * per, per)]
        copies.append(pltpu.make_async_copy(group, sig_ref.at[i], sems.at[3 + i]))
    for copy in copies:
        copy.start()
    for copy in copies:
        copy.wait()
    start = lax.axis_index("energy") * (layers * per)
    eye = identity(n)
    bond = coupling_ref[...] * pattern_ref[...].astype(F32)
    for i, (peer, out_ref) in enumerate(zip(towards, out_refs)):
        out_ref[2 * per] = bond
        for p in range(per):
            pos = jnp.full((1, n), start + peer * per + p, jnp.int32).astype(F32)
            zre = 5.0 + 2.0 * pos / total
            mag = zre * zre + 1.0
            qre = zre / mag
            qim = -1.0 / mag
            sre = ham_ref[0] + sig_ref[i, p, 0]
            sim = ham_ref[1] + sig_ref[i, p, 1]
            a1 = jnp.concatenate([qre * sre - qim * sim, qre * sim + qim * sre], axis=1)
            a1_pair = split(a1)
            a1_right = (right_form(a1_pair[0]), right_form(a1_pair[1]))
            a2 = dot3(a1_pair, a1_right)
            a2_pair = split(a2)
            a2_right = (right_form(a2_pair[0]), right_form(a2_pair[1]))
            a3 = dot3(a1_pair, a2_right)
            a4 = dot3(a2_pair, a2_right)
            s = eye + (a1 + (a2 + a3))
            x = s + dot3(split(s), right_pair(a4))
            re, im = x[:, :n], x[:, n:]
            out_ref[2 * p] = qre * re - qim * im
            out_ref[2 * p + 1] = qre * im + qim * re


def chain_kernel(layers, *refs):
    in_slots, out_slots = refs[:layers], refs[layers : 2 * layers]
    g_ref, bond_ref = refs[2 * layers :]
    _, per, _, n, _ = g_ref.shape
    for peer, in_slot in zip(peers(layers), in_slots):
        for p in range(per):
            g_ref[peer, p] = in_slot[2 * p : 2 * p + 2]
        bond_ref[peer] = in_slot[2 * per]
    bonds = [None] + [bond_ref[l] for l in range(1, layers)]
    bonds_t = [None] + [b.T for b in bonds[1:]]
    for p in range(per):
        g = [jnp.concatenate([g_ref[l, p, 0], g_ref[l, p, 1]], axis=1) for l in range(layers)]
        down = [None] * layers
        up = [None] * layers
        for l in range(layers):
            high, low = split(g[l])
            tall = (
                jnp.concatenate([high[:, :n], high[:, n:]], axis=0),
                jnp.concatenate([low[:, :n], low[:, n:]], axis=0),
            )
            wide = (high, low)
            if l > 0:
                u = dot3(tall, split(bonds[l]))
                v = dot3(split(bonds_t[l]), wide)
                down[l] = (split(jnp.concatenate([u[:n], u[n:]], axis=1)), right_pair(v))
            if l + 1 < layers:
                u = dot3(tall, split(bonds_t[l + 1]))
                v = dot3(split(bonds[l + 1]), wide)
                up[l] = (split(jnp.concatenate([u[:n], u[n:]], axis=1)), right_pair(v))
        green = list(g)
        gleft = g[0]
        gright = g[layers - 1]
        for step in range(1, layers):
            l = step
            u, v = down[l]
            term = dot3(split(dot3(u, right_pair(gleft))), v)
            green[l] = green[l] + term
            gleft = g[l] + term
            l = layers - 1 - step
            u, v = up[l]
            term = dot3(split(dot3(u, right_pair(gright))), v)
            green[l] = green[l] + term
            gright = g[l] + term
        for l in range(layers):
            near = [green[m] for m in (l - 1, l + 1) if 0 <= m < layers]
            y = green[l] + 0.5 * sum(near[1:], near[0]) if near else green[l]
            g_ref[l, p, 0] = y[:, :n]
            g_ref[l, p, 1] = y[:, n:]
    for peer, out_slot in zip(peers(layers), out_slots):
        out_slot[...] = g_ref[peer]


def momentum_kernel(momentum, slots, *refs):
    core = lax.axis_index("mom")
    out_ref = refs[-1]
    per = refs[0].shape[0]

    def place(blocks):
        for i, block in enumerate(blocks):
            out_ref[i * per : (i + 1) * per] = block[...]

    @pl.when(core == momentum)
    def _():
        place(refs[:slots])

    @pl.when(core != momentum)
    def _():
        place(refs[slots : 2 * slots])


def by_energy_kernel(momentum, layers, order, *refs):
    here = lax.axis_index("len")
    parts, out_ref = refs[:-1], refs[-1]
    per = out_ref.shape[0] // layers
    masks = [0] + orders(layers)[momentum]
    slots = [(part, i) for part in parts for i in range(part.shape[0] // per)]
    for slot, (part, i) in zip(order, slots):
        for p in range(per):
            out_ref[(here ^ masks[slot]) * per + p] = part[i * per + p]


def occupation(pos, total, n):
    return 1.0 / (1.0 + jnp.exp(8.0 * jnp.full((1, n), pos, jnp.int32).astype(F32) / total - 4.0))


def local_kernel(total, shift_ref, weight_ref, zero_ref, one_ref, ret_ref, les_ref, table_ref):
    n = table_ref.shape[1]
    phonons = shift_ref.shape[0]
    for t in range(1, total // 2 + 1):
        value = 0.0
        for m in range(phonons):
            value = value + jnp.where(shift_ref[m] == t, weight_ref[m], 0.0)
        table_ref[t : t + 1] = jnp.full((1, n), value, F32)
    items = [(0, 0), (1, 0)]
    mix_kernel(total, items, True, False, table_ref, zero_ref, one_ref, ret_ref, les_ref)


def mix_kernel(total, items, first, last, table_ref, *refs):
    count = len(items)
    inputs = count + (0 if first else 3 if last else 2)
    sums_in = refs[count:inputs]
    results = refs[inputs : inputs + 2]
    targets = refs[inputs + 2 : inputs + 4] if last else results
    local_e, _, n, _ = refs[0].shape
    place = lax.axis_index("energy")
    places = lax.axis_size("energy")
    core = lax.axis_index("mom")

    def copy_out(i, a):
        return pltpu.make_async_copy(targets[i].at[a], results[i].at[a], refs[-1].at[i, a])

    def body(here, some):
        most = total // 2
        terms = [[] for _ in range(local_e)]
        for i, (momentum, d) in enumerate(items):
            sign, factor = (-1, 1.0) if momentum == here else (1, 0.5)
            source = place + sign * d
            factor = jnp.where((source >= 0) & (source < places), factor, 0.0)
            for b in range(local_e):
                occ = occupation(source * local_e + b, total, n)
                for a in range(local_e):
                    t = d * local_e + sign * (b - a)
                    if some[i] and 1 <= t <= most:
                        weight = table_ref[t : t + 1] * factor
                        terms[a].append((refs[i], b, weight, weight * occ))
        for i in range(2):
            for a in range(local_e):
                if first:
                    sums = [jnp.zeros((n, n), F32)] * 2
                else:
                    sums = [sums_in[i][a, c] for c in range(2)]
                for source, b, *weights in terms[a]:
                    sums = [sums[c] + weights[i] * source[b, c] for c in range(2)]
                if (first or last) and i == 1:
                    sums = [sums[0] - sums[0].T, sums[1] + sums[1].T]
                    if last:
                        sums = [sums[c] + sums_in[2][a, c] for c in range(2)]
                for c in range(2):
                    targets[i][a, c] = sums[c]
                if last:
                    copy_out(i, a).start()

    def present(here, momentum, d):
        return place >= d if momentum == here else place + d < places

    for here in range(2):
        if not last:
            pl.when(core == here)(functools.partial(body, here, [True] * count))
            continue
        for some in itertools.product([False, True], repeat=count):
            fits = core == here
            for (momentum, d), there in zip(items, some):
                fits = fits & (present(here, momentum, d) == there)
            pl.when(fits)(functools.partial(body, here, some))

    if last:
        for a in range(local_e):
            copy_out(0, a).wait()
            copy_out(1, a).wait()


def whole(count):
    return [pl.BlockSpec(memory_space=pltpu.VMEM)] * count


def params():
    return pltpu.CompilerParams(vmem_limit_bytes=VMEM_LIMIT)


def shards(hamiltonian, sigma_prev, coupling, coupling_pattern, phonon_shift, phonon_weight):
    local_e, _, n, _ = sigma_prev.shape[2:]
    layers = lax.axis_size("len")
    count = lax.axis_size("energy")
    moms = lax.axis_size("mom")
    total = local_e * count
    per = local_e // layers
    block = jax.ShapeDtypeStruct((local_e, 2, n, n), F32)
    first, second = orders(layers)

    def exchange(slots, i):
        if i == 0:
            return slots[0]
        pairs = []
        for l in range(layers):
            for k in range(moms):
                peer = l ^ (first, second)[k][i - 1]
                pairs.append((l * moms + k, peer * moms + k))
        return lax.ppermute(slots[i], ("len", "mom"), pairs)

    anywhere = pl.BlockSpec(memory_space=pltpu.HBM)
    inputs = (hamiltonian[0, 0], sigma_prev[0, 0], coupling[0], coupling_pattern)
    inputs = [pltpu.with_memory_space_constraint(value, pltpu.HBM) for value in inputs]

    def inverse(slots):
        return pl.pallas_call(
            functools.partial(inverse_kernel, total, layers, slots),
            out_shape=[jax.ShapeDtypeStruct((2 * per + 1, n, n), F32)] * len(slots),
            in_specs=[anywhere] * 4,
            out_specs=whole(len(slots)),
            scratch_shapes=[
                pltpu.VMEM((2, n, n), F32),
                pltpu.VMEM((len(slots), per, 2, n, n), F32),
                pltpu.VMEM((n, n), F32),
                pltpu.VMEM((n, n), jnp.int32),
                pltpu.SemaphoreType.DMA((3 + len(slots),)),
            ],
            compiler_params=params(),
            cost_estimate=pl.CostEstimate(
                flops=len(slots) * per * 96 * n**3, bytes_accessed=len(slots) * 8 * n * n, transcendentals=0
            ),
            name="inverse",
        )(*inputs)

    half = (layers + 1) // 2
    early = tuple(range(1, half + 1))
    late = tuple(range(half + 1, layers)) + (0,)
    sent = dict(zip(early, inverse(early))) | dict(zip(late, inverse(late)))
    part = jax.ShapeDtypeStruct((per, 2, n, n), F32)
    sent = pl.pallas_call(
        functools.partial(chain_kernel, layers),
        out_shape=[part] * layers,
        in_specs=whole(layers),
        out_specs=whole(layers),
        scratch_shapes=[pltpu.VMEM((layers, per, 2, n, n), F32), pltpu.VMEM((layers, n, n), F32)],
        compiler_params=params(),
        name="chains",
    )(*[exchange(sent, i) for i in range(layers)])
    own = [exchange(sent, i) for i in range(layers)]
    both_ways = [(k, moms - 1 - k) for k in range(moms)]
    little = pl.CostEstimate(flops=0, bytes_accessed=8 * n, transcendentals=0)

    def call(kernel, shape, *operands, name):
        return pl.pallas_call(
            kernel,
            out_shape=jax.ShapeDtypeStruct((shape, 2, n, n), F32),
            in_specs=whole(len(operands)),
            out_specs=whole(1)[0],
            compiler_params=params(),
            cost_estimate=little,
            name=name,
        )(*operands)

    def of_momentum(momentum, own, other):
        kernel = functools.partial(momentum_kernel, momentum, len(own))
        return call(kernel, len(own) * per, *own, *other, name="momentum")

    def by_energy(momentum, parts):
        kernel = functools.partial(by_energy_kernel, momentum, layers, sum(chunks, []))
        return call(kernel, local_e, *parts, name="by_energy")

    reach = -(-(total // 2) // local_e)

    ring = [z * moms for z in range(count)] + [z * moms + 1 for z in reversed(range(count))]
    ring = list(zip(ring, ring[1:] + ring[:1]))
    ways = ring, [(target, source) for source, target in ring]

    def hop(value, role):
        return lax.ppermute(value, ("energy", "mom"), ways[role])

    chunks = [[0], list(range(1, layers - 1)), [layers - 1]]
    fields = [[], []]
    hops = [[], []]
    for c in chunks:
        if len(hops[0]) == 1:
            own, _ = lax.optimization_barrier((own, hops[0]))
            ahead = [hop(hops[m][0], m) for m in range(2)]
        held = [own[i] for i in c]
        other = [lax.ppermute(v, "mom", both_ways) for v in held]
        parts = [of_momentum(m, held, other) for m in range(2)]
        for m in range(2):
            fields[m].append(parts[m])
        if len(hops[0]) == 2:
            parts = [lax.optimization_barrier((parts[m], ahead[m]))[0] for m in range(2)]
        for m in range(2):
            hops[m].append(hop(parts[m], m))
    zero, one = (by_energy(m, fields[m]) for m in range(2))
    smem = pl.BlockSpec(memory_space=pltpu.SMEM)
    retarded, local_lesser, table = pl.pallas_call(
        functools.partial(local_kernel, total),
        out_shape=[block] * 2 + [jax.ShapeDtypeStruct((total // 2 + 8, n), F32)],
        in_specs=[smem, smem] + whole(2),
        out_specs=whole(3),
        compiler_params=params(),
        name="local",
    )(phonon_shift, phonon_weight, zero, one)

    def mix(items, blocks, sums, last=False):
        scratch = [pltpu.VMEM(block.shape, F32)] * 2 + [pltpu.SemaphoreType.DMA((2, local_e))]
        return pl.pallas_call(
            functools.partial(mix_kernel, total, items, False, last),
            out_shape=[block] * 2,
            in_specs=whole(1 + len(blocks) + len(sums)),
            out_specs=[pl.BlockSpec(memory_space=pl.ANY)] * 2 if last else whole(2),
            scratch_shapes=scratch if last else [],
            compiler_params=params(),
            name="mix",
        )(table, *blocks, *sums)

    sums = [retarded, jnp.zeros_like(local_lesser)]
    for d in range(1, reach + 1):
        if d == 1:
            fields = hops
        elif d == 2:
            big, _ = lax.optimization_barrier((fields[0][1], fields[1][2]))
            fields = [[ahead[m], hop([big, fields[1][1]][m], m), hop(fields[m][2], m)] for m in range(2)]
        else:
            fields = [[hop(part, m) for part in fields[m]] for m in range(2)]
        zero, one = (by_energy(m, fields[m]) for m in range(2))
        if d < reach:
            sums = mix([(0, d), (1, d)], [zero, one], sums)
    sums = mix([(0, reach), (1, reach)], [zero, one], [*sums, local_lesser], last=True)
    retarded, lesser = sums
    return (retarded[None, None], lesser[None, None])


def solution(mesh):
    in_specs = (
        P("mom", "len", None, None, None),
        P("mom", "len", "energy", None, None, None),
        P("len", None, None),
        P(),
        P(),
        P(),
    )
    out_specs = (
        P("mom", "len", "energy", None, None, None),
        P("mom", "len", "energy", None, None, None),
    )
    return jax.shard_map(shards, mesh=mesh, in_specs=in_specs, out_specs=out_specs, check_vma=False)
```

```python
import functools
import itertools

import jax
import jax.numpy as jnp
from jax import lax
from jax.experimental import pallas as pl
from jax.experimental.pallas import tpu as pltpu
from jax.sharding import PartitionSpec as P

F32 = jnp.float32
BF16 = jnp.bfloat16
VMEM_LIMIT = 16 * 1024 * 1024


def split(x):
    high = x.astype(BF16)
    return high, (x - high.astype(F32)).astype(BF16)


def dot(a, b):
    return jnp.dot(a, b, preferred_element_type=F32)


def dot3(a, b):
    rows = a[0].shape[0]
    both = dot(jnp.concatenate([a[0], a[1]], axis=0), b[0])
    return both[:rows] + (both[rows:] + dot(a[0], b[1]))


def right_form(m):
    n = m.shape[0]
    re, im = m[:, :n], m[:, n:]
    return jnp.concatenate([m, jnp.concatenate([-im, re], axis=1)], axis=0)


def right_pair(m):
    high, low = split(m)
    return right_form(high), right_form(low)


def identity(n):
    rows = lax.broadcasted_iota(jnp.int32, (n, 2 * n), 0)
    cols = lax.broadcasted_iota(jnp.int32, (n, 2 * n), 1)
    return (rows == cols).astype(F32)


def orders(layers):
    first = [layers - 1] + list(range(1, layers - 1))
    second = list(first)
    if layers > 3:
        second[1], second[2] = second[2], second[1]
    return first, second


def peers(layers):
    here = lax.axis_index("len")
    core = lax.axis_index("mom")
    first, second = orders(layers)
    return [here] + [here ^ jnp.where(core == 0, a, b) for a, b in zip(first, second)]


def inverse_kernel(total, layers, slots, ham_any, sig_any, coupling_any, pattern_any, *refs):
    out_refs = refs[: len(slots)]
    ham_ref, sig_ref, coupling_ref, pattern_ref, sems = refs[len(slots) :]
    _, per, _, n, _ = sig_ref.shape
    towards = [peers(layers)[slot] for slot in slots]
    copies = [
        pltpu.make_async_copy(ham_any, ham_ref, sems.at[0]),
        pltpu.make_async_copy(coupling_any, coupling_ref, sems.at[1]),
        pltpu.make_async_copy(pattern_any, pattern_ref, sems.at[2]),
    ]
    for i, peer in enumerate(towards):
        group = sig_any.at[pl.ds(peer * per, per)]
        copies.append(pltpu.make_async_copy(group, sig_ref.at[i], sems.at[3 + i]))
    for copy in copies:
        copy.start()
    for copy in copies:
        copy.wait()
    start = lax.axis_index("energy") * (layers * per)
    eye = identity(n)
    bond = coupling_ref[...] * pattern_ref[...].astype(F32)
    for i, (peer, out_ref) in enumerate(zip(towards, out_refs)):
        out_ref[2 * per] = bond
        for p in range(per):
            pos = jnp.full((1, n), start + peer * per + p, jnp.int32).astype(F32)
            zre = 5.0 + 2.0 * pos / total
            mag = zre * zre + 1.0
            qre = zre / mag
            qim = -1.0 / mag
            sre = ham_ref[0] + sig_ref[i, p, 0]
            sim = ham_ref[1] + sig_ref[i, p, 1]
            a1 = jnp.concatenate([qre * sre - qim * sim, qre * sim + qim * sre], axis=1)
            a1_pair = split(a1)
            a1_right = (right_form(a1_pair[0]), right_form(a1_pair[1]))
            a2 = dot3(a1_pair, a1_right)
            a2_pair = split(a2)
            a2_right = (right_form(a2_pair[0]), right_form(a2_pair[1]))
            a3 = dot3(a1_pair, a2_right)
            a4 = dot3(a2_pair, a2_right)
            s = eye + (a1 + (a2 + a3))
            x = s + dot3(split(s), right_pair(a4))
            re, im = x[:, :n], x[:, n:]
            out_ref[2 * p] = qre * re - qim * im
            out_ref[2 * p + 1] = qre * im + qim * re


def chain_kernel(layers, *refs):
    in_slots, out_slots = refs[:layers], refs[layers : 2 * layers]
    g_ref, bond_ref = refs[2 * layers :]
    _, per, _, n, _ = g_ref.shape
    for peer, in_slot in zip(peers(layers), in_slots):
        for p in range(per):
            g_ref[peer, p] = in_slot[2 * p : 2 * p + 2]
        bond_ref[peer] = in_slot[2 * per]
    bonds = [None] + [bond_ref[l] for l in range(1, layers)]
    bonds_t = [None] + [b.T for b in bonds[1:]]
    for p in range(per):
        g = [jnp.concatenate([g_ref[l, p, 0], g_ref[l, p, 1]], axis=1) for l in range(layers)]
        down = [None] * layers
        up = [None] * layers
        for l in range(layers):
            high, low = split(g[l])
            tall = (
                jnp.concatenate([high[:, :n], high[:, n:]], axis=0),
                jnp.concatenate([low[:, :n], low[:, n:]], axis=0),
            )
            wide = (high, low)
            if l > 0:
                u = dot3(tall, split(bonds[l]))
                v = dot3(split(bonds_t[l]), wide)
                down[l] = (split(jnp.concatenate([u[:n], u[n:]], axis=1)), right_pair(v))
            if l + 1 < layers:
                u = dot3(tall, split(bonds_t[l + 1]))
                v = dot3(split(bonds[l + 1]), wide)
                up[l] = (split(jnp.concatenate([u[:n], u[n:]], axis=1)), right_pair(v))
        green = list(g)
        gleft = g[0]
        gright = g[layers - 1]
        for step in range(1, layers):
            l = step
            u, v = down[l]
            term = dot3(split(dot3(u, right_pair(gleft))), v)
            green[l] = green[l] + term
            gleft = g[l] + term
            l = layers - 1 - step
            u, v = up[l]
            term = dot3(split(dot3(u, right_pair(gright))), v)
            green[l] = green[l] + term
            gright = g[l] + term
        for l in range(layers):
            near = [green[m] for m in (l - 1, l + 1) if 0 <= m < layers]
            y = green[l] + 0.5 * sum(near[1:], near[0]) if near else green[l]
            g_ref[l, p, 0] = y[:, :n]
            g_ref[l, p, 1] = y[:, n:]
    for peer, out_slot in zip(peers(layers), out_slots):
        out_slot[...] = g_ref[peer]


def momentum_kernel(momentum, slots, *refs):
    core = lax.axis_index("mom")
    out_ref = refs[-1]
    per = refs[0].shape[0]

    def place(blocks):
        for i, block in enumerate(blocks):
            out_ref[i * per : (i + 1) * per] = block[...]

    @pl.when(core == momentum)
    def _():
        place(refs[:slots])

    @pl.when(core != momentum)
    def _():
        place(refs[slots : 2 * slots])


def by_energy_kernel(momentum, layers, order, *refs):
    here = lax.axis_index("len")
    parts, out_ref = refs[:-1], refs[-1]
    per = out_ref.shape[0] // layers
    masks = [0] + orders(layers)[momentum]
    slots = [(part, i) for part in parts for i in range(part.shape[0] // per)]
    for slot, (part, i) in zip(order, slots):
        for p in range(per):
            out_ref[(here ^ masks[slot]) * per + p] = part[i * per + p]


def occupation(pos, total, n):
    return 1.0 / (1.0 + jnp.exp(8.0 * jnp.full((1, n), pos, jnp.int32).astype(F32) / total - 4.0))


def local_kernel(total, shift_ref, weight_ref, zero_ref, one_ref, ret_ref, les_ref, table_ref):
    n = table_ref.shape[1]
    phonons = shift_ref.shape[0]
    for t in range(1, total // 2 + 1):
        value = 0.0
        for m in range(phonons):
            value = value + jnp.where(shift_ref[m] == t, weight_ref[m], 0.0)
        table_ref[t : t + 1] = jnp.full((1, n), value, F32)
    items = [(0, 0), (1, 0)]
    mix_kernel(total, items, True, False, table_ref, zero_ref, one_ref, ret_ref, les_ref)


def mix_kernel(total, items, first, last, table_ref, *refs):
    count = len(items)
    inputs = count + (0 if first else 3 if last else 2)
    sums_in = refs[count:inputs]
    results = refs[inputs : inputs + 2]
    targets = refs[inputs + 2 : inputs + 4] if last else results
    local_e, _, n, _ = refs[0].shape
    place = lax.axis_index("energy")
    places = lax.axis_size("energy")
    core = lax.axis_index("mom")

    def copy_out(i, a):
        return pltpu.make_async_copy(targets[i].at[a], results[i].at[a], refs[-1].at[i, a])

    def body(here, some):
        most = total // 2
        terms = [[] for _ in range(local_e)]
        for i, (momentum, d) in enumerate(items):
            sign, factor = (-1, 1.0) if momentum == here else (1, 0.5)
            source = place + sign * d
            factor = jnp.where((source >= 0) & (source < places), factor, 0.0)
            for b in range(local_e):
                occ = occupation(source * local_e + b, total, n)
                for a in range(local_e):
                    t = d * local_e + sign * (b - a)
                    if some[i] and 1 <= t <= most:
                        weight = table_ref[t : t + 1] * factor
                        terms[a].append((refs[i], b, weight, weight * occ))
        for i in range(2):
            for a in range(local_e):
                if first:
                    sums = [jnp.zeros((n, n), F32)] * 2
                else:
                    sums = [sums_in[i][a, c] for c in range(2)]
                for source, b, *weights in terms[a]:
                    sums = [sums[c] + weights[i] * source[b, c] for c in range(2)]
                if (first or last) and i == 1:
                    sums = [sums[0] - sums[0].T, sums[1] + sums[1].T]
                    if last:
                        sums = [sums[c] + sums_in[2][a, c] for c in range(2)]
                for c in range(2):
                    targets[i][a, c] = sums[c]
                if last:
                    copy_out(i, a).start()

    def present(here, momentum, d):
        return place >= d if momentum == here else place + d < places

    for here in range(2):
        if not last:
            pl.when(core == here)(functools.partial(body, here, [True] * count))
            continue
        for some in itertools.product([False, True], repeat=count):
            fits = core == here
            for (momentum, d), there in zip(items, some):
                fits = fits & (present(here, momentum, d) == there)
            pl.when(fits)(functools.partial(body, here, some))

    if last:
        for a in range(local_e):
            copy_out(0, a).wait()
            copy_out(1, a).wait()


def whole(count):
    return [pl.BlockSpec(memory_space=pltpu.VMEM)] * count


def params():
    return pltpu.CompilerParams(vmem_limit_bytes=VMEM_LIMIT)


def shards(hamiltonian, sigma_prev, coupling, coupling_pattern, phonon_shift, phonon_weight):
    local_e, _, n, _ = sigma_prev.shape[2:]
    layers = lax.axis_size("len")
    count = lax.axis_size("energy")
    moms = lax.axis_size("mom")
    total = local_e * count
    per = local_e // layers
    block = jax.ShapeDtypeStruct((local_e, 2, n, n), F32)
    first, second = orders(layers)

    def exchange(slots, i):
        if i == 0:
            return slots[0]
        pairs = []
        for l in range(layers):
            for k in range(moms):
                peer = l ^ (first, second)[k][i - 1]
                pairs.append((l * moms + k, peer * moms + k))
        return lax.ppermute(slots[i], ("len", "mom"), pairs)

    anywhere = pl.BlockSpec(memory_space=pltpu.HBM)
    inputs = (hamiltonian[0, 0], sigma_prev[0, 0], coupling[0], coupling_pattern)
    inputs = [pltpu.with_memory_space_constraint(value, pltpu.HBM) for value in inputs]

    def inverse(slots):
        return pl.pallas_call(
            functools.partial(inverse_kernel, total, layers, slots),
            out_shape=[jax.ShapeDtypeStruct((2 * per + 1, n, n), F32)] * len(slots),
            in_specs=[anywhere] * 4,
            out_specs=whole(len(slots)),
            scratch_shapes=[
                pltpu.VMEM((2, n, n), F32),
                pltpu.VMEM((len(slots), per, 2, n, n), F32),
                pltpu.VMEM((n, n), F32),
                pltpu.VMEM((n, n), jnp.int32),
                pltpu.SemaphoreType.DMA((3 + len(slots),)),
            ],
            compiler_params=params(),
            cost_estimate=pl.CostEstimate(
                flops=len(slots) * per * 96 * n**3, bytes_accessed=len(slots) * 8 * n * n, transcendentals=0
            ),
            name="inverse",
        )(*inputs)

    early = (1,)
    late = tuple(range(2, layers)) + (0,)
    sent = dict(zip(early, inverse(early))) | dict(zip(late, inverse(late)))
    part = jax.ShapeDtypeStruct((per, 2, n, n), F32)
    sent = pl.pallas_call(
        functools.partial(chain_kernel, layers),
        out_shape=[part] * layers,
        in_specs=whole(layers),
        out_specs=whole(layers),
        scratch_shapes=[pltpu.VMEM((layers, per, 2, n, n), F32), pltpu.VMEM((layers, n, n), F32)],
        compiler_params=params(),
        name="chains",
    )(*[exchange(sent, i) for i in range(layers)])
    own = [exchange(sent, i) for i in range(layers)]
    both_ways = [(k, moms - 1 - k) for k in range(moms)]
    little = pl.CostEstimate(flops=0, bytes_accessed=8 * n, transcendentals=0)

    def call(kernel, shape, *operands, name):
        return pl.pallas_call(
            kernel,
            out_shape=jax.ShapeDtypeStruct((shape, 2, n, n), F32),
            in_specs=whole(len(operands)),
            out_specs=whole(1)[0],
            compiler_params=params(),
            cost_estimate=little,
            name=name,
        )(*operands)

    def of_momentum(momentum, own, other):
        kernel = functools.partial(momentum_kernel, momentum, len(own))
        return call(kernel, len(own) * per, *own, *other, name="momentum")

    def by_energy(momentum, parts):
        kernel = functools.partial(by_energy_kernel, momentum, layers, sum(chunks, []))
        return call(kernel, local_e, *parts, name="by_energy")

    reach = -(-(total // 2) // local_e)

    ring = [z * moms for z in range(count)] + [z * moms + 1 for z in reversed(range(count))]
    ring = list(zip(ring, ring[1:] + ring[:1]))
    ways = ring, [(target, source) for source, target in ring]

    def hop(value, role):
        return lax.ppermute(value, ("energy", "mom"), ways[role])

    chunks = [[0], list(range(1, layers - 1)), [layers - 1]]
    fields = [[], []]
    hops = [[], []]
    for c in chunks:
        if len(hops[0]) == 1:
            own, _ = lax.optimization_barrier((own, hops[0]))
            ahead = [hop(hops[m][0], m) for m in range(2)]
        held = [own[i] for i in c]
        other = [lax.ppermute(v, "mom", both_ways) for v in held]
        parts = [of_momentum(m, held, other) for m in range(2)]
        for m in range(2):
            fields[m].append(parts[m])
        if len(hops[0]) == 2:
            parts, _ = lax.optimization_barrier((parts, ahead))
        for m in range(2):
            hops[m].append(hop(parts[m], m))
    zero, one = (by_energy(m, fields[m]) for m in range(2))
    smem = pl.BlockSpec(memory_space=pltpu.SMEM)
    retarded, local_lesser, table = pl.pallas_call(
        functools.partial(local_kernel, total),
        out_shape=[block] * 2 + [jax.ShapeDtypeStruct((total // 2 + 8, n), F32)],
        in_specs=[smem, smem] + whole(2),
        out_specs=whole(3),
        compiler_params=params(),
        name="local",
    )(phonon_shift, phonon_weight, zero, one)

    def mix(items, blocks, sums, last=False):
        scratch = [pltpu.VMEM(block.shape, F32)] * 2 + [pltpu.SemaphoreType.DMA((2, local_e))]
        return pl.pallas_call(
            functools.partial(mix_kernel, total, items, False, last),
            out_shape=[block] * 2,
            in_specs=whole(1 + len(blocks) + len(sums)),
            out_specs=[pl.BlockSpec(memory_space=pl.ANY)] * 2 if last else whole(2),
            scratch_shapes=scratch if last else [],
            compiler_params=params(),
            name="mix",
        )(table, *blocks, *sums)

    sums = [retarded, jnp.zeros_like(local_lesser)]
    for d in range(1, reach + 1):
        if d == 1:
            fields = hops
        elif d == 2:
            big, _ = lax.optimization_barrier((fields[0][1], fields[1][2]))
            fields = [[ahead[m], hop([big, fields[1][1]][m], m), hop(fields[m][2], m)] for m in range(2)]
        else:
            fields = [[hop(part, m) for part in fields[m]] for m in range(2)]
        zero, one = (by_energy(m, fields[m]) for m in range(2))
        if d < reach:
            sums = mix([(0, d), (1, d)], [zero, one], sums)
    sums = mix([(0, reach), (1, reach)], [zero, one], [*sums, local_lesser], last=True)
    retarded, lesser = sums
    return (retarded[None, None], lesser[None, None])


def solution(mesh):
    in_specs = (
        P("mom", "len", None, None, None),
        P("mom", "len", "energy", None, None, None),
        P("len", None, None),
        P(),
        P(),
        P(),
    )
    out_specs = (
        P("mom", "len", "energy", None, None, None),
        P("mom", "len", "energy", None, None, None),
    )
    return jax.shard_map(shards, mesh=mesh, in_specs=in_specs, out_specs=out_specs, check_vma=False)
```

```python
import functools
import itertools

import jax
import jax.numpy as jnp
from jax import lax
from jax.experimental import pallas as pl
from jax.experimental.pallas import tpu as pltpu
from jax.sharding import PartitionSpec as P

F32 = jnp.float32
BF16 = jnp.bfloat16
VMEM_LIMIT = 16 * 1024 * 1024


def split(x):
    high = x.astype(BF16)
    return high, (x - high.astype(F32)).astype(BF16)


def dot(a, b):
    return jnp.dot(a, b, preferred_element_type=F32)


def dot3(a, b):
    rows = a[0].shape[0]
    both = dot(jnp.concatenate([a[0], a[1]], axis=0), b[0])
    return both[:rows] + (both[rows:] + dot(a[0], b[1]))


def right_form(m):
    n = m.shape[0]
    re, im = m[:, :n], m[:, n:]
    return jnp.concatenate([m, jnp.concatenate([-im, re], axis=1)], axis=0)


def right_pair(m):
    high, low = split(m)
    return right_form(high), right_form(low)


def identity(n):
    rows = lax.broadcasted_iota(jnp.int32, (n, 2 * n), 0)
    cols = lax.broadcasted_iota(jnp.int32, (n, 2 * n), 1)
    return (rows == cols).astype(F32)


def orders(layers):
    first = [layers - 1] + list(range(1, layers - 1))
    second = list(first)
    if layers > 3:
        second[1], second[2] = second[2], second[1]
    return first, second


def peers(layers):
    here = lax.axis_index("len")
    core = lax.axis_index("mom")
    first, second = orders(layers)
    return [here] + [here ^ jnp.where(core == 0, a, b) for a, b in zip(first, second)]


def inverse_kernel(total, layers, slots, ham_any, sig_any, coupling_any, pattern_any, *refs):
    out_refs = refs[: len(slots)]
    ham_ref, sig_ref, coupling_ref, pattern_ref, sems = refs[len(slots) :]
    _, per, _, n, _ = sig_ref.shape
    towards = [peers(layers)[slot] for slot in slots]
    copies = [
        pltpu.make_async_copy(ham_any, ham_ref, sems.at[0]),
        pltpu.make_async_copy(coupling_any, coupling_ref, sems.at[1]),
        pltpu.make_async_copy(pattern_any, pattern_ref, sems.at[2]),
    ]
    for i, peer in enumerate(towards):
        group = sig_any.at[pl.ds(peer * per, per)]
        copies.append(pltpu.make_async_copy(group, sig_ref.at[i], sems.at[3 + i]))
    for copy in copies:
        copy.start()
    for copy in copies:
        copy.wait()
    start = lax.axis_index("energy") * (layers * per)
    eye = identity(n)
    bond = coupling_ref[...] * pattern_ref[...].astype(F32)
    for i, (peer, out_ref) in enumerate(zip(towards, out_refs)):
        out_ref[2 * per] = bond
        for p in range(per):
            pos = jnp.full((1, n), start + peer * per + p, jnp.int32).astype(F32)
            zre = 5.0 + 2.0 * pos / total
            mag = zre * zre + 1.0
            qre = zre / mag
            qim = -1.0 / mag
            sre = ham_ref[0] + sig_ref[i, p, 0]
            sim = ham_ref[1] + sig_ref[i, p, 1]
            a1 = jnp.concatenate([qre * sre - qim * sim, qre * sim + qim * sre], axis=1)
            a1_pair = split(a1)
            a1_right = (right_form(a1_pair[0]), right_form(a1_pair[1]))
            a2 = dot3(a1_pair, a1_right)
            a2_pair = split(a2)
            a2_right = (right_form(a2_pair[0]), right_form(a2_pair[1]))
            a3 = dot3(a1_pair, a2_right)
            a4 = dot3(a2_pair, a2_right)
            s = eye + (a1 + (a2 + a3))
            x = s + dot3(split(s), right_pair(a4))
            re, im = x[:, :n], x[:, n:]
            out_ref[2 * p] = qre * re - qim * im
            out_ref[2 * p + 1] = qre * im + qim * re


def chain_kernel(layers, *refs):
    in_slots, out_slots = refs[:layers], refs[layers : 2 * layers]
    g_ref, bond_ref = refs[2 * layers :]
    _, per, _, n, _ = g_ref.shape
    for peer, in_slot in zip(peers(layers), in_slots):
        for p in range(per):
            g_ref[peer, p] = in_slot[2 * p : 2 * p + 2]
        bond_ref[peer] = in_slot[2 * per]
    bonds = [None] + [bond_ref[l] for l in range(1, layers)]
    bonds_t = [None] + [b.T for b in bonds[1:]]
    for p in range(per):
        g = [jnp.concatenate([g_ref[l, p, 0], g_ref[l, p, 1]], axis=1) for l in range(layers)]
        down = [None] * layers
        up = [None] * layers
        for l in range(layers):
            high, low = split(g[l])
            tall = (
                jnp.concatenate([high[:, :n], high[:, n:]], axis=0),
                jnp.concatenate([low[:, :n], low[:, n:]], axis=0),
            )
            wide = (high, low)
            if l > 0:
                u = dot3(tall, split(bonds[l]))
                v = dot3(split(bonds_t[l]), wide)
                down[l] = (split(jnp.concatenate([u[:n], u[n:]], axis=1)), right_pair(v))
            if l + 1 < layers:
                u = dot3(tall, split(bonds_t[l + 1]))
                v = dot3(split(bonds[l + 1]), wide)
                up[l] = (split(jnp.concatenate([u[:n], u[n:]], axis=1)), right_pair(v))
        green = list(g)
        gleft = g[0]
        gright = g[layers - 1]
        for step in range(1, layers):
            l = step
            u, v = down[l]
            term = dot3(split(dot3(u, right_pair(gleft))), v)
            green[l] = green[l] + term
            gleft = g[l] + term
            l = layers - 1 - step
            u, v = up[l]
            term = dot3(split(dot3(u, right_pair(gright))), v)
            green[l] = green[l] + term
            gright = g[l] + term
        for l in range(layers):
            near = [green[m] for m in (l - 1, l + 1) if 0 <= m < layers]
            y = green[l] + 0.5 * sum(near[1:], near[0]) if near else green[l]
            g_ref[l, p, 0] = y[:, :n]
            g_ref[l, p, 1] = y[:, n:]
    for peer, out_slot in zip(peers(layers), out_slots):
        out_slot[...] = g_ref[peer]


def momentum_kernel(momentum, slots, *refs):
    core = lax.axis_index("mom")
    out_ref = refs[-1]
    per = refs[0].shape[0]

    def place(blocks):
        for i, block in enumerate(blocks):
            out_ref[i * per : (i + 1) * per] = block[...]

    @pl.when(core == momentum)
    def _():
        place(refs[:slots])

    @pl.when(core != momentum)
    def _():
        place(refs[slots : 2 * slots])


def by_energy_kernel(momentum, layers, order, *refs):
    here = lax.axis_index("len")
    parts, out_ref = refs[:-1], refs[-1]
    per = out_ref.shape[0] // layers
    masks = [0] + orders(layers)[momentum]
    slots = [(part, i) for part in parts for i in range(part.shape[0] // per)]
    for slot, (part, i) in zip(order, slots):
        for p in range(per):
            out_ref[(here ^ masks[slot]) * per + p] = part[i * per + p]


def occupation(pos, total, n):
    return 1.0 / (1.0 + jnp.exp(8.0 * jnp.full((1, n), pos, jnp.int32).astype(F32) / total - 4.0))


def local_kernel(total, shift_ref, weight_ref, zero_ref, one_ref, ret_ref, les_ref, table_ref):
    n = table_ref.shape[1]
    phonons = shift_ref.shape[0]
    for t in range(1, total // 2 + 1):
        value = 0.0
        for m in range(phonons):
            value = value + jnp.where(shift_ref[m] == t, weight_ref[m], 0.0)
        table_ref[t : t + 1] = jnp.full((1, n), value, F32)
    items = [(0, 0), (1, 0)]
    mix_kernel(total, items, True, False, table_ref, zero_ref, one_ref, ret_ref, les_ref)


def mix_kernel(total, items, first, last, table_ref, *refs):
    count = len(items)
    inputs = count + (0 if first else 3 if last else 2)
    sums_in = refs[count:inputs]
    results = refs[inputs : inputs + 2]
    targets = refs[inputs + 2 : inputs + 4] if last else results
    local_e, _, n, _ = refs[0].shape
    place = lax.axis_index("energy")
    places = lax.axis_size("energy")
    core = lax.axis_index("mom")

    def copy_out(i, a):
        return pltpu.make_async_copy(targets[i].at[a], results[i].at[a], refs[-1].at[i, a])

    def body(here, some):
        most = total // 2
        terms = [[] for _ in range(local_e)]
        for i, (momentum, d) in enumerate(items):
            sign, factor = (-1, 1.0) if momentum == here else (1, 0.5)
            source = place + sign * d
            factor = jnp.where((source >= 0) & (source < places), factor, 0.0)
            for b in range(local_e):
                occ = occupation(source * local_e + b, total, n)
                for a in range(local_e):
                    t = d * local_e + sign * (b - a)
                    if some[i] and 1 <= t <= most:
                        weight = table_ref[t : t + 1] * factor
                        terms[a].append((refs[i], b, weight, weight * occ))
        for i in range(2):
            for a in range(local_e):
                if first:
                    sums = [jnp.zeros((n, n), F32)] * 2
                else:
                    sums = [sums_in[i][a, c] for c in range(2)]
                for source, b, *weights in terms[a]:
                    sums = [sums[c] + weights[i] * source[b, c] for c in range(2)]
                if (first or last) and i == 1:
                    sums = [sums[0] - sums[0].T, sums[1] + sums[1].T]
                    if last:
                        sums = [sums[c] + sums_in[2][a, c] for c in range(2)]
                for c in range(2):
                    targets[i][a, c] = sums[c]
                if last:
                    copy_out(i, a).start()

    def present(here, momentum, d):
        return place >= d if momentum == here else place + d < places

    for here in range(2):
        if not last:
            pl.when(core == here)(functools.partial(body, here, [True] * count))
            continue
        for some in itertools.product([False, True], repeat=count):
            fits = core == here
            for (momentum, d), there in zip(items, some):
                fits = fits & (present(here, momentum, d) == there)
            pl.when(fits)(functools.partial(body, here, some))

    if last:
        for a in range(local_e):
            copy_out(0, a).wait()
            copy_out(1, a).wait()


def whole(count):
    return [pl.BlockSpec(memory_space=pltpu.VMEM)] * count


def params():
    return pltpu.CompilerParams(vmem_limit_bytes=VMEM_LIMIT)


def shards(hamiltonian, sigma_prev, coupling, coupling_pattern, phonon_shift, phonon_weight):
    local_e, _, n, _ = sigma_prev.shape[2:]
    layers = lax.axis_size("len")
    count = lax.axis_size("energy")
    moms = lax.axis_size("mom")
    total = local_e * count
    per = local_e // layers
    block = jax.ShapeDtypeStruct((local_e, 2, n, n), F32)
    first, second = orders(layers)

    def exchange(slots, i):
        if i == 0:
            return slots[0]
        pairs = []
        for l in range(layers):
            for k in range(moms):
                peer = l ^ (first, second)[k][i - 1]
                pairs.append((l * moms + k, peer * moms + k))
        return lax.ppermute(slots[i], ("len", "mom"), pairs)

    anywhere = pl.BlockSpec(memory_space=pltpu.HBM)
    inputs = (hamiltonian[0, 0], sigma_prev[0, 0], coupling[0], coupling_pattern)
    inputs = [pltpu.with_memory_space_constraint(value, pltpu.HBM) for value in inputs]

    def inverse(slots):
        return pl.pallas_call(
            functools.partial(inverse_kernel, total, layers, slots),
            out_shape=[jax.ShapeDtypeStruct((2 * per + 1, n, n), F32)] * len(slots),
            in_specs=[anywhere] * 4,
            out_specs=whole(len(slots)),
            scratch_shapes=[
                pltpu.VMEM((2, n, n), F32),
                pltpu.VMEM((len(slots), per, 2, n, n), F32),
                pltpu.VMEM((n, n), F32),
                pltpu.VMEM((n, n), jnp.int32),
                pltpu.SemaphoreType.DMA((3 + len(slots),)),
            ],
            compiler_params=params(),
            cost_estimate=pl.CostEstimate(
                flops=len(slots) * per * 96 * n**3, bytes_accessed=len(slots) * 8 * n * n, transcendentals=0
            ),
            name="inverse",
        )(*inputs)

    early = (1,)
    late = tuple(range(2, layers))
    sent = {i: v for c in (early, late, (0,)) for i, v in zip(c, inverse(c))}
    part = jax.ShapeDtypeStruct((per, 2, n, n), F32)
    sent = pl.pallas_call(
        functools.partial(chain_kernel, layers),
        out_shape=[part] * layers,
        in_specs=whole(layers),
        out_specs=whole(layers),
        scratch_shapes=[pltpu.VMEM((layers, per, 2, n, n), F32), pltpu.VMEM((layers, n, n), F32)],
        compiler_params=params(),
        name="chains",
    )(*[exchange(sent, i) for i in range(layers)])
    own = [exchange(sent, i) for i in range(layers)]
    both_ways = [(k, moms - 1 - k) for k in range(moms)]
    little = pl.CostEstimate(flops=0, bytes_accessed=8 * n, transcendentals=0)

    def call(kernel, shape, *operands, name):
        return pl.pallas_call(
            kernel,
            out_shape=jax.ShapeDtypeStruct((shape, 2, n, n), F32),
            in_specs=whole(len(operands)),
            out_specs=whole(1)[0],
            compiler_params=params(),
            cost_estimate=little,
            name=name,
        )(*operands)

    def of_momentum(momentum, own, other):
        kernel = functools.partial(momentum_kernel, momentum, len(own))
        return call(kernel, len(own) * per, *own, *other, name="momentum")

    def by_energy(momentum, parts):
        kernel = functools.partial(by_energy_kernel, momentum, layers, sum(chunks, []))
        return call(kernel, local_e, *parts, name="by_energy")

    reach = -(-(total // 2) // local_e)

    ring = [z * moms for z in range(count)] + [z * moms + 1 for z in reversed(range(count))]
    ring = list(zip(ring, ring[1:] + ring[:1]))
    ways = ring, [(target, source) for source, target in ring]

    def hop(value, role):
        return lax.ppermute(value, ("energy", "mom"), ways[role])

    chunks = [[0], list(range(1, layers - 1)), [layers - 1]]
    fields = [[], []]
    hops = [[], []]
    for c in chunks:
        if len(hops[0]) == 1:
            own, _ = lax.optimization_barrier((own, hops[0]))
            ahead = [hop(hops[m][0], m) for m in range(2)]
        held = [own[i] for i in c]
        other = [lax.ppermute(v, "mom", both_ways) for v in held]
        parts = [of_momentum(m, held, other) for m in range(2)]
        for m in range(2):
            fields[m].append(parts[m])
        if len(hops[0]) == 2:
            parts, _ = lax.optimization_barrier((parts, ahead))
        for m in range(2):
            hops[m].append(hop(parts[m], m))
    zero, one = (by_energy(m, fields[m]) for m in range(2))
    smem = pl.BlockSpec(memory_space=pltpu.SMEM)
    retarded, local_lesser, table = pl.pallas_call(
        functools.partial(local_kernel, total),
        out_shape=[block] * 2 + [jax.ShapeDtypeStruct((total // 2 + 8, n), F32)],
        in_specs=[smem, smem] + whole(2),
        out_specs=whole(3),
        compiler_params=params(),
        name="local",
    )(phonon_shift, phonon_weight, zero, one)

    def mix(items, blocks, sums, last=False):
        scratch = [pltpu.VMEM(block.shape, F32)] * 2 + [pltpu.SemaphoreType.DMA((2, local_e))]
        return pl.pallas_call(
            functools.partial(mix_kernel, total, items, False, last),
            out_shape=[block] * 2,
            in_specs=whole(1 + len(blocks) + len(sums)),
            out_specs=[pl.BlockSpec(memory_space=pl.ANY)] * 2 if last else whole(2),
            scratch_shapes=scratch if last else [],
            compiler_params=params(),
            name="mix",
        )(table, *blocks, *sums)

    sums = [retarded, jnp.zeros_like(local_lesser)]
    for d in range(1, reach + 1):
        if d == 1:
            fields = hops
        elif d == 2:
            big, _ = lax.optimization_barrier((fields[0][1], fields[1][2]))
            fields = [[ahead[m], hop([big, fields[1][1]][m], m), hop(fields[m][2], m)] for m in range(2)]
        else:
            fields = [[hop(part, m) for part in fields[m]] for m in range(2)]
        zero, one = (by_energy(m, fields[m]) for m in range(2))
        if d < reach:
            sums = mix([(0, d), (1, d)], [zero, one], sums)
    sums = mix([(0, reach), (1, reach)], [zero, one], [*sums, local_lesser], last=True)
    retarded, lesser = sums
    return (retarded[None, None], lesser[None, None])


def solution(mesh):
    in_specs = (
        P("mom", "len", None, None, None),
        P("mom", "len", "energy", None, None, None),
        P("len", None, None),
        P(),
        P(),
        P(),
    )
    out_specs = (
        P("mom", "len", "energy", None, None, None),
        P("mom", "len", "energy", None, None, None),
    )
    return jax.shard_map(shards, mesh=mesh, in_specs=in_specs, out_specs=out_specs, check_vma=False)
```
